512 devices in a mesh: dp: 32 (over x, z_hi, core), mp: 4 (over y), root: 4 (over z_lo).
Axes of the slice: x: 4, y: 4, z: 16 (z_hi: 4, z_lo: 4; z = z_hi * 4 + z_lo), core: 2. Of those that a mesh axis runs over, the one named last changes fastest.
Arguments:
- acts: bfloat16 [32768, 2048], P('dp', 'mp'), may hold values from -6 to 6
- grads_out: bfloat16 [32768, 4096], P('dp', 'root'), may hold values from -6 to 6
- prec_left: bfloat16 [4, 8, 512, 512], P('mp', 'root', 'dp')
- prec_right: bfloat16 [4, 8, 512, 512], P('mp', 'root', 'dp')
- stats_old: float32 [32, 512, 512], P('dp', 'mp')
- listed: int32 [16], replicated, may hold values from 0 to 31, as said below
- owner: int32 [16], replicated, may hold values from 0 to 3
Outputs:
- update: bfloat16 [4, 512, 4096], P('mp', 'dp', 'root')
- new_stats: float32 [4, 32, 512, 512], P('root', 'dp', 'mp')
- new_roots: float32 [4, 32, 512, 512], P('root', 'dp', 'mp')
The draws below stay inside these ranges and needn't reach their ends.
Inputs may be any that keep to these rules, and one draw needn't show every extreme that they name: `listed`: 16 distinct block numbers; block 0 and block 31 are always among them.
All inputs are finite; a program needn't handle non-finite values.
Results may differ from the reference program's by a relative error of at most 0.0057.
Values may be sent and summed in bfloat16 or wider, within the bound.
No kernel may reach another device: no remote copies, remote signals or barrier semaphores. Data moves between devices by JAX's collectives and lax.ppermute only.
A program may use at most 64 MiB of HBM per device.

```python
import math
import jax
import jax.numpy as jnp
from jax import lax

B = 512
REFRESH = 16
ITERS = 2
TOKENS = 32768
NBLK = 32
REFRESH_SLOTS = 32
N_MP = 4
N_ROOT = 4


def symmetric_blocks(key, lead, low_scale, high_scale, reach):
    first, second = jax.random.split(key)
    diag = jnp.exp(jax.random.uniform(first, lead + (B,), jnp.float32, math.log(low_scale), math.log(high_scale)))
    raw = jax.random.uniform(second, lead + (B, B), jnp.float32, -1.0, 1.0)
    mixed = 0.5 * (raw + jnp.swapaxes(raw, -1, -2))
    smaller = jnp.minimum(diag[..., :, None], diag[..., None, :])
    identity = jnp.eye(B, dtype=jnp.float32)
    return identity * diag[..., :, None] + (1.0 - identity) * smaller * mixed * (reach / (B - 1))


def block_statistics(key, lead, low_scale, high_scale, shared, low_weight, high_weight):
    first, second, third, fourth = jax.random.split(key, 4)
    diag = jnp.exp(jax.random.uniform(first, lead + (B,), jnp.float32, math.log(low_scale), math.log(high_scale)))
    raw = jax.random.uniform(second, lead + (B, B), jnp.float32, -1.0, 1.0)
    mixed = 0.5 * (raw + jnp.swapaxes(raw, -1, -2))
    magnitude = jax.random.uniform(third, lead + (B,), jnp.float32, low_weight, high_weight)
    signs = jax.random.rademacher(fourth, lead + (B,), jnp.float32)
    root_diag = jnp.sqrt(diag)
    paired = root_diag[..., :, None] * root_diag[..., None, :]
    identity = jnp.eye(B, dtype=jnp.float32)
    bulk = identity * diag[..., :, None] + (1.0 - identity) * paired * mixed * B ** (-0.5)
    vector = root_diag * magnitude * signs
    return bulk + shared * B ** (-0.5) * vector[..., :, None] * vector[..., None, :]


def draw_prec_left(key, part):
    key = jax.random.fold_in(key, 3)
    value_entries = symmetric_blocks(key, (N_MP, NBLK // N_MP), 0.5, 2.0, 5.0)
    return value_entries.astype(jnp.bfloat16)


def draw_prec_right(key, part):
    key = jax.random.fold_in(key, 5)
    value_entries = symmetric_blocks(key, (N_MP, NBLK // N_MP), 0.5, 2.0, 5.0)
    return value_entries.astype(jnp.bfloat16)


def draw_stats_old(key, part):
    key = jax.random.fold_in(key, 7)
    value_entries = block_statistics(key, (REFRESH_SLOTS,), 0.01, 10.0, 2.1, 0.5, 1.5)
    return value_entries


def draw_listed(key, part):
    key = jax.random.fold_in(key, 11)
    first, second = jax.random.split(key)
    middle = jax.random.permutation(first, NBLK - 2)[:REFRESH - 2].astype(jnp.int32) + 1
    ends = jnp.array([0, NBLK - 1], dtype=jnp.int32)
    chosen = jnp.concatenate([ends, middle])
    return jax.random.permutation(second, chosen).astype(jnp.int32)


def set_ends(entries, rng, low, top_value):
    place = [jax.random.randint(jax.random.fold_in(rng, axis), (), 0, length) for axis, length in enumerate(entries.shape)]
    main_axis = entries.shape.index(max(entries.shape))
    next_to = place[:main_axis] + [(place[main_axis] + 1) % entries.shape[main_axis]] + place[main_axis + 1:]
    return entries.at[tuple(place)].set(low).at[tuple(next_to)].set(top_value)


def spiked(drawn, key, source, target, blocks, factor):
    def block_of(position):
        return (jnp.arange(drawn.shape[position]) // (drawn.shape[position] // blocks)).reshape((-1,) + (1,) * (drawn.ndim - 1 - position))

    first = jax.random.permutation(key, blocks)[block_of(target)]
    far = (block_of(target) + blocks // 2) % blocks
    return jnp.where((block_of(source) == first) | (block_of(source) == far), factor * drawn, drawn)


def block_levels(key, dims, cuts, low, largest):
    gain, own = 1.0, jax.random.fold_in(key, 6)
    for position, shards_of in cuts:
        draws = jnp.exp(jax.random.uniform(jax.random.fold_in(own, position), (shards_of,), jnp.float32, low / len(cuts), largest / len(cuts)))
        gain = gain * jnp.repeat(draws, dims[position] // shards_of).reshape([-1 if axis == position else 1 for axis in range(len(dims))])
    return gain


def normal_values(stream_key, shape, spread, bound, cuts=(), held_as=jnp.bfloat16):
    drawn = spread * jax.random.normal(stream_key, shape, jnp.float32)
    if cuts:
        drawn = drawn * block_levels(stream_key, shape, cuts, -0.22, 0.18)
    return jnp.clip(drawn, -bound, bound).astype(held_as)


def gaussian_with(stream_key, shape, spread, most, cuts, heavy, kind=jnp.bfloat16):
    values = spread * jax.random.normal(stream_key, shape, jnp.float32)
    if cuts:
        values = values * block_levels(stream_key, shape, cuts, -0.22, 0.18)
    return jnp.clip(spiked(values, jax.random.fold_in(stream_key, 3), *heavy), -most, most).astype(kind)


def setup_inputs(seed: int = 0) -> dict:
    streams_of = jax.random.split(jax.random.key(seed), 8)
    acts = gaussian_with(streams_of[0], (TOKENS, N_MP * B), 1.0, 6.0, ((0, 32), (1, 4)), (0, 1, 32, 2.75))
    grads_out = normal_values(streams_of[1], (TOKENS, 2 * N_ROOT * B), 1.0, 6.0, ((0, 32), (1, 4)))
    prec_left = draw_prec_left(jax.random.fold_in(streams_of[7], 71), 0)
    prec_right = draw_prec_right(jax.random.fold_in(streams_of[7], 71), 0)
    stats_old = draw_stats_old(jax.random.fold_in(streams_of[7], 71), 0)
    listed = draw_listed(jax.random.fold_in(streams_of[7], 71), 0)
    owner = set_ends(jax.random.randint(streams_of[6], (REFRESH,), 0, N_ROOT), jax.random.fold_in(streams_of[6], 1), 0, N_ROOT - 1).astype(jnp.int32)
    return dict(acts=acts, grads_out=grads_out, prec_left=prec_left, prec_right=prec_right, stats_old=stats_old, listed=listed, owner=owner)


decay_rate = 0.6

def matmul_high(left, right):
    return jnp.dot(left, right, precision=lax.Precision.HIGHEST, preferred_element_type=jnp.float32)

def inverse_root(matrix):
    identity = jnp.eye(B, dtype=jnp.float32)
    norm_value = jnp.sqrt(jnp.sum(matrix * matrix))
    factor = 2.5 / norm_value
    iterate = jnp.sqrt(jnp.sqrt(factor)) * identity
    coupled = factor * matrix
    for step in range(ITERS):
        factor_matrix = (5.0 * identity - coupled) * 0.25
        iterate = matmul_high(iterate, factor_matrix)
        for power in range(4):
            coupled = matmul_high(coupled, factor_matrix)
    return iterate

def reference(acts, grads_out, prec_left, prec_right, stats_old, listed, owner):
    col_blocks = 2 * N_ROOT
    grad = jnp.dot(acts.T, grads_out, preferred_element_type=jnp.float32) * TOKENS ** (-0.5)
    grad_low = grad.astype(jnp.bfloat16)
    blocks = grad_low.reshape(N_MP, B, col_blocks, B).transpose(0, 2, 1, 3)
    left_part = jnp.einsum('ijab,ijbc->ijac', prec_left.astype(jnp.float32), blocks.astype(jnp.float32)).astype(jnp.bfloat16)
    update = jnp.einsum('ijab,ijbc->ijac', left_part.astype(jnp.float32), prec_right.astype(jnp.float32)).astype(jnp.bfloat16)
    update = update.transpose(0, 2, 1, 3).reshape(N_MP, B, col_blocks * B)

    def refresh_preconditioners(slot_pos):
        block_id = listed[slot_pos // 2]
        chosen = blocks[block_id // col_blocks, block_id % col_blocks]
        side = jnp.where(slot_pos % 2 == 0, chosen, chosen.T)
        product = jnp.dot(side, side.T, preferred_element_type=jnp.float32)
        stats = decay_rate * stats_old[slot_pos] + (1.0 - decay_rate) / B * product
        return (stats, inverse_root(stats))
    gathered_statistics, gathered_roots = lax.map(refresh_preconditioners, jnp.arange(REFRESH_SLOTS, dtype=jnp.int32))
    slot_holder_index = owner[jnp.arange(REFRESH_SLOTS, dtype=jnp.int32) // 2]
    owned = slot_holder_index[None, :] == jnp.arange(N_ROOT, dtype=jnp.int32)[:, None]
    new_stats = jnp.where(owned[:, :, None, None], gathered_statistics[None], jnp.zeros((), jnp.float32))
    new_roots = jnp.where(owned[:, :, None, None], gathered_roots[None], jnp.zeros((), jnp.float32))
    return (update, new_stats, new_roots)
```

```python
import functools

import jax
import jax.numpy as jnp
from jax import lax
from jax.experimental import pallas as pl
from jax.experimental.pallas import tpu as pltpu
from jax.sharding import Mesh, PartitionSpec as P

B = 512
DECAY = 0.6
KAPPA = 1.25 ** 4
X, ZH, CORE = 4, 4, 2
CHIPS = X * ZH
PART = B // X
ROWS = B // CHIPS
GRID = ("x", "zh")
F32, BF16 = jnp.float32, jnp.bfloat16
VMEM = pl.BlockSpec(memory_space=pltpu.VMEM)
SMEM = pl.BlockSpec(memory_space=pltpu.SMEM)


def dot(left, right, left_dim=1, right_dim=0):
    dims = (((left_dim,), (right_dim,)), ((), ()))
    return lax.dot_general(left, right, dims, preferred_element_type=F32)


def params():
    return pltpu.CompilerParams(vmem_limit_bytes=32 * 1024 * 1024)


def cost(flops, nbytes):
    return pl.CostEstimate(flops=flops, bytes_accessed=nbytes, transcendentals=0)


def shape(dims, dtype=BF16):
    return jax.ShapeDtypeStruct(dims, dtype)


def accumulate(total, part):
    @pl.when(pl.program_id(0) == 0)
    def _():
        total[...] = part

    @pl.when(pl.program_id(0) > 0)
    def _():
        total[...] += part


def other_kernel(index_ref, acts_ref, grads_ref, left_ref, right_ref, turned_ref, out_ref, total):
    other = index_ref[0]
    turned = acts_ref[...].T
    turned_ref[...] = turned
    accumulate(total, dot(turned, grads_ref[...]))

    @pl.when(pl.program_id(0) == pl.num_programs(0) - 1)
    def _():
        rows = left_ref.shape[2]
        out_ref[:B] = total[...].astype(BF16)
        out_ref[B : B + rows] = left_ref[0, other]
        out_ref[B + rows :] = right_ref[0, other]


def other_half(acts, grads, prec_left, prec_right, index):
    tokens, rows = acts.shape[0], prec_left.shape[2]
    steps = 4
    piece = tokens // steps
    whole = lambda *dims: pl.BlockSpec(dims, lambda k, index: (0,) * len(dims))
    return pl.pallas_call(
        other_kernel,
        grid_spec=pltpu.PrefetchScalarGridSpec(
            num_scalar_prefetch=1,
            grid=(steps,),
            in_specs=[
                pl.BlockSpec((piece, B), lambda k, index: (k, 0)),
                pl.BlockSpec((piece, B), lambda k, index: (k, index[0])),
                whole(*prec_left.shape),
                whole(*prec_right.shape),
            ],
            out_specs=[
                pl.BlockSpec((B, piece), lambda k, index: (0, k)),
                whole(B + 2 * rows, B),
            ],
            scratch_shapes=[pltpu.VMEM((B, B), F32)],
        ),
        out_shape=[shape((B, tokens)), shape((B + 2 * rows, B))],
        cost_estimate=cost(2 * tokens * B * B, 4 * tokens * B),
        name="other_half",
    )(index.reshape(1), acts, grads, prec_left, prec_right)


def own_kernel(index_ref, turned_ref, grads_ref, out_ref):
    at = pl.multiple_of(index_ref[0] * B, B)
    out_ref[...] = dot(turned_ref[...], grads_ref[:, pl.ds(at, B)])


def join_kernel(index_ref, own_ref, got_ref, left_ref, right_ref, out_ref, left_out, right_out):
    core = index_ref[0]
    rows = left_ref.shape[2]
    out_ref[...] = (own_ref[...] + got_ref[:B].astype(F32)).astype(BF16).T
    mine = pl.ds(pl.multiple_of(core * rows, rows), rows)
    theirs = pl.ds(pl.multiple_of((1 - core) * rows, rows), rows)
    left_out[mine, :] = left_ref[0, core]
    left_out[theirs, :] = got_ref[B : B + rows]
    right_out[mine, :] = right_ref[0, core]
    right_out[theirs, :] = got_ref[B + rows :]


def shifted(value, axis):
    size = lax.axis_size(axis)
    return [
        lax.ppermute(value, axis, [(at, (at + step) % size) for at in range(size)])
        for step in range(1, size)
    ]


def place(out_ref, parts, index):
    rows = parts[0].shape[0]
    for step, part in enumerate(parts):
        at = (index + len(parts) - step) % len(parts) * rows
        out_ref[pl.ds(pl.multiple_of(at, rows), rows), :] = part[...]


def part_kernel(axis_at, info_ref, one, two, three, four, out_ref):
    place(out_ref, (one, two, three, four), info_ref[axis_at])


def added(parts_ref):
    total = parts_ref[0].astype(F32)
    for part in range(1, parts_ref.shape[0]):
        total = total + parts_ref[part].astype(F32)
    return total


def sum_kernel(parts_ref, out_ref):
    out_ref[...] = added(parts_ref).astype(BF16)


def pack_kernel(scale, parts_ref, *refs):
    grad_ref, pieces_ref = refs[-2:]
    grad = (added(parts_ref) * scale).astype(BF16)
    grad_ref[...] = grad
    cores, n_mp, n_root, rows, lanes = pieces_ref.shape
    for c in range(cores):
        for m in range(n_mp):
            piece = grad[c * rows : (c + 1) * rows, m * lanes : (m + 1) * lanes]
            for r in range(n_root):
                pieces_ref[c, m, r] = piece


def left_kernel(info_ref, grad_ref, own_ref, one, two, three, out_ref, low, high, prec):
    x, zh = info_ref[1], info_ref[2]
    half, lanes = out_ref.shape[1:]
    for ref, slot in ((low, zh), (high, (zh + 2) % ZH)):
        ref[...] = jnp.zeros_like(ref)
        ref[pl.ds(pl.multiple_of(slot * ROWS, ROWS), ROWS), :] = grad_ref[...]
    place(prec, (own_ref, one, two, three), x)
    rows = prec[...].reshape(CHIPS, ROWS, B)
    out = dot(rows[:, :half].reshape(CHIPS * half, B), low[...], 1, 1)
    out = out + dot(rows[:, half:].reshape(CHIPS * half, B), high[...], 1, 1)
    out_ref[...] = out.astype(BF16).reshape(CHIPS, half, lanes)


def choose_kernel(place_ref, blocks_ref, left_ref, *refs):
    half, out_ref = left_ref.shape[1], refs[-1]
    for j in range(CHIPS):
        out_ref[j, :half] = blocks_ref[place_ref[j]]
        out_ref[j, half:] = left_ref[j]


def spread_kernel(parts_ref, *refs):
    half, out_ref = parts_ref.shape[1] // 2, refs[-1]
    for peer in range(out_ref.shape[0]):
        out_ref[peer] = parts_ref[:, :half]


def update_kernel(info_ref, parts_ref, own_ref, one, two, three, keep_ref, send_ref, left, prec):
    core, x = info_ref[0], info_ref[1]
    half, lanes = keep_ref.shape[0], parts_ref.shape[2]
    place(prec, (own_ref, one, two, three), x)
    slot = lax.broadcasted_iota(jnp.int32, (half, lanes), 1) // ROWS
    for w in range(X):
        low = jnp.zeros((half, lanes), F32)
        high = jnp.zeros((half, lanes), F32)
        for z in range(ZH):
            part = parts_ref[w * ZH + z, half:].astype(F32)
            low = low + jnp.where(slot == z, part, 0.0)
            high = high + jnp.where(slot == (z + 2) % ZH, part, 0.0)
        at = slice(w * lanes, (w + 1) * lanes)
        left[:half, at] = low.astype(BF16)
        left[half:, at] = pltpu.roll(high, lanes // 2, 1).astype(BF16)
    out = dot(left[...], prec[...])
    keep_ref[...] = jnp.where(core == 0, out[:half], out[half:]).astype(BF16)
    send_ref[...] = jnp.where(core == 0, out[half:], out[:half]).astype(BF16)


def refresh_kernel(info_ref, owner_ref, pieces_ref, own_ref, low_ref, one, two, three, stats_ref, roots_ref, block, product, old):
    core, x, zh, mp, root = (info_ref[at] for at in range(5))
    n_mp = pieces_ref.shape[1]
    rows, lanes = pieces_ref.shape[3:]
    quarter = own_ref.shape[0]
    for c in range(CORE):
        for m in range(n_mp):
            for j in range(CHIPS):
                at = j * ROWS + c * rows
                block[at : at + rows, m * lanes : (m + 1) * lanes] = pieces_ref[c, m, j]

    place(old, (low_ref, one, two, three), mp)

    @pl.when(core == 0)
    def _():
        value = block[...]
        product[...] = dot(value, value, 0, 0) * ((1.0 - DECAY) / B)

    @pl.when(core != 0)
    def _():
        value = block[...]
        product[...] = dot(value, value, 1, 1) * ((1.0 - DECAY) / B)

    mine = pl.ds(pl.multiple_of(mp * quarter, quarter), quarter)
    stats_rows = DECAY * own_ref[...] + product[mine, :]
    full = DECAY * old[...].astype(F32) + product[...]
    square = jnp.sum(full * full, axis=0, keepdims=True)
    factor = 2.5 / jnp.sqrt(jnp.sum(square, axis=1, keepdims=True))
    block[...] = (full * (factor * 0.2)).astype(BF16)
    e_rows = stats_rows * (factor * 0.2)
    y = e_rows
    for _ in range(5):
        y = y - dot(y.astype(BF16), block[...])
    line = lax.broadcasted_iota(jnp.int32, (quarter, B), 0) + mp * quarter
    unit = jnp.where(line == lax.broadcasted_iota(jnp.int32, (quarter, B), 1), 1.0, 0.0)
    roots_rows = (jnp.sqrt(jnp.sqrt(factor)) * 1.5625) * (unit - e_rows - KAPPA * y)
    owned = owner_ref[x * ZH + zh] == root
    stats_ref[...] = jnp.where(owned, stats_rows, 0.0)
    roots_ref[...] = jnp.where(owned, roots_rows, 0.0)


def kernel_call(kernel, name, in_specs, out_shape, scratch=(), work=None, awaited=0):
    return pl.pallas_call(
        kernel,
        in_specs=in_specs + [pl.BlockSpec(memory_space=pl.ANY)] * awaited,
        out_specs=[VMEM] * len(out_shape),
        out_shape=out_shape,
        scratch_shapes=list(scratch),
        compiler_params=params(),
        cost_estimate=work,
        name=name,
    )


def local(acts, grads_out, prec_left, prec_right, stats_old, listed, owner):
    x, zh, core = (lax.axis_index(name) for name in ("x", "zh", "core"))
    mp, root = lax.axis_index("mp"), lax.axis_index("root")
    n_mp, n_root = lax.axis_size("mp"), lax.axis_size("root")
    quarter = B // n_mp
    lanes, half = B // n_mp, ROWS // CORE
    tokens = acts.shape[0] * CHIPS * CORE
    swap = ((0, 1), (1, 0))
    info = jnp.stack([core, x, zh, mp, root])

    turned, send = other_half(acts, grads_out, prec_left, prec_right, 1 - core)
    got = lax.ppermute(send, "core", swap)
    (own,) = kernel_call(
        own_kernel,
        "own_half",
        [SMEM, VMEM, VMEM],
        [shape((B, B), F32)],
        work=cost(2 * acts.shape[0] * B * B, 4 * acts.shape[0] * B),
    )(core.reshape(1), turned, grads_out)
    total, left_rows, right_rows = kernel_call(
        join_kernel,
        "join",
        [SMEM] + [VMEM] * 4,
        [shape((B, B)), shape((ROWS, B)), shape((ROWS, B))],
    )(core.reshape(1), own, got, prec_left, prec_right)
    total = lax.all_to_all(total.reshape(X, PART, B), "x", 0, 0)
    got = shifted(left_rows, "zh")
    (total,) = kernel_call(sum_kernel, "sum_x", [VMEM], [shape((PART, B))])(total)
    (left_part,) = kernel_call(
        functools.partial(part_kernel, 2), "left_rows", [SMEM] + [VMEM] * 4, [shape((PART, B))]
    )(info, left_rows, *got)
    left_parts = [left_part] + shifted(left_part, "x")
    old_own = stats_old[0]
    old_low = old_own.astype(BF16)
    olds = [old_low] + shifted(old_low, "mp")
    total = lax.all_to_all(total.reshape(ZH, ROWS, B), "zh", 0, 0)
    grad, pieces = kernel_call(
        functools.partial(pack_kernel, tokens ** -0.5),
        "pack",
        [VMEM],
        [shape((ROWS, B)), shape((CORE, n_mp, n_root, half, lanes))],
        awaited=6,
    )(total, *left_parts[1:], *olds[1:])

    blocks = lax.all_to_all(pieces.reshape(-1, half, lanes), ("core", "mp", "root"), 0, 0)
    (left,) = kernel_call(
        left_kernel,
        "left",
        [SMEM] + [VMEM] * 5,
        [shape((CHIPS, half, lanes))],
        [pltpu.VMEM((lanes, B), BF16)] * 2 + [pltpu.VMEM((B, B), BF16)],
        cost(4 * CHIPS * half * lanes * B, 2 * B * B),
    )(info, grad, *left_parts)
    got = shifted(right_rows, "zh")
    at = (listed % 2) * (n_mp * n_root) + listed // 2
    (chosen,) = kernel_call(
        choose_kernel, "choose", [SMEM, VMEM, VMEM], [shape((CHIPS, 2 * half, lanes))], awaited=3
    )(at, blocks, left, *got)
    parts = lax.all_to_all(chosen, GRID, 0, 0)
    (right_part,) = kernel_call(
        functools.partial(part_kernel, 2), "right_rows", [SMEM] + [VMEM] * 4, [shape((PART, B))]
    )(info, right_rows, *got)
    right_parts = [right_part] + shifted(right_part, "x")
    (mine,) = kernel_call(
        spread_kernel,
        "spread",
        [VMEM],
        [shape((CORE * n_mp, CHIPS, half, lanes))],
        awaited=3,
    )(parts, *right_parts[1:])
    gathered = lax.all_to_all(mine, ("core", "mp"), 0, 0)
    gathered = gathered.reshape((CORE, n_mp) + gathered.shape[1:])

    keep, send = kernel_call(
        update_kernel,
        "update",
        [SMEM] + [VMEM] * 5,
        [shape((half, B))] * 2,
        [pltpu.VMEM((ROWS, B), BF16), pltpu.VMEM((B, B), BF16)],
        cost(2 * ROWS * B * B, 2 * B * B),
    )(info, parts, *right_parts)
    got = lax.ppermute(send, "core", swap)
    update = jnp.where(
        core == 0, jnp.concatenate([keep, got], 1), jnp.concatenate([got, keep], 1)
    )

    new_stats, new_roots = kernel_call(
        refresh_kernel,
        "refresh",
        [SMEM, SMEM] + [VMEM] * 6,
        [shape((quarter, B), F32)] * 2,
        [pltpu.VMEM((B, B), BF16), pltpu.VMEM((B, B), F32), pltpu.VMEM((B, B), BF16)],
        cost(2 * B ** 3 + 10 * quarter * B * B, 2 * B * B * 2),
    )(info, owner, gathered, old_own, *olds)
    return update[None], new_stats[None, None], new_roots[None, None]


def solution(mesh):
    n_dp, n_mp, n_root = mesh.devices.shape
    fine = Mesh(
        mesh.devices.reshape(X, ZH, CORE, n_mp, n_root), ("x", "zh", "core", "mp", "root")
    )
    dp = ("x", "zh", "core")
    in_specs = (
        P(dp, "mp"),
        P(dp, "root"),
        P("mp", "root", dp, None),
        P("mp", "root", dp, None),
        P(dp, "mp", None),
        P(),
        P(),
    )
    out_specs = (P("mp", dp, "root"), P("root", dp, "mp", None), P("root", dp, "mp", None))
    return jax.shard_map(local, mesh=fine, in_specs=in_specs, out_specs=out_specs, check_vma=False)
```

```python
import functools

import jax
import jax.numpy as jnp
from jax import lax
from jax.experimental import pallas as pl
from jax.experimental.pallas import tpu as pltpu
from jax.sharding import Mesh, PartitionSpec as P

B = 512
DECAY = 0.6
KAPPA = 1.25 ** 4
X, ZH, CORE = 4, 4, 2
CHIPS = X * ZH
PART = B // X
ROWS = B // CHIPS
GRID = ("x", "zh")
F32, BF16 = jnp.float32, jnp.bfloat16
VMEM = pl.BlockSpec(memory_space=pltpu.VMEM)
SMEM = pl.BlockSpec(memory_space=pltpu.SMEM)


def dot(left, right, left_dim=1, right_dim=0):
    dims = (((left_dim,), (right_dim,)), ((), ()))
    return lax.dot_general(left, right, dims, preferred_element_type=F32)


def params():
    return pltpu.CompilerParams(vmem_limit_bytes=32 * 1024 * 1024)


def cost(flops, nbytes):
    return pl.CostEstimate(flops=flops, bytes_accessed=nbytes, transcendentals=0)


def shape(dims, dtype=BF16):
    return jax.ShapeDtypeStruct(dims, dtype)


def other_kernel(index_ref, acts_ref, grads_ref, left_ref, right_ref, turned_ref, out_ref, own_ref, acts_buf, grads_buf, total, sems):
    other = index_ref[0]
    steps, piece = acts_buf.shape[:2]

    def half(which):
        return pl.ds(pl.multiple_of(which * B, B), B)

    copies = []
    for k in range(steps):
        rows = pl.ds(k * piece, piece)
        copies.append(
            (
                pltpu.make_async_copy(acts_ref.at[rows, :], acts_buf.at[k], sems.at[0, k]),
                pltpu.make_async_copy(
                    grads_ref.at[rows, half(other)], grads_buf.at[k], sems.at[1, k]
                ),
            )
        )
        for copy in copies[-1]:
            copy.start()
    last = pltpu.make_async_copy(grads_ref.at[:, half(1 - other)], own_ref, sems.at[2, 0])
    last.start()
    rows = left_ref.shape[2]
    prec = [
        pltpu.make_async_copy(
            ref.at[0, other], out_ref.at[pl.ds(B + side * rows, rows), :], sems.at[3, side]
        )
        for side, ref in enumerate((left_ref, right_ref))
    ]
    for copy in prec:
        copy.start()
    for k, (acts_copy, grads_copy) in enumerate(copies):
        acts_copy.wait()
        turned = acts_buf[k].T
        turned_ref[:, k * piece : (k + 1) * piece] = turned
        grads_copy.wait()
        part = dot(turned, grads_buf[k])
        if k == 0:
            total[...] = part
        elif k < steps - 1:
            total[...] += part
        else:
            out_ref[:B] = (total[...] + part).astype(BF16)
    for copy in (last, *prec):
        copy.wait()


def other_half(acts, grads, prec_left, prec_right, index):
    tokens, rows = acts.shape[0], prec_left.shape[2]
    steps = 2
    anywhere = pl.BlockSpec(memory_space=pl.ANY)
    buffer = pltpu.VMEM((steps, tokens // steps, B), BF16)
    return pl.pallas_call(
        other_kernel,
        in_specs=[SMEM] + [anywhere] * 4,
        out_specs=[VMEM] * 3,
        out_shape=[shape((B, tokens)), shape((B + 2 * rows, B)), shape((tokens, B))],
        scratch_shapes=[
            buffer,
            buffer,
            pltpu.VMEM((B, B), F32),
            pltpu.SemaphoreType.DMA((4, steps)),
        ],
        compiler_params=pltpu.CompilerParams(vmem_limit_bytes=51 * 1024 * 1024),
        cost_estimate=cost(2 * tokens * B * B, 6 * tokens * B),
        name="other_half",
    )(index.reshape(1), acts, grads, prec_left, prec_right)


def own_kernel(turned_ref, grads_ref, out_ref):
    out_ref[...] = dot(turned_ref[...], grads_ref[...])


def join_kernel(index_ref, own_ref, got_ref, left_ref, right_ref, out_ref, prec_ref):
    core = index_ref[0]
    rows = left_ref.shape[2]
    out_ref[...] = (own_ref[...] + got_ref[:B].astype(F32)).astype(BF16).T
    mine = pl.ds(pl.multiple_of(core * rows, rows), rows)
    theirs = pl.ds(pl.multiple_of((1 - core) * rows, rows), rows)
    for side, ref in enumerate((left_ref, right_ref)):
        prec_ref[side, mine, :] = ref[0, core]
        prec_ref[side, theirs, :] = got_ref[B + side * rows : B + (side + 1) * rows]


def shifted(value, axis):
    size = lax.axis_size(axis)
    return [
        lax.ppermute(value, axis, [(at, (at + step) % size) for at in range(size)])
        for step in range(1, size)
    ]


def place(out_ref, parts, index):
    rows = parts[0].shape[0]
    for step, part in enumerate(parts):
        at = (index + len(parts) - step) % len(parts) * rows
        out_ref[pl.ds(pl.multiple_of(at, rows), rows), :] = part[...]


def part_kernel(info_ref, one, two, three, four, *out_refs):
    zh = info_ref[2]
    for side, ref in enumerate(out_refs):
        place(ref, [part.at[side] for part in (one, two, three, four)], zh)


def added(parts_ref):
    total = parts_ref[0].astype(F32)
    for part in range(1, parts_ref.shape[0]):
        total = total + parts_ref[part].astype(F32)
    return total


def sum_kernel(parts_ref, *refs):
    out_ref = refs[-1]
    out_ref[...] = added(parts_ref).astype(BF16)


def pack_kernel(scale, parts_ref, *refs):
    grad_ref, pieces_ref = refs[-2:]
    grad = (added(parts_ref) * scale).astype(BF16)
    grad_ref[...] = grad
    cores, n_mp, n_root, rows, lanes = pieces_ref.shape
    for c in range(cores):
        for m in range(n_mp):
            piece = grad[c * rows : (c + 1) * rows, m * lanes : (m + 1) * lanes]
            for r in range(n_root):
                pieces_ref[c, m, r] = piece


def left_kernel(info_ref, grad_ref, own_ref, one, two, three, out_ref, low, high, prec):
    x, zh = info_ref[1], info_ref[2]
    half, lanes = out_ref.shape[1:]
    for ref, slot in ((low, zh), (high, (zh + 2) % ZH)):
        ref[...] = jnp.zeros_like(ref)
        ref[pl.ds(pl.multiple_of(slot * ROWS, ROWS), ROWS), :] = grad_ref[...]
    place(prec, (own_ref, one, two, three), x)
    rows = prec[...].reshape(CHIPS, ROWS, B)
    out = dot(rows[:, :half].reshape(CHIPS * half, B), low[...], 1, 1)
    out = out + dot(rows[:, half:].reshape(CHIPS * half, B), high[...], 1, 1)
    out_ref[...] = out.astype(BF16).reshape(CHIPS, half, lanes)


def choose_kernel(place_ref, blocks_ref, left_ref, *refs):
    half, out_ref = left_ref.shape[1], refs[-1]
    for j in range(CHIPS):
        out_ref[j, :half] = blocks_ref[place_ref[j]]
        out_ref[j, half:] = left_ref[j]


def spread_kernel(parts_ref, *refs):
    half, out_ref = parts_ref.shape[1] // 2, refs[-1]
    for peer in range(out_ref.shape[0]):
        out_ref[peer] = parts_ref[:, :half]


def update_kernel(info_ref, parts_ref, own_ref, one, two, three, keep_ref, send_ref, left, prec):
    core, x = info_ref[0], info_ref[1]
    half, lanes = keep_ref.shape[0], parts_ref.shape[2]
    place(prec, (own_ref, one, two, three), x)
    slot = lax.broadcasted_iota(jnp.int32, (half, lanes), 1) // ROWS
    for w in range(X):
        low = jnp.zeros((half, lanes), F32)
        high = jnp.zeros((half, lanes), F32)
        for z in range(ZH):
            part = parts_ref[w * ZH + z, half:].astype(F32)
            low = low + jnp.where(slot == z, part, 0.0)
            high = high + jnp.where(slot == (z + 2) % ZH, part, 0.0)
        at = slice(w * lanes, (w + 1) * lanes)
        left[:half, at] = low.astype(BF16)
        left[half:, at] = pltpu.roll(high, lanes // 2, 1).astype(BF16)
    out = dot(left[...], prec[...])
    keep_ref[...] = jnp.where(core == 0, out[:half], out[half:]).astype(BF16)
    send_ref[...] = jnp.where(core == 0, out[half:], out[:half]).astype(BF16)


def refresh_kernel(info_ref, owner_ref, pieces_ref, own_ref, low_ref, one, two, three, stats_ref, roots_ref, block, product, old):
    core, x, zh, mp, root = (info_ref[at] for at in range(5))
    n_mp = pieces_ref.shape[1]
    rows, lanes = pieces_ref.shape[3:]
    quarter = own_ref.shape[0]
    for c in range(CORE):
        for m in range(n_mp):
            for j in range(CHIPS):
                at = j * ROWS + c * rows
                block[at : at + rows, m * lanes : (m + 1) * lanes] = pieces_ref[c, m, j]

    place(old, (low_ref, one, two, three), mp)

    @pl.when(core == 0)
    def _():
        value = block[...]
        product[...] = dot(value, value, 0, 0) * ((1.0 - DECAY) / B)

    @pl.when(core != 0)
    def _():
        value = block[...]
        product[...] = dot(value, value, 1, 1) * ((1.0 - DECAY) / B)

    mine = pl.ds(pl.multiple_of(mp * quarter, quarter), quarter)
    stats_rows = DECAY * own_ref[...] + product[mine, :]
    full = DECAY * old[...].astype(F32) + product[...]
    square = jnp.sum(full * full, axis=0, keepdims=True)
    factor = 2.5 / jnp.sqrt(jnp.sum(square, axis=1, keepdims=True))
    block[...] = (full * (factor * 0.2)).astype(BF16)
    e_rows = stats_rows * (factor * 0.2)
    y = e_rows
    for _ in range(5):
        y = y - dot(y.astype(BF16), block[...])
    line = lax.broadcasted_iota(jnp.int32, (quarter, B), 0) + mp * quarter
    unit = jnp.where(line == lax.broadcasted_iota(jnp.int32, (quarter, B), 1), 1.0, 0.0)
    roots_rows = (jnp.sqrt(jnp.sqrt(factor)) * 1.5625) * (unit - e_rows - KAPPA * y)
    owned = owner_ref[x * ZH + zh] == root
    stats_ref[...] = jnp.where(owned, stats_rows, 0.0)
    roots_ref[...] = jnp.where(owned, roots_rows, 0.0)


def kernel_call(kernel, name, in_specs, out_shape, scratch=(), work=None, awaited=0):
    return pl.pallas_call(
        kernel,
        in_specs=in_specs + [pl.BlockSpec(memory_space=pl.ANY)] * awaited,
        out_specs=[VMEM] * len(out_shape),
        out_shape=out_shape,
        scratch_shapes=list(scratch),
        compiler_params=params(),
        cost_estimate=work,
        name=name,
    )


def local(acts, grads_out, prec_left, prec_right, stats_old, listed, owner):
    x, zh, core = (lax.axis_index(name) for name in ("x", "zh", "core"))
    mp, root = lax.axis_index("mp"), lax.axis_index("root")
    n_mp, n_root = lax.axis_size("mp"), lax.axis_size("root")
    quarter = B // n_mp
    lanes, half = B // n_mp, ROWS // CORE
    tokens = acts.shape[0] * CHIPS * CORE
    swap = ((0, 1), (1, 0))
    info = jnp.stack([core, x, zh, mp, root])

    turned, send, grads_own = other_half(acts, grads_out, prec_left, prec_right, 1 - core)
    got = lax.ppermute(send, "core", swap)
    (own,) = kernel_call(
        own_kernel,
        "own_half",
        [VMEM, VMEM],
        [shape((B, B), F32)],
        work=cost(2 * acts.shape[0] * B * B, 4 * acts.shape[0] * B),
    )(turned, grads_own)
    total, prec = kernel_call(
        join_kernel,
        "join",
        [SMEM] + [VMEM] * 4,
        [shape((B, B)), shape((2, ROWS, B))],
    )(core.reshape(1), own, got, prec_left, prec_right)
    total = lax.all_to_all(total.reshape(X, PART, B), "x", 0, 0)
    got = shifted(prec, "zh")
    (total,) = kernel_call(sum_kernel, "sum_x", [VMEM], [shape((PART, B))], awaited=3)(
        total, *got
    )
    left_part, right_part = kernel_call(
        part_kernel, "prec_rows", [SMEM] + [VMEM] * 4, [shape((PART, B))] * 2
    )(info, prec, *got)
    left_parts = [left_part] + shifted(left_part, "x")
    right_parts = [right_part] + shifted(right_part, "x")
    old_own = stats_old[0]
    old_low = old_own.astype(BF16)
    olds = [old_low] + shifted(old_low, "mp")
    total = lax.all_to_all(total.reshape(ZH, ROWS, B), "zh", 0, 0)
    grad, pieces = kernel_call(
        functools.partial(pack_kernel, tokens ** -0.5),
        "pack",
        [VMEM],
        [shape((ROWS, B)), shape((CORE, n_mp, n_root, half, lanes))],
        awaited=3,
    )(total, *left_parts[1:])

    blocks = lax.all_to_all(pieces.reshape(-1, half, lanes), ("core", "mp", "root"), 0, 0)
    (left,) = kernel_call(
        left_kernel,
        "left",
        [SMEM] + [VMEM] * 5,
        [shape((CHIPS, half, lanes))],
        [pltpu.VMEM((lanes, B), BF16)] * 2 + [pltpu.VMEM((B, B), BF16)],
        cost(4 * CHIPS * half * lanes * B, 2 * B * B),
    )(info, grad, *left_parts)
    at = (listed % 2) * (n_mp * n_root) + listed // 2
    (chosen,) = kernel_call(
        choose_kernel, "choose", [SMEM, VMEM, VMEM], [shape((CHIPS, 2 * half, lanes))], awaited=3
    )(at, blocks, left, *right_parts[1:])
    parts = lax.all_to_all(chosen, GRID, 0, 0)
    (mine,) = kernel_call(
        spread_kernel,
        "spread",
        [VMEM],
        [shape((CORE * n_mp, CHIPS, half, lanes))],
        awaited=3,
    )(parts, *olds[1:])
    gathered = lax.all_to_all(mine, ("core", "mp"), 0, 0)
    gathered = gathered.reshape((CORE, n_mp) + gathered.shape[1:])

    keep, send = kernel_call(
        update_kernel,
        "update",
        [SMEM] + [VMEM] * 5,
        [shape((half, B))] * 2,
        [pltpu.VMEM((ROWS, B), BF16), pltpu.VMEM((B, B), BF16)],
        cost(2 * ROWS * B * B, 2 * B * B),
    )(info, parts, *right_parts)
    got = lax.ppermute(send, "core", swap)
    update = jnp.where(
        core == 0, jnp.concatenate([keep, got], 1), jnp.concatenate([got, keep], 1)
    )

    new_stats, new_roots = kernel_call(
        refresh_kernel,
        "refresh",
        [SMEM, SMEM] + [VMEM] * 6,
        [shape((quarter, B), F32)] * 2,
        [pltpu.VMEM((B, B), BF16), pltpu.VMEM((B, B), F32), pltpu.VMEM((B, B), BF16)],
        cost(2 * B ** 3 + 10 * quarter * B * B, 2 * B * B * 2),
    )(info, owner, gathered, old_own, *olds)
    return update[None], new_stats[None, None], new_roots[None, None]


def solution(mesh):
    n_dp, n_mp, n_root = mesh.devices.shape
    fine = Mesh(
        mesh.devices.reshape(X, ZH, CORE, n_mp, n_root), ("x", "zh", "core", "mp", "root")
    )
    dp = ("x", "zh", "core")
    in_specs = (
        P(dp, "mp"),
        P(dp, "root"),
        P("mp", "root", dp, None),
        P("mp", "root", dp, None),
        P(dp, "mp", None),
        P(),
        P(),
    )
    out_specs = (P("mp", dp, "root"), P("root", dp, "mp", None), P("root", dp, "mp", None))
    return jax.shard_map(local, mesh=fine, in_specs=in_specs, out_specs=out_specs, check_vma=False)
```

```python
import functools

import jax
import jax.numpy as jnp
from jax import lax
from jax.experimental import pallas as pl
from jax.experimental.pallas import tpu as pltpu
from jax.sharding import Mesh, PartitionSpec as P

B = 512
DECAY = 0.6
KAPPA = 1.25 ** 4
X, ZH, CORE = 4, 4, 2
CHIPS = X * ZH
PART = B // X
ROWS = B // CHIPS
F32, BF16 = jnp.float32, jnp.bfloat16
VMEM = pl.BlockSpec(memory_space=pltpu.VMEM)
SMEM = pl.BlockSpec(memory_space=pltpu.SMEM)


def dot(left, right, left_dim=1, right_dim=0):
    dims = (((left_dim,), (right_dim,)), ((), ()))
    return lax.dot_general(left, right, dims, preferred_element_type=F32)


def params():
    return pltpu.CompilerParams(vmem_limit_bytes=32 * 1024 * 1024)


def cost(flops, nbytes):
    return pl.CostEstimate(flops=flops, bytes_accessed=nbytes, transcendentals=0)


def shape(dims, dtype=BF16):
    return jax.ShapeDtypeStruct(dims, dtype)


def other_kernel(index_ref, acts_ref, grads_ref, turned_ref, out_ref, own_ref, acts_buf, grads_buf, total, sems):
    other = index_ref[0]
    steps, piece = acts_buf.shape[:2]

    def half(which):
        return pl.ds(pl.multiple_of(which * B, B), B)

    copies = []
    for k in range(steps):
        rows = pl.ds(k * piece, piece)
        copies.append(
            (
                pltpu.make_async_copy(acts_ref.at[rows, :], acts_buf.at[k], sems.at[0, k]),
                pltpu.make_async_copy(
                    grads_ref.at[rows, half(other)], grads_buf.at[k], sems.at[1, k]
                ),
            )
        )
        for copy in copies[-1]:
            copy.start()
    last = pltpu.make_async_copy(grads_ref.at[:, half(1 - other)], own_ref, sems.at[2, 0])
    last.start()
    for k, (acts_copy, grads_copy) in enumerate(copies):
        acts_copy.wait()
        turned = acts_buf[k].T
        turned_ref[:, k * piece : (k + 1) * piece] = turned
        grads_copy.wait()
        part = dot(turned, grads_buf[k])
        if k == 0:
            total[...] = part
        elif k < steps - 1:
            total[...] += part
        else:
            out_ref[...] = (total[...] + part).astype(BF16)
    last.wait()


def other_half(acts, grads, index):
    tokens, steps = acts.shape[0], 2
    anywhere = pl.BlockSpec(memory_space=pl.ANY)
    buffer = pltpu.VMEM((steps, tokens // steps, B), BF16)
    return pl.pallas_call(
        other_kernel,
        in_specs=[SMEM, anywhere, anywhere],
        out_specs=[VMEM] * 3,
        out_shape=[shape((B, tokens)), shape((B, B)), shape((tokens, B))],
        scratch_shapes=[
            buffer,
            buffer,
            pltpu.VMEM((B, B), F32),
            pltpu.SemaphoreType.DMA((3, steps)),
        ],
        compiler_params=pltpu.CompilerParams(vmem_limit_bytes=51 * 1024 * 1024),
        cost_estimate=cost(2 * tokens * B * B, 6 * tokens * B),
        name="other_half",
    )(index.reshape(1), acts, grads)


def own_kernel(turned_ref, grads_ref, out_ref):
    out_ref[...] = dot(turned_ref[...], grads_ref[...])


def join_kernel(own_ref, got_ref, out_ref):
    out_ref[...] = (own_ref[...] + got_ref[...].astype(F32)).astype(BF16).T


def shift(value, axis, step):
    size = lax.axis_size(axis)
    return lax.ppermute(value, axis, [(at, (at + step) % size) for at in range(size)])


def shifted(value, axis):
    return [shift(value, axis, step) for step in range(1, lax.axis_size(axis))]


def place(out_ref, parts, index):
    rows = parts[0].shape[0]
    for step, part in enumerate(parts):
        at = (index + len(parts) - step) % len(parts) * rows
        out_ref[pl.ds(pl.multiple_of(at, rows), rows), :] = part[...]


def added(parts_ref):
    total = parts_ref[0].astype(F32)
    for part in range(1, parts_ref.shape[0]):
        total = total + parts_ref[part].astype(F32)
    return total


def sum_kernel(info_ref, parts_ref, mine_ref, theirs_ref, *refs):
    keep_ref, left_ref, send_one, send_two = refs[-5:-1]
    right, core = refs[-1], info_ref[0]
    rows = mine_ref.shape[1]
    for side, ref in enumerate((left_ref, right)):
        ref[pl.ds(pl.multiple_of(core * rows, rows), rows), :] = mine_ref[side]
        ref[pl.ds(pl.multiple_of((1 - core) * rows, rows), rows), :] = theirs_ref[side]
    total = added(parts_ref)
    keep_ref[...] = total
    half = PART // 2
    for part, ref in enumerate((send_one, send_two)):
        ref[:half] = total[part * half : (part + 1) * half].astype(BF16)
        ref[half:] = right[part * rows : (part + 1) * rows]


def middle_kernel(keep_ref, sent_one, sent_two, got_one, got_two, out_ref, send_one, send_two):
    half = PART // 2
    for part, (sent, got, ref) in enumerate(
        ((sent_one, got_one, send_one), (sent_two, got_two, send_two))
    ):
        at = slice(part * half, (part + 1) * half)
        total = keep_ref[at] + got[:half].astype(F32)
        out_ref[at] = total
        rows = sent.shape[0] - half
        ref[:half] = total.astype(BF16)
        ref[half : half + rows] = sent[half:]
        ref[half + rows :] = got[half:]


def pack_kernel(scale, info_ref, keep_ref, sent_one, sent_two, got_one, got_two, *refs):
    grad_ref, pieces_ref, right_ref = refs[-3:]
    zh = info_ref[2]
    half, rows = PART // 2, ROWS // 2
    near = zh + 1 - 2 * (zh % 2)
    far = ZH - 1 - zh
    across = far + 1 - 2 * (far % 2)
    for part, (sent, got, mates) in enumerate(
        (
            (sent_one, got_one, (zh, near, far, across)),
            (sent_two, got_two, (zh, far, near, across)),
        )
    ):
        at = slice(part * half, (part + 1) * half)
        grad_ref[at] = ((keep_ref[at] + got[:half].astype(F32)) * scale).astype(BF16)
        for place_at, mate in enumerate(mates):
            source = (sent, got)[place_at // 2]
            start = half + place_at % 2 * rows
            to = pl.multiple_of(mate * ROWS + part * rows, rows)
            right_ref[pl.ds(to, rows), :] = source[start : start + rows]
    cores, n_mp, n_root, rows, lanes = pieces_ref.shape
    for c in range(cores):
        for r in range(n_root):
            at = (c * n_root + r) * rows
            for m in range(n_mp):
                pieces_ref[c, m, r] = grad_ref[at : at + rows, m * lanes : (m + 1) * lanes]


def choose_kernel(info_ref, place_ref, blocks_ref, *refs):
    out_ref = refs[-1]
    for w in range(X):
        out_ref[w] = blocks_ref[place_ref[w * ZH + info_ref[2]]]


def spread_kernel(parts_ref, *refs):
    out_ref = refs[-1]
    for peer in range(out_ref.shape[0]):
        out_ref[peer] = parts_ref[...]


def update_kernel(info_ref, *refs):
    x = info_ref[1]
    sides, (grad, right), outs, (left, total) = refs[:4], refs[4:6], refs[6:10], refs[10:]
    place(left, sides, x)
    total[...] = dot(dot(left[...], grad[...], 1, 1).astype(BF16), right[...])
    for step, ref in enumerate(outs):
        at = pl.multiple_of((x + step) % X * ROWS, ROWS)
        ref[...] = total[pl.ds(at, ROWS), :].astype(ref.dtype)


def halves_kernel(info_ref, own_ref, one, two, three, keep_ref, send_ref):
    core = info_ref[0]
    total = own_ref[...]
    for got in (one, two, three):
        total = total + got[...].astype(F32)
    half = keep_ref.shape[0]
    keep_ref[...] = jnp.where(core == 0, total[:half], total[half:]).astype(BF16)
    send_ref[...] = jnp.where(core == 0, total[half:], total[:half]).astype(BF16)


def refresh_kernel(info_ref, owner_ref, pieces_ref, own_ref, low_ref, one, two, three, stats_ref, roots_ref, block, product, old):
    core, x, zh, mp, root = (info_ref[at] for at in range(5))
    n_mp, n_root = pieces_ref.shape[1:3]
    rows, lanes = pieces_ref.shape[4:]
    quarter = own_ref.shape[0]
    for c in range(CORE):
        for m in range(n_mp):
            for r in range(n_root):
                for w in range(X):
                    at = w * PART + (c * n_root + r) * rows
                    block[at : at + rows, m * lanes : (m + 1) * lanes] = pieces_ref[c, m, r, w]

    place(old, (low_ref, one, two, three), mp)

    @pl.when(core == 0)
    def _():
        value = block[...]
        product[...] = dot(value, value, 0, 0) * ((1.0 - DECAY) / B)

    @pl.when(core != 0)
    def _():
        value = block[...]
        product[...] = dot(value, value, 1, 1) * ((1.0 - DECAY) / B)

    mine = pl.ds(pl.multiple_of(mp * quarter, quarter), quarter)
    stats_rows = DECAY * own_ref[...] + product[mine, :]
    full = DECAY * old[...].astype(F32) + product[...]
    square = jnp.sum(full * full, axis=0, keepdims=True)
    factor = 2.5 / jnp.sqrt(jnp.sum(square, axis=1, keepdims=True))
    block[...] = (full * (factor * 0.2)).astype(BF16)
    e_rows = stats_rows * (factor * 0.2)
    y = e_rows
    for _ in range(5):
        y = y - dot(y.astype(BF16), block[...])
    line = lax.broadcasted_iota(jnp.int32, (quarter, B), 0) + mp * quarter
    unit = jnp.where(line == lax.broadcasted_iota(jnp.int32, (quarter, B), 1), 1.0, 0.0)
    roots_rows = (jnp.sqrt(jnp.sqrt(factor)) * 1.5625) * (unit - e_rows - KAPPA * y)
    owned = owner_ref[x * ZH + zh] == root
    stats_ref[...] = jnp.where(owned, stats_rows, 0.0)
    roots_ref[...] = jnp.where(owned, roots_rows, 0.0)


def kernel_call(kernel, name, in_specs, out_shape, scratch=(), work=None, awaited=0):
    return pl.pallas_call(
        kernel,
        in_specs=in_specs + [pl.BlockSpec(memory_space=pl.ANY)] * awaited,
        out_specs=[VMEM] * len(out_shape),
        out_shape=out_shape,
        scratch_shapes=list(scratch),
        compiler_params=params(),
        cost_estimate=work,
        name=name,
    )


def local(acts, grads_out, prec_left, prec_right, stats_old, listed, owner):
    x, zh, core = (lax.axis_index(name) for name in ("x", "zh", "core"))
    mp, root = lax.axis_index("mp"), lax.axis_index("root")
    n_mp, n_root = lax.axis_size("mp"), lax.axis_size("root")
    quarter = B // n_mp
    lanes, half = B // n_mp, ROWS // CORE
    tokens = acts.shape[0] * CHIPS * CORE
    swap = ((0, 1), (1, 0))
    info = jnp.stack([core, x, zh, mp, root])

    turned, send, grads_own = other_half(acts, grads_out, 1 - core)
    got = lax.ppermute(send, "core", swap)
    (own,) = kernel_call(
        own_kernel,
        "own_half",
        [VMEM, VMEM],
        [shape((B, B), F32)],
        work=cost(2 * acts.shape[0] * B * B, 4 * acts.shape[0] * B),
    )(turned, grads_own)
    (total,) = kernel_call(join_kernel, "join", [VMEM, VMEM], [shape((B, B))])(own, got)
    total = lax.all_to_all(total.reshape(X, PART, B), "x", 0, 0)
    prec = jnp.stack([prec_left[0], prec_right[0]])
    mine = lax.dynamic_index_in_dim(prec, core, 1, keepdims=False)
    theirs = lax.ppermute(
        lax.dynamic_index_in_dim(prec, 1 - core, 1, keepdims=False), "core", swap
    )
    old_own = stats_old[0]
    old_low = old_own.astype(BF16)
    olds = [old_low] + shifted(old_low, "mp")
    keep, left_rows, *sends = kernel_call(
        sum_kernel,
        "sum_x",
        [SMEM] + [VMEM] * 3,
        [shape((PART, B), F32), shape((ROWS, B))] + [shape((PART // 2 + half, B))] * 2,
        [pltpu.VMEM((ROWS, B), BF16)],
        awaited=3,
    )(info, total, mine, theirs, *olds[1:])
    near = [(z, z ^ 1) for z in range(ZH)]
    far = [(z, ZH - 1 - z) for z in range(ZH)]
    got = [lax.ppermute(sends[0], "zh", near), lax.ppermute(sends[1], "zh", far)]
    lefts = [left_rows] + shifted(left_rows, "x")
    keep, *sends = kernel_call(
        middle_kernel,
        "middle",
        [VMEM] * 5,
        [shape((PART, B), F32)] + [shape((PART // 2 + 2 * half, B))] * 2,
    )(keep, *sends, *got)
    got = [lax.ppermute(sends[0], "zh", far), lax.ppermute(sends[1], "zh", near)]
    grad, pieces, right_part = kernel_call(
        functools.partial(pack_kernel, tokens ** -0.5),
        "pack",
        [SMEM] + [VMEM] * 5,
        [shape((PART, B)), shape((CORE, n_mp, n_root, half, lanes)), shape((PART, B))],
        awaited=3,
    )(info, keep, *sends, *got, *lefts[1:])

    blocks = lax.all_to_all(pieces.reshape(-1, half, lanes), ("core", "mp", "root"), 0, 0)

    own, *sends = kernel_call(
        update_kernel,
        "update",
        [SMEM] + [VMEM] * 6,
        [shape((ROWS, B), F32)] + [shape((ROWS, B))] * 3,
        [pltpu.VMEM((PART, B), BF16), pltpu.VMEM((PART, B), F32)],
        cost(2 * PART * B * (PART + B), 6 * PART * B),
    )(info, *lefts, grad, right_part)
    got = [shift(send, "x", step) for step, send in enumerate(sends, 1)]

    at = (listed % 2) * (n_mp * n_root) + listed // 2
    (chosen,) = kernel_call(
        choose_kernel, "choose", [SMEM, SMEM, VMEM], [shape((X, half, lanes))], awaited=3
    )(info, at, blocks, *got)
    parts = lax.all_to_all(chosen, "x", 0, 0)
    (mine,) = kernel_call(
        spread_kernel, "spread", [VMEM], [shape((CORE * n_mp * n_root, X, half, lanes))]
    )(parts)
    gathered = lax.all_to_all(mine, ("core", "mp", "root"), 0, 0)
    gathered = gathered.reshape((CORE, n_mp, n_root) + gathered.shape[1:])
    keep, send = kernel_call(
        halves_kernel, "halves", [SMEM] + [VMEM] * 4, [shape((half, B))] * 2
    )(info, own, *got)
    got = lax.ppermute(send, "core", swap)
    update = jnp.where(
        core == 0, jnp.concatenate([keep, got], 1), jnp.concatenate([got, keep], 1)
    )

    new_stats, new_roots = kernel_call(
        refresh_kernel,
        "refresh",
        [SMEM, SMEM] + [VMEM] * 6,
        [shape((quarter, B), F32)] * 2,
        [pltpu.VMEM((B, B), BF16), pltpu.VMEM((B, B), F32), pltpu.VMEM((B, B), BF16)],
        cost(2 * B ** 3 + 10 * quarter * B * B, 2 * B * B * 2),
    )(info, owner, gathered, old_own, *olds)
    return update[None], new_stats[None, None], new_roots[None, None]


def solution(mesh):
    n_dp, n_mp, n_root = mesh.devices.shape
    fine = Mesh(
        mesh.devices.reshape(X, ZH, CORE, n_mp, n_root), ("x", "zh", "core", "mp", "root")
    )
    dp = ("x", "zh", "core")
    in_specs = (
        P(dp, "mp"),
        P(dp, "root"),
        P("mp", "root", dp, None),
        P("mp", "root", dp, None),
        P(dp, "mp", None),
        P(),
        P(),
    )
    out_specs = (P("mp", dp, "root"), P("root", dp, "mp", None), P("root", dp, "mp", None))
    return jax.shard_map(local, mesh=fine, in_specs=in_specs, out_specs=out_specs, check_vma=False)
```

```python
import functools

import jax
import jax.numpy as jnp
from jax import lax
from jax.experimental import pallas as pl
from jax.experimental.pallas import tpu as pltpu
from jax.sharding import Mesh, PartitionSpec as P

B = 512
DECAY = 0.6
KAPPA = 1.25 ** 4
X, ZH, CORE = 4, 4, 2
CHIPS = X * ZH
PART = B // X
ROWS = B // CHIPS
F32, BF16 = jnp.float32, jnp.bfloat16
VMEM = pl.BlockSpec(memory_space=pltpu.VMEM)
SMEM = pl.BlockSpec(memory_space=pltpu.SMEM)


def dot(left, right, left_dim=1, right_dim=0):
    dims = (((left_dim,), (right_dim,)), ((), ()))
    return lax.dot_general(left, right, dims, preferred_element_type=F32)


def params():
    return pltpu.CompilerParams(vmem_limit_bytes=32 * 1024 * 1024)


def cost(flops, nbytes):
    return pl.CostEstimate(flops=flops, bytes_accessed=nbytes, transcendentals=0)


def shape(dims, dtype=BF16):
    return jax.ShapeDtypeStruct(dims, dtype)


def other_kernel(index_ref, acts_ref, grads_ref, turned_ref, out_ref, own_ref, acts_buf, grads_buf, total, sems):
    other = index_ref[0]
    steps, piece = acts_buf.shape[:2]

    def half(which):
        return pl.ds(pl.multiple_of(which * B, B), B)

    copies = []
    for k in range(steps):
        rows = pl.ds(k * piece, piece)
        copies.append(
            (
                pltpu.make_async_copy(acts_ref.at[rows, :], acts_buf.at[k], sems.at[0, k]),
                pltpu.make_async_copy(
                    grads_ref.at[rows, half(other)], grads_buf.at[k], sems.at[1, k]
                ),
            )
        )
        for copy in copies[-1]:
            copy.start()
    last = pltpu.make_async_copy(grads_ref.at[:, half(1 - other)], own_ref, sems.at[2, 0])
    last.start()
    for k, (acts_copy, grads_copy) in enumerate(copies):
        acts_copy.wait()
        turned = acts_buf[k].T
        turned_ref[:, k * piece : (k + 1) * piece] = turned
        grads_copy.wait()
        part = dot(turned, grads_buf[k])
        if k == 0:
            total[...] = part
        elif k < steps - 1:
            total[...] += part
        else:
            out_ref[...] = (total[...] + part).astype(BF16)
    last.wait()


def other_half(acts, grads, index):
    tokens, steps = acts.shape[0], 2
    anywhere = pl.BlockSpec(memory_space=pl.ANY)
    buffer = pltpu.VMEM((steps, tokens // steps, B), BF16)
    return pl.pallas_call(
        other_kernel,
        in_specs=[SMEM, anywhere, anywhere],
        out_specs=[VMEM] * 3,
        out_shape=[shape((B, tokens)), shape((B, B)), shape((tokens, B))],
        scratch_shapes=[
            buffer,
            buffer,
            pltpu.VMEM((B, B), F32),
            pltpu.SemaphoreType.DMA((3, steps)),
        ],
        compiler_params=pltpu.CompilerParams(vmem_limit_bytes=51 * 1024 * 1024),
        cost_estimate=cost(2 * tokens * B * B, 6 * tokens * B),
        name="other_half",
    )(index.reshape(1), acts, grads)


def own_kernel(turned_ref, grads_ref, out_ref):
    out_ref[...] = dot(turned_ref[...], grads_ref[...])


def join_kernel(own_ref, got_ref, out_ref):
    out_ref[...] = (own_ref[...] + got_ref[...].astype(F32)).astype(BF16).T


def shift(value, axis, step):
    size = lax.axis_size(axis)
    return lax.ppermute(value, axis, [(at, (at + step) % size) for at in range(size)])


def shifted(value, axis):
    return [shift(value, axis, step) for step in range(1, lax.axis_size(axis))]


def place(out_ref, parts, index):
    rows = parts[0].shape[0]
    for step, part in enumerate(parts):
        at = (index + len(parts) - step) % len(parts) * rows
        out_ref[pl.ds(pl.multiple_of(at, rows), rows), :] = part[...]


def added(parts_ref):
    total = parts_ref[0].astype(F32)
    for part in range(1, parts_ref.shape[0]):
        total = total + parts_ref[part].astype(F32)
    return total


def sum_kernel(info_ref, parts_ref, mine_ref, theirs_ref, *refs):
    keep_ref, left_ref, send_one, send_two = refs[-5:-1]
    right, core = refs[-1], info_ref[0]
    rows = mine_ref.shape[1]
    for side, ref in enumerate((left_ref, right)):
        ref[pl.ds(pl.multiple_of(core * rows, rows), rows), :] = mine_ref[side]
        ref[pl.ds(pl.multiple_of((1 - core) * rows, rows), rows), :] = theirs_ref[side]
    total = added(parts_ref)
    keep_ref[...] = total
    half = PART // 2
    for part, ref in enumerate((send_one, send_two)):
        ref[:half] = total[part * half : (part + 1) * half].astype(BF16)
        ref[half:] = right[part * rows : (part + 1) * rows]


def middle_kernel(keep_ref, sent_one, sent_two, got_one, got_two, *refs):
    out_ref, send_one, send_two = refs[-3:]
    half = PART // 2
    for part, (sent, got, ref) in enumerate(
        ((sent_one, got_one, send_one), (sent_two, got_two, send_two))
    ):
        at = slice(part * half, (part + 1) * half)
        total = keep_ref[at] + got[:half].astype(F32)
        out_ref[at] = total
        rows = sent.shape[0] - half
        ref[:half] = total.astype(BF16)
        ref[half : half + rows] = sent[half:]
        ref[half + rows :] = got[half:]


def pack_kernel(scale, info_ref, keep_ref, sent_one, sent_two, got_one, got_two, *refs):
    grad_ref, pieces_ref, right_ref = refs[-3:]
    zh = info_ref[2]
    half, rows = PART // 2, ROWS // 2
    near = zh + 1 - 2 * (zh % 2)
    far = ZH - 1 - zh
    across = far + 1 - 2 * (far % 2)
    for part, (sent, got, mates) in enumerate(
        (
            (sent_one, got_one, (zh, near, far, across)),
            (sent_two, got_two, (zh, far, near, across)),
        )
    ):
        at = slice(part * half, (part + 1) * half)
        grad_ref[at] = ((keep_ref[at] + got[:half].astype(F32)) * scale).astype(BF16)
        for place_at, mate in enumerate(mates):
            source = (sent, got)[place_at // 2]
            start = half + place_at % 2 * rows
            to = pl.multiple_of(mate * ROWS + part * rows, rows)
            right_ref[pl.ds(to, rows), :] = source[start : start + rows]
    cores, n_mp, n_root, rows, lanes = pieces_ref.shape
    for c in range(cores):
        for r in range(n_root):
            at = (c * n_root + r) * rows
            for m in range(n_mp):
                pieces_ref[c, m, r] = grad_ref[at : at + rows, m * lanes : (m + 1) * lanes]


def choose_kernel(info_ref, place_ref, blocks_ref, *refs):
    out_ref = refs[-1]
    for w in range(X):
        out_ref[w] = blocks_ref[place_ref[w * ZH + info_ref[2]]]


def spread_kernel(info_ref, parts_ref, total_ref, out_ref, *outs):
    x = info_ref[1]
    for peer in range(out_ref.shape[0]):
        out_ref[peer] = parts_ref[...]
    for step, ref in enumerate(outs):
        at = pl.multiple_of((x + step) % X * ROWS, ROWS)
        ref[...] = total_ref[pl.ds(at, ROWS), :].astype(ref.dtype)


def update_kernel(info_ref, own_ref, one, two, three, grad_ref, right_ref, out_ref, left):
    place(left, (own_ref, one, two, three), info_ref[1])
    product = dot(left[...], grad_ref[...], 1, 1).astype(BF16)
    out_ref[...] = dot(product, right_ref[...])


def halves_kernel(info_ref, own_ref, one, two, three, keep_ref, send_ref):
    core = info_ref[0]
    total = own_ref[...]
    for got in (one, two, three):
        total = total + got[...].astype(F32)
    half = keep_ref.shape[0]
    keep_ref[...] = jnp.where(core == 0, total[:half], total[half:]).astype(BF16)
    send_ref[...] = jnp.where(core == 0, total[half:], total[:half]).astype(BF16)


def refresh_kernel(info_ref, owner_ref, pieces_ref, own_ref, low_ref, one, two, three, stats_ref, roots_ref, block, product, old):
    core, x, zh, mp, root = (info_ref[at] for at in range(5))
    n_mp, n_root = pieces_ref.shape[1:3]
    rows, lanes = pieces_ref.shape[4:]
    quarter = own_ref.shape[0]
    for c in range(CORE):
        for m in range(n_mp):
            for r in range(n_root):
                for w in range(X):
                    at = w * PART + (c * n_root + r) * rows
                    block[at : at + rows, m * lanes : (m + 1) * lanes] = pieces_ref[c, m, r, w]

    place(old, (low_ref, one, two, three), mp)

    @pl.when(core == 0)
    def _():
        value = block[...]
        product[...] = dot(value, value, 0, 0) * ((1.0 - DECAY) / B)

    @pl.when(core != 0)
    def _():
        value = block[...]
        product[...] = dot(value, value, 1, 1) * ((1.0 - DECAY) / B)

    mine = pl.ds(pl.multiple_of(mp * quarter, quarter), quarter)
    stats_rows = DECAY * own_ref[...] + product[mine, :]
    full = DECAY * old[...].astype(F32) + product[...]
    square = jnp.sum(full * full, axis=0, keepdims=True)
    factor = 2.5 / jnp.sqrt(jnp.sum(square, axis=1, keepdims=True))
    block[...] = (full * (factor * 0.2)).astype(BF16)
    e_rows = stats_rows * (factor * 0.2)
    y = e_rows
    for _ in range(5):
        y = y - dot(y.astype(BF16), block[...])
    line = lax.broadcasted_iota(jnp.int32, (quarter, B), 0) + mp * quarter
    unit = jnp.where(line == lax.broadcasted_iota(jnp.int32, (quarter, B), 1), 1.0, 0.0)
    roots_rows = (jnp.sqrt(jnp.sqrt(factor)) * 1.5625) * (unit - e_rows - KAPPA * y)
    owned = owner_ref[x * ZH + zh] == root
    stats_ref[...] = jnp.where(owned, stats_rows, 0.0)
    roots_ref[...] = jnp.where(owned, roots_rows, 0.0)


def kernel_call(kernel, name, in_specs, out_shape, scratch=(), work=None, awaited=0):
    return pl.pallas_call(
        kernel,
        in_specs=in_specs + [pl.BlockSpec(memory_space=pl.ANY)] * awaited,
        out_specs=[VMEM] * len(out_shape),
        out_shape=out_shape,
        scratch_shapes=list(scratch),
        compiler_params=params(),
        cost_estimate=work,
        name=name,
    )


def local(acts, grads_out, prec_left, prec_right, stats_old, listed, owner):
    x, zh, core = (lax.axis_index(name) for name in ("x", "zh", "core"))
    mp, root = lax.axis_index("mp"), lax.axis_index("root")
    n_mp, n_root = lax.axis_size("mp"), lax.axis_size("root")
    quarter = B // n_mp
    lanes, half = B // n_mp, ROWS // CORE
    tokens = acts.shape[0] * CHIPS * CORE
    swap = ((0, 1), (1, 0))
    info = jnp.stack([core, x, zh, mp, root])

    turned, send, grads_own = other_half(acts, grads_out, 1 - core)
    got = lax.ppermute(send, "core", swap)
    (own,) = kernel_call(
        own_kernel,
        "own_half",
        [VMEM, VMEM],
        [shape((B, B), F32)],
        work=cost(2 * acts.shape[0] * B * B, 4 * acts.shape[0] * B),
    )(turned, grads_own)
    (total,) = kernel_call(join_kernel, "join", [VMEM, VMEM], [shape((B, B))])(own, got)
    total = lax.all_to_all(total.reshape(X, PART, B), "x", 0, 0)
    prec = jnp.stack([prec_left[0], prec_right[0]])
    mine = lax.dynamic_index_in_dim(prec, core, 1, keepdims=False)
    theirs = lax.ppermute(
        lax.dynamic_index_in_dim(prec, 1 - core, 1, keepdims=False), "core", swap
    )
    old_own = stats_old[0]
    old_low = old_own.astype(BF16)
    olds = [old_low] + shifted(old_low, "mp")
    keep, left_rows, *sends = kernel_call(
        sum_kernel,
        "sum_x",
        [SMEM] + [VMEM] * 3,
        [shape((PART, B), F32), shape((ROWS, B))] + [shape((PART // 2 + half, B))] * 2,
        [pltpu.VMEM((ROWS, B), BF16)],
        awaited=1,
    )(info, total, mine, theirs, olds[1])
    near = [(z, z ^ 1) for z in range(ZH)]
    far = [(z, ZH - 1 - z) for z in range(ZH)]
    got = [lax.ppermute(sends[0], "zh", near), lax.ppermute(sends[1], "zh", far)]
    lefts = [left_rows] + shifted(left_rows, "x")
    keep, *sends = kernel_call(
        middle_kernel,
        "middle",
        [VMEM] * 5,
        [shape((PART, B), F32)] + [shape((PART // 2 + 2 * half, B))] * 2,
        awaited=3,
    )(keep, *sends, *got, *lefts[1:])
    got = [lax.ppermute(sends[0], "zh", far), lax.ppermute(sends[1], "zh", near)]
    grad, pieces, right_part = kernel_call(
        functools.partial(pack_kernel, tokens ** -0.5),
        "pack",
        [SMEM] + [VMEM] * 5,
        [shape((PART, B)), shape((CORE, n_mp, n_root, half, lanes)), shape((PART, B))],
        awaited=2,
    )(info, keep, *sends, *got, *olds[2:])

    blocks = lax.all_to_all(pieces.reshape(-1, half, lanes), ("core", "mp", "root"), 0, 0)

    (total,) = kernel_call(
        update_kernel,
        "update",
        [SMEM] + [VMEM] * 6,
        [shape((PART, B), F32)],
        [pltpu.VMEM((PART, B), BF16)],
        cost(2 * PART * B * (PART + B), 6 * PART * B),
    )(info, *lefts, grad, right_part)

    at = (listed % 2) * (n_mp * n_root) + listed // 2
    (chosen,) = kernel_call(
        choose_kernel, "choose", [SMEM, SMEM, VMEM], [shape((X, half, lanes))], awaited=1
    )(info, at, blocks, total)
    parts = lax.all_to_all(chosen, "x", 0, 0)
    mine, own, *sends = kernel_call(
        spread_kernel,
        "spread",
        [SMEM, VMEM, VMEM],
        [shape((CORE * n_mp * n_root, X, half, lanes)), shape((ROWS, B), F32)]
        + [shape((ROWS, B))] * 3,
    )(info, parts, total)
    gathered = lax.all_to_all(mine, ("core", "mp", "root"), 0, 0)
    gathered = gathered.reshape((CORE, n_mp, n_root) + gathered.shape[1:])
    got = [shift(send, "x", step) for step, send in enumerate(sends, 1)]
    keep, send = kernel_call(
        halves_kernel, "halves", [SMEM] + [VMEM] * 4, [shape((half, B))] * 2
    )(info, own, *got)
    got = lax.ppermute(send, "core", swap)
    update = jnp.where(
        core == 0, jnp.concatenate([keep, got], 1), jnp.concatenate([got, keep], 1)
    )

    new_stats, new_roots = kernel_call(
        refresh_kernel,
        "refresh",
        [SMEM, SMEM] + [VMEM] * 6,
        [shape((quarter, B), F32)] * 2,
        [pltpu.VMEM((B, B), BF16), pltpu.VMEM((B, B), F32), pltpu.VMEM((B, B), BF16)],
        cost(2 * B ** 3 + 10 * quarter * B * B, 2 * B * B * 2),
    )(info, owner, gathered, old_own, *olds)
    return update[None], new_stats[None, None], new_roots[None, None]


def solution(mesh):
    n_dp, n_mp, n_root = mesh.devices.shape
    fine = Mesh(
        mesh.devices.reshape(X, ZH, CORE, n_mp, n_root), ("x", "zh", "core", "mp", "root")
    )
    dp = ("x", "zh", "core")
    in_specs = (
        P(dp, "mp"),
        P(dp, "root"),
        P("mp", "root", dp, None),
        P("mp", "root", dp, None),
        P(dp, "mp", None),
        P(),
        P(),
    )
    out_specs = (P("mp", dp, "root"), P("root", dp, "mp", None), P("root", dp, "mp", None))
    return jax.shard_map(local, mesh=fine, in_specs=in_specs, out_specs=out_specs, check_vma=False)
```

```python
import functools

import jax
import jax.numpy as jnp
from jax import lax
from jax.experimental import pallas as pl
from jax.experimental.pallas import tpu as pltpu
from jax.sharding import Mesh, PartitionSpec as P

B = 512
DECAY = 0.6
KAPPA = 1.25 ** 4
X, ZH, CORE = 4, 4, 2
CHIPS = X * ZH
PART = B // X
ROWS = B // CHIPS
F32, BF16 = jnp.float32, jnp.bfloat16
VMEM = pl.BlockSpec(memory_space=pltpu.VMEM)
SMEM = pl.BlockSpec(memory_space=pltpu.SMEM)


def dot(left, right, left_dim=1, right_dim=0):
    dims = (((left_dim,), (right_dim,)), ((), ()))
    return lax.dot_general(left, right, dims, preferred_element_type=F32)


def params():
    return pltpu.CompilerParams(vmem_limit_bytes=32 * 1024 * 1024)


def cost(flops, nbytes):
    return pl.CostEstimate(flops=flops, bytes_accessed=nbytes, transcendentals=0)


def shape(dims, dtype=BF16):
    return jax.ShapeDtypeStruct(dims, dtype)


def other_kernel(index_ref, acts_ref, grads_ref, turned_ref, out_ref, own_ref, acts_buf, grads_buf, total, sems):
    other = index_ref[0]
    steps, piece = acts_buf.shape[:2]

    def half(which):
        return pl.ds(pl.multiple_of(which * B, B), B)

    copies = []
    for k in range(steps):
        rows = pl.ds(k * piece, piece)
        copies.append(
            (
                pltpu.make_async_copy(acts_ref.at[rows, :], acts_buf.at[k], sems.at[0, k]),
                pltpu.make_async_copy(
                    grads_ref.at[rows, half(other)], grads_buf.at[k], sems.at[1, k]
                ),
            )
        )
        for copy in copies[-1]:
            copy.start()
    last = pltpu.make_async_copy(grads_ref.at[:, half(1 - other)], own_ref, sems.at[2, 0])
    last.start()
    for k, (acts_copy, grads_copy) in enumerate(copies):
        acts_copy.wait()
        turned = acts_buf[k].T
        turned_ref[:, k * piece : (k + 1) * piece] = turned
        grads_copy.wait()
        part = dot(turned, grads_buf[k])
        if k == 0:
            total[...] = part
        elif k < steps - 1:
            total[...] += part
        else:
            out_ref[...] = (total[...] + part).astype(BF16)
    last.wait()


def other_half(acts, grads, index):
    tokens, steps = acts.shape[0], 2
    anywhere = pl.BlockSpec(memory_space=pl.ANY)
    buffer = pltpu.VMEM((steps, tokens // steps, B), BF16)
    return pl.pallas_call(
        other_kernel,
        in_specs=[SMEM, anywhere, anywhere],
        out_specs=[VMEM] * 3,
        out_shape=[shape((B, tokens)), shape((B, B)), shape((tokens, B))],
        scratch_shapes=[
            buffer,
            buffer,
            pltpu.VMEM((B, B), F32),
            pltpu.SemaphoreType.DMA((3, steps)),
        ],
        compiler_params=pltpu.CompilerParams(vmem_limit_bytes=51 * 1024 * 1024),
        cost_estimate=cost(2 * tokens * B * B, 6 * tokens * B),
        name="other_half",
    )(index.reshape(1), acts, grads)


def own_kernel(turned_ref, grads_ref, out_ref):
    out_ref[...] = dot(turned_ref[...], grads_ref[...])


def join_kernel(own_ref, got_ref, out_ref):
    out_ref[...] = (own_ref[...] + got_ref[...].astype(F32)).astype(BF16).T


def shift(value, axis, step):
    size = lax.axis_size(axis)
    return lax.ppermute(value, axis, [(at, (at + step) % size) for at in range(size)])


def shifted(value, axis):
    return [shift(value, axis, step) for step in range(1, lax.axis_size(axis))]


def place(out_ref, parts, index):
    rows = parts[0].shape[0]
    for step, part in enumerate(parts):
        at = (index + len(parts) - step) % len(parts) * rows
        out_ref[pl.ds(pl.multiple_of(at, rows), rows), :] = part[...]


def added(parts_ref):
    total = parts_ref[0].astype(F32)
    for part in range(1, parts_ref.shape[0]):
        total = total + parts_ref[part].astype(F32)
    return total


def sum_kernel(info_ref, parts_ref, mine_ref, theirs_ref, *refs):
    keep_ref, left_ref, send_one, send_two = refs[-5:-1]
    right, core = refs[-1], info_ref[0]
    rows = mine_ref.shape[1]
    for side, ref in enumerate((left_ref, right)):
        ref[pl.ds(pl.multiple_of(core * rows, rows), rows), :] = mine_ref[side]
        ref[pl.ds(pl.multiple_of((1 - core) * rows, rows), rows), :] = theirs_ref[side]
    total = added(parts_ref)
    keep_ref[...] = total
    half = PART // 2
    for part, ref in enumerate((send_one, send_two)):
        ref[:half] = total[part * half : (part + 1) * half].astype(BF16)
        ref[half:] = right[part * rows : (part + 1) * rows]


def middle_kernel(keep_ref, sent_one, sent_two, got_one, got_two, *refs):
    out_ref, send_one, send_two = refs[-3:]
    half = PART // 2
    for part, (sent, got, ref) in enumerate(
        ((sent_one, got_one, send_one), (sent_two, got_two, send_two))
    ):
        at = slice(part * half, (part + 1) * half)
        total = keep_ref[at] + got[:half].astype(F32)
        out_ref[at] = total
        rows = sent.shape[0] - half
        ref[:half] = total.astype(BF16)
        ref[half : half + rows] = sent[half:]
        ref[half + rows :] = got[half:]


def pack_kernel(scale, info_ref, keep_ref, sent_one, sent_two, got_one, got_two, *refs):
    grad_ref, pieces_ref, right_ref = refs[-3:]
    zh = info_ref[2]
    half, rows = PART // 2, ROWS // 2
    near = zh + 1 - 2 * (zh % 2)
    far = ZH - 1 - zh
    across = far + 1 - 2 * (far % 2)
    for part, (sent, got, mates) in enumerate(
        (
            (sent_one, got_one, (zh, near, far, across)),
            (sent_two, got_two, (zh, far, near, across)),
        )
    ):
        at = slice(part * half, (part + 1) * half)
        grad_ref[at] = ((keep_ref[at] + got[:half].astype(F32)) * scale).astype(BF16)
        for place_at, mate in enumerate(mates):
            source = (sent, got)[place_at // 2]
            start = half + place_at % 2 * rows
            to = pl.multiple_of(mate * ROWS + part * rows, rows)
            right_ref[pl.ds(to, rows), :] = source[start : start + rows]
    cores, n_mp, n_root, rows, lanes = pieces_ref.shape
    for c in range(cores):
        for r in range(n_root):
            at = (c * n_root + r) * rows
            for m in range(n_mp):
                pieces_ref[c, m, r] = grad_ref[at : at + rows, m * lanes : (m + 1) * lanes]


def cast_kernel(value_ref, *refs):
    refs[-1][...] = value_ref[...].astype(BF16)


def choose_kernel(info_ref, place_ref, blocks_ref, total_ref, *refs):
    out_ref = refs[-1]
    rows, lanes = out_ref.shape[2:]
    for w in range(X):
        tile = blocks_ref[place_ref[w * ZH + info_ref[2]]]
        for c in range(CORE):
            out_ref[w * CORE + c, 0] = tile
            at = w * ROWS + c * rows
            for lane in range(B // lanes):
                part = total_ref[at : at + rows, lane * lanes : (lane + 1) * lanes]
                out_ref[w * CORE + c, 1 + lane] = part.astype(BF16)


def spread_kernel(info_ref, parts_ref, out_ref):
    core = info_ref[0]
    for w in range(X):
        tile = parts_ref[w * CORE + core, 0]
        for peer in range(out_ref.shape[0]):
            out_ref[peer, w] = tile


def finish_kernel(parts_ref, out_ref):
    lanes = parts_ref.shape[3]
    for c in range(CORE):
        for lane in range(B // lanes):
            total = parts_ref[c, 1 + lane].astype(F32)
            for w in range(1, X):
                total = total + parts_ref[w * CORE + c, 1 + lane].astype(F32)
            at = c * B + lane * lanes
            out_ref[:, at : at + lanes] = total.astype(BF16)


def update_kernel(info_ref, own_ref, one, two, three, grad_ref, right_ref, out_ref, left):
    place(left, (own_ref, one, two, three), info_ref[1])
    product = dot(left[...], grad_ref[...], 1, 1).astype(BF16)
    out_ref[...] = dot(product, right_ref[...])


def refresh_kernel(info_ref, owner_ref, mine_ref, theirs_ref, own_ref, low_ref, one, two, three, stats_ref, roots_ref, block, product, old):
    core, x, zh, mp, root = (info_ref[at] for at in range(5))
    n_mp, n_root, _, rows, lanes = mine_ref.shape
    quarter = own_ref.shape[0]
    for ref, side in ((mine_ref, core), (theirs_ref, 1 - core)):
        for r in range(n_root):
            for w in range(X):
                at = pl.ds(pl.multiple_of(w * PART + (side * n_root + r) * rows, rows), rows)
                for m in range(n_mp):
                    block[at, m * lanes : (m + 1) * lanes] = ref[m, r, w]
    place(old, (low_ref, one, two, three), mp)

    @pl.when(core == 0)
    def _():
        value = block[...]
        product[...] = dot(value, value, 0, 0) * ((1.0 - DECAY) / B)

    @pl.when(core != 0)
    def _():
        value = block[...]
        product[...] = dot(value, value, 1, 1) * ((1.0 - DECAY) / B)

    mine = pl.ds(pl.multiple_of(mp * quarter, quarter), quarter)
    stats_rows = DECAY * own_ref[...] + product[mine, :]
    full = DECAY * old[...].astype(F32) + product[...]
    square = jnp.sum(full * full, axis=0, keepdims=True)
    factor = 2.5 / jnp.sqrt(jnp.sum(square, axis=1, keepdims=True))
    block[...] = (full * (factor * 0.2)).astype(BF16)
    e_rows = stats_rows * (factor * 0.2)
    y = e_rows
    for _ in range(5):
        y = y - dot(y.astype(BF16), block[...])
    line = lax.broadcasted_iota(jnp.int32, (quarter, B), 0) + mp * quarter
    unit = jnp.where(line == lax.broadcasted_iota(jnp.int32, (quarter, B), 1), 1.0, 0.0)
    roots_rows = (jnp.sqrt(jnp.sqrt(factor)) * 1.5625) * (unit - e_rows - KAPPA * y)
    owned = owner_ref[x * ZH + zh] == root
    stats_ref[...] = jnp.where(owned, stats_rows, 0.0)
    roots_ref[...] = jnp.where(owned, roots_rows, 0.0)


def kernel_call(kernel, name, in_specs, out_shape, scratch=(), work=None, awaited=0):
    return pl.pallas_call(
        kernel,
        in_specs=in_specs + [pl.BlockSpec(memory_space=pl.ANY)] * awaited,
        out_specs=[VMEM] * len(out_shape),
        out_shape=out_shape,
        scratch_shapes=list(scratch),
        compiler_params=params(),
        cost_estimate=work,
        name=name,
    )


def local(acts, grads_out, prec_left, prec_right, stats_old, listed, owner):
    x, zh, core = (lax.axis_index(name) for name in ("x", "zh", "core"))
    mp, root = lax.axis_index("mp"), lax.axis_index("root")
    n_mp, n_root = lax.axis_size("mp"), lax.axis_size("root")
    quarter = B // n_mp
    lanes, half = B // n_mp, ROWS // CORE
    tokens = acts.shape[0] * CHIPS * CORE
    swap = ((0, 1), (1, 0))
    info = jnp.stack([core, x, zh, mp, root])

    turned, send, grads_own = other_half(acts, grads_out, 1 - core)
    got = lax.ppermute(send, "core", swap)
    (own,) = kernel_call(
        own_kernel,
        "own_half",
        [VMEM, VMEM],
        [shape((B, B), F32)],
        work=cost(2 * acts.shape[0] * B * B, 4 * acts.shape[0] * B),
    )(turned, grads_own)
    (total,) = kernel_call(join_kernel, "join", [VMEM, VMEM], [shape((B, B))])(own, got)
    total = lax.all_to_all(total.reshape(X, PART, B), "x", 0, 0)
    prec = jnp.stack([prec_left[0], prec_right[0]])
    mine = lax.dynamic_index_in_dim(prec, core, 1, keepdims=False)
    theirs = lax.ppermute(
        lax.dynamic_index_in_dim(prec, 1 - core, 1, keepdims=False), "core", swap
    )
    keep, left_rows, *sends = kernel_call(
        sum_kernel,
        "sum_x",
        [SMEM] + [VMEM] * 3,
        [shape((PART, B), F32), shape((ROWS, B))] + [shape((PART // 2 + half, B))] * 2,
        [pltpu.VMEM((ROWS, B), BF16)],
    )(info, total, mine, theirs)
    near = [(z, z ^ 1) for z in range(ZH)]
    far = [(z, ZH - 1 - z) for z in range(ZH)]
    got = [lax.ppermute(sends[0], "zh", near), lax.ppermute(sends[1], "zh", far)]
    lefts = [left_rows] + shifted(left_rows, "x")
    keep, *sends = kernel_call(
        middle_kernel,
        "middle",
        [VMEM] * 5,
        [shape((PART, B), F32)] + [shape((PART // 2 + 2 * half, B))] * 2,
        awaited=3,
    )(keep, *sends, *got, *lefts[1:])
    got = [lax.ppermute(sends[0], "zh", far), lax.ppermute(sends[1], "zh", near)]
    grad, pieces, right_part = kernel_call(
        functools.partial(pack_kernel, tokens ** -0.5),
        "pack",
        [SMEM] + [VMEM] * 5,
        [shape((PART, B)), shape((CORE, n_mp, n_root, half, lanes)), shape((PART, B))],
    )(info, keep, *sends, *got)
    old_own = stats_old[0]
    (old_low,) = kernel_call(
        cast_kernel, "cast", [VMEM], [shape((quarter, B))], awaited=1
    )(old_own, got[0])
    olds = [old_low] + shifted(old_low, "mp")

    blocks = lax.all_to_all(pieces.reshape(-1, half, lanes), ("core", "mp", "root"), 0, 0)

    (total,) = kernel_call(
        update_kernel,
        "update",
        [SMEM] + [VMEM] * 6,
        [shape((PART, B), F32)],
        [pltpu.VMEM((PART, B), BF16)],
        cost(2 * PART * B * (PART + B), 6 * PART * B),
    )(info, *lefts, grad, right_part)

    at = (listed % 2) * (n_mp * n_root) + listed // 2
    (chosen,) = kernel_call(
        choose_kernel,
        "choose",
        [SMEM, SMEM, VMEM, VMEM],
        [shape((X * CORE, 1 + B // lanes, half, lanes))],
        awaited=3,
    )(info, at, blocks, total, *olds[1:])
    parts = lax.all_to_all(chosen, ("x", "core"), 0, 0)
    (mine,) = kernel_call(
        spread_kernel, "spread", [SMEM, VMEM], [shape((n_mp * n_root, X, half, lanes))]
    )(info, parts)
    mine = lax.all_to_all(mine, ("mp", "root"), 0, 0)
    theirs = lax.ppermute(mine, "core", swap)
    gathered = [value.reshape((n_mp, n_root) + value.shape[1:]) for value in (mine, theirs)]
    (update,) = kernel_call(finish_kernel, "finish", [VMEM], [shape((half, 2 * B))])(parts)

    new_stats, new_roots = kernel_call(
        refresh_kernel,
        "refresh",
        [SMEM, SMEM] + [VMEM] * 7,
        [shape((quarter, B), F32)] * 2,
        [pltpu.VMEM((B, B), BF16), pltpu.VMEM((B, B), F32), pltpu.VMEM((B, B), BF16)],
        cost(2 * B ** 3 + 10 * quarter * B * B, 2 * B * B * 2),
    )(info, owner, *gathered, old_own, *olds)
    return update[None], new_stats[None, None], new_roots[None, None]


def solution(mesh):
    n_dp, n_mp, n_root = mesh.devices.shape
    fine = Mesh(
        mesh.devices.reshape(X, ZH, CORE, n_mp, n_root), ("x", "zh", "core", "mp", "root")
    )
    dp = ("x", "zh", "core")
    in_specs = (
        P(dp, "mp"),
        P(dp, "root"),
        P("mp", "root", dp, None),
        P("mp", "root", dp, None),
        P(dp, "mp", None),
        P(),
        P(),
    )
    out_specs = (P("mp", dp, "root"), P("root", dp, "mp", None), P("root", dp, "mp", None))
    return jax.shard_map(local, mesh=fine, in_specs=in_specs, out_specs=out_specs, check_vma=False)
```

```python
import functools

import jax
import jax.numpy as jnp
from jax import lax
from jax.experimental import pallas as pl
from jax.experimental.pallas import tpu as pltpu
from jax.sharding import Mesh, PartitionSpec as P

B = 512
DECAY = 0.6
KAPPA = 1.25 ** 4
X, ZH, CORE = 4, 4, 2
CHIPS = X * ZH
PART = B // X
ROWS = B // CHIPS
F32, BF16 = jnp.float32, jnp.bfloat16
VMEM = pl.BlockSpec(memory_space=pltpu.VMEM)
SMEM = pl.BlockSpec(memory_space=pltpu.SMEM)


def dot(left, right, left_dim=1, right_dim=0):
    dims = (((left_dim,), (right_dim,)), ((), ()))
    return lax.dot_general(left, right, dims, preferred_element_type=F32)


def params():
    return pltpu.CompilerParams(vmem_limit_bytes=32 * 1024 * 1024)


def cost(flops, nbytes):
    return pl.CostEstimate(flops=flops, bytes_accessed=nbytes, transcendentals=0)


def shape(dims, dtype=BF16):
    return jax.ShapeDtypeStruct(dims, dtype)


def other_kernel(index_ref, acts_ref, grads_ref, turned_ref, out_ref, own_ref, acts_buf, grads_buf, total, sems):
    other = index_ref[0]
    steps, piece = acts_buf.shape[:2]

    def half(which):
        return pl.ds(pl.multiple_of(which * B, B), B)

    copies = []
    for k in range(steps):
        rows = pl.ds(k * piece, piece)
        copies.append(
            (
                pltpu.make_async_copy(acts_ref.at[rows, :], acts_buf.at[k], sems.at[0, k]),
                pltpu.make_async_copy(
                    grads_ref.at[rows, half(other)], grads_buf.at[k], sems.at[1, k]
                ),
            )
        )
        for copy in copies[-1]:
            copy.start()
    last = pltpu.make_async_copy(grads_ref.at[:, half(1 - other)], own_ref, sems.at[2, 0])
    last.start()
    for k, (acts_copy, grads_copy) in enumerate(copies):
        acts_copy.wait()
        turned = acts_buf[k].T
        turned_ref[:, k * piece : (k + 1) * piece] = turned
        grads_copy.wait()
        part = dot(turned, grads_buf[k])
        if k == 0:
            total[...] = part
        elif k < steps - 1:
            total[...] += part
        else:
            out_ref[...] = (total[...] + part).astype(BF16)
    last.wait()


def other_half(acts, grads, index):
    tokens, steps = acts.shape[0], 2
    anywhere = pl.BlockSpec(memory_space=pl.ANY)
    buffer = pltpu.VMEM((steps, tokens // steps, B), BF16)
    return pl.pallas_call(
        other_kernel,
        in_specs=[SMEM, anywhere, anywhere],
        out_specs=[VMEM] * 3,
        out_shape=[shape((B, tokens)), shape((B, B)), shape((tokens, B))],
        scratch_shapes=[
            buffer,
            buffer,
            pltpu.VMEM((B, B), F32),
            pltpu.SemaphoreType.DMA((3, steps)),
        ],
        compiler_params=pltpu.CompilerParams(vmem_limit_bytes=51 * 1024 * 1024),
        cost_estimate=cost(2 * tokens * B * B, 6 * tokens * B),
        name="other_half",
    )(index.reshape(1), acts, grads)


def own_kernel(turned_ref, grads_ref, out_ref):
    out_ref[...] = dot(turned_ref[...], grads_ref[...])


def join_kernel(own_ref, got_ref, out_ref):
    out_ref[...] = (own_ref[...] + got_ref[...].astype(F32)).astype(BF16).T


def shift(value, axis, step):
    size = lax.axis_size(axis)
    return lax.ppermute(value, axis, [(at, (at + step) % size) for at in range(size)])


def shifted(value, axis):
    return [shift(value, axis, step) for step in range(1, lax.axis_size(axis))]


def place(out_ref, parts, index):
    rows = parts[0].shape[0]
    for step, part in enumerate(parts):
        at = (index + len(parts) - step) % len(parts) * rows
        out_ref[pl.ds(pl.multiple_of(at, rows), rows), :] = part[...]


def added(parts_ref):
    total = parts_ref[0].astype(F32)
    for part in range(1, parts_ref.shape[0]):
        total = total + parts_ref[part].astype(F32)
    return total


def sum_kernel(info_ref, parts_ref, mine_ref, theirs_ref, *refs):
    keep_ref, left_ref, send_one, send_two = refs[-5:-1]
    right, core = refs[-1], info_ref[0]
    rows = mine_ref.shape[1]
    for side, ref in enumerate((left_ref, right)):
        ref[pl.ds(pl.multiple_of(core * rows, rows), rows), :] = mine_ref[side]
        ref[pl.ds(pl.multiple_of((1 - core) * rows, rows), rows), :] = theirs_ref[side]
    total = added(parts_ref)
    keep_ref[...] = total
    half = PART // 2
    for part, ref in enumerate((send_one, send_two)):
        ref[:half] = total[part * half : (part + 1) * half].astype(BF16)
        ref[half:] = right[part * rows : (part + 1) * rows]


def middle_kernel(keep_ref, sent_one, sent_two, got_one, got_two, *refs):
    out_ref, send_one, send_two = refs[-3:]
    half = PART // 2
    for part, (sent, got, ref) in enumerate(
        ((sent_one, got_one, send_one), (sent_two, got_two, send_two))
    ):
        at = slice(part * half, (part + 1) * half)
        total = keep_ref[at] + got[:half].astype(F32)
        out_ref[at] = total
        rows = sent.shape[0] - half
        ref[:half] = total.astype(BF16)
        ref[half : half + rows] = sent[half:]
        ref[half + rows :] = got[half:]


def pack_kernel(scale, info_ref, keep_ref, sent_one, sent_two, got_one, got_two, *refs):
    grad_ref, pieces_ref, right_ref = refs[-3:]
    zh = info_ref[2]
    half, rows = PART // 2, ROWS // 2
    near = zh + 1 - 2 * (zh % 2)
    far = ZH - 1 - zh
    across = far + 1 - 2 * (far % 2)
    for part, (sent, got, mates) in enumerate(
        (
            (sent_one, got_one, (zh, near, far, across)),
            (sent_two, got_two, (zh, far, near, across)),
        )
    ):
        at = slice(part * half, (part + 1) * half)
        grad_ref[at] = ((keep_ref[at] + got[:half].astype(F32)) * scale).astype(BF16)
        for place_at, mate in enumerate(mates):
            source = (sent, got)[place_at // 2]
            start = half + place_at % 2 * rows
            to = pl.multiple_of(mate * ROWS + part * rows, rows)
            right_ref[pl.ds(to, rows), :] = source[start : start + rows]
    n_mp, n_root, cores, rows, lanes = pieces_ref.shape
    for c in range(cores):
        for r in range(n_root):
            at = (c * n_root + r) * rows
            for m in range(n_mp):
                pieces_ref[m, r, c] = grad_ref[at : at + rows, m * lanes : (m + 1) * lanes]


def copy_kernel(value_ref, *refs):
    refs[-1][...] = value_ref[...]


def choose_kernel(info_ref, listed_ref, blocks_ref, total_ref, *refs):
    out_ref = refs[-1]
    rows, lanes = out_ref.shape[2:]
    for w in range(X):
        pair = listed_ref[w * ZH + info_ref[2]] // 2
        for c in range(CORE):
            out_ref[w * CORE + c, 0] = blocks_ref[pair, c]
            at = w * ROWS + c * rows
            for lane in range(B // lanes):
                part = total_ref[at : at + rows, lane * lanes : (lane + 1) * lanes]
                out_ref[w * CORE + c, 1 + lane] = part.astype(BF16)


def spread_kernel(info_ref, listed_ref, parts_ref, out_ref):
    holder = listed_ref[info_ref[1] * ZH + info_ref[2]] % 2
    for w in range(X):
        tile = parts_ref[w * CORE + holder, 0]
        for peer in range(out_ref.shape[0]):
            out_ref[peer, w] = tile


def finish_kernel(parts_ref, out_ref):
    lanes = parts_ref.shape[3]
    for c in range(CORE):
        for lane in range(B // lanes):
            total = parts_ref[c, 1 + lane].astype(F32)
            for w in range(1, X):
                total = total + parts_ref[w * CORE + c, 1 + lane].astype(F32)
            at = c * B + lane * lanes
            out_ref[:, at : at + lanes] = total.astype(BF16)


def update_kernel(info_ref, own_ref, one, two, three, grad_ref, right_ref, out_ref, left):
    place(left, (own_ref, one, two, three), info_ref[1])
    product = dot(left[...], grad_ref[...], 1, 1).astype(BF16)
    out_ref[...] = dot(product, right_ref[...])


def refresh_kernel(info_ref, owner_ref, mine_ref, theirs_ref, own_ref, low_ref, one, two, three, stats_ref, roots_ref, block, product, old):
    core, x, zh, mp, root = (info_ref[at] for at in range(5))
    n_mp, n_root, _, rows, lanes = mine_ref.shape
    quarter = own_ref.shape[0]
    for ref, side in ((mine_ref, core), (theirs_ref, 1 - core)):
        for r in range(n_root):
            for w in range(X):
                at = pl.ds(pl.multiple_of(w * PART + (side * n_root + r) * rows, rows), rows)
                for m in range(n_mp):
                    block[at, m * lanes : (m + 1) * lanes] = ref[m, r, w]
    place(old, (low_ref, one, two, three), mp)

    @pl.when(core == 0)
    def _():
        value = block[...]
        product[...] = dot(value, value, 0, 0) * ((1.0 - DECAY) / B)

    @pl.when(core != 0)
    def _():
        value = block[...]
        product[...] = dot(value, value, 1, 1) * ((1.0 - DECAY) / B)

    mine = pl.ds(pl.multiple_of(mp * quarter, quarter), quarter)
    stats_rows = DECAY * own_ref[...] + product[mine, :]
    full = DECAY * old[...].astype(F32) + product[...]
    square = jnp.sum(full * full, axis=0, keepdims=True)
    factor = 2.5 / jnp.sqrt(jnp.sum(square, axis=1, keepdims=True))
    block[...] = (full * (factor * 0.2)).astype(BF16)
    e_rows = stats_rows * (factor * 0.2)
    y = e_rows
    for _ in range(5):
        y = y - dot(y.astype(BF16), block[...])
    line = lax.broadcasted_iota(jnp.int32, (quarter, B), 0) + mp * quarter
    unit = jnp.where(line == lax.broadcasted_iota(jnp.int32, (quarter, B), 1), 1.0, 0.0)
    roots_rows = (jnp.sqrt(jnp.sqrt(factor)) * 1.5625) * (unit - e_rows - KAPPA * y)
    owned = owner_ref[x * ZH + zh] == root
    stats_ref[...] = jnp.where(owned, stats_rows, 0.0)
    roots_ref[...] = jnp.where(owned, roots_rows, 0.0)


def kernel_call(kernel, name, in_specs, out_shape, scratch=(), work=None, awaited=0):
    return pl.pallas_call(
        kernel,
        in_specs=in_specs + [pl.BlockSpec(memory_space=pl.ANY)] * awaited,
        out_specs=[VMEM] * len(out_shape),
        out_shape=out_shape,
        scratch_shapes=list(scratch),
        compiler_params=params(),
        cost_estimate=work,
        name=name,
    )


def local(acts, grads_out, prec_left, prec_right, stats_old, listed, owner):
    x, zh, core = (lax.axis_index(name) for name in ("x", "zh", "core"))
    mp, root = lax.axis_index("mp"), lax.axis_index("root")
    n_mp, n_root = lax.axis_size("mp"), lax.axis_size("root")
    quarter = B // n_mp
    lanes, half = B // n_mp, ROWS // CORE
    tokens = acts.shape[0] * CHIPS * CORE
    swap = ((0, 1), (1, 0))
    info = jnp.stack([core, x, zh, mp, root])

    turned, send, grads_own = other_half(acts, grads_out, 1 - core)
    got = lax.ppermute(send, "core", swap)
    (own,) = kernel_call(
        own_kernel,
        "own_half",
        [VMEM, VMEM],
        [shape((B, B), F32)],
        work=cost(2 * acts.shape[0] * B * B, 4 * acts.shape[0] * B),
    )(turned, grads_own)
    (total,) = kernel_call(join_kernel, "join", [VMEM, VMEM], [shape((B, B))])(own, got)
    total = lax.all_to_all(total.reshape(X, PART, B), "x", 0, 0)
    prec = jnp.stack([prec_left[0], prec_right[0]])
    mine = lax.dynamic_index_in_dim(prec, core, 1, keepdims=False)
    theirs = lax.ppermute(
        lax.dynamic_index_in_dim(prec, 1 - core, 1, keepdims=False), "core", swap
    )
    old_own = stats_old[0]
    old_low = old_own.astype(BF16)
    olds = [old_low] + shifted(old_low, "mp")
    keep, left_rows, *sends = kernel_call(
        sum_kernel,
        "sum_x",
        [SMEM] + [VMEM] * 3,
        [shape((PART, B), F32), shape((ROWS, B))] + [shape((PART // 2 + half, B))] * 2,
        [pltpu.VMEM((ROWS, B), BF16)],
        awaited=1,
    )(info, total, mine, theirs, olds[1])
    near = [(z, z ^ 1) for z in range(ZH)]
    far = [(z, ZH - 1 - z) for z in range(ZH)]
    got = [lax.ppermute(sends[0], "zh", near), lax.ppermute(sends[1], "zh", far)]
    lefts = [left_rows, shift(left_rows, "x", 1)]
    keep, *sends = kernel_call(
        middle_kernel,
        "middle",
        [VMEM] * 5,
        [shape((PART, B), F32)] + [shape((PART // 2 + 2 * half, B))] * 2,
        awaited=1,
    )(keep, *sends, *got, lefts[1])
    got = [lax.ppermute(sends[0], "zh", far), lax.ppermute(sends[1], "zh", near)]
    (left_later,) = kernel_call(
        copy_kernel, "left_rows", [VMEM], [shape((ROWS, B))], awaited=1
    )(left_rows, got[0])
    lefts += [shift(left_later, "x", step) for step in range(2, X)]
    grad, pieces, right_part = kernel_call(
        functools.partial(pack_kernel, tokens ** -0.5),
        "pack",
        [SMEM] + [VMEM] * 5,
        [shape((PART, B)), shape((n_mp, n_root, CORE, half, lanes)), shape((PART, B))],
        awaited=2,
    )(info, keep, *sends, *got, *lefts[2:])


    pieces = pieces.reshape((n_mp * n_root,) + pieces.shape[2:])
    blocks = lax.all_to_all(pieces, ("mp", "root"), 0, 0)

    (total,) = kernel_call(
        update_kernel,
        "update",
        [SMEM] + [VMEM] * 6,
        [shape((PART, B), F32)],
        [pltpu.VMEM((PART, B), BF16)],
        cost(2 * PART * B * (PART + B), 6 * PART * B),
    )(info, *lefts, grad, right_part)

    (chosen,) = kernel_call(
        choose_kernel,
        "choose",
        [SMEM, SMEM, VMEM, VMEM],
        [shape((X * CORE, 1 + B // lanes, half, lanes))],
        awaited=1,
    )(info, listed, blocks, total, olds[2])
    parts = lax.all_to_all(chosen, ("x", "core"), 0, 0)
    (mine,) = kernel_call(
        spread_kernel, "spread", [SMEM, SMEM, VMEM], [shape((n_mp * n_root, X, half, lanes))]
    )(info, listed, parts)
    mine = lax.all_to_all(mine, ("mp", "root"), 0, 0)
    theirs = lax.ppermute(mine, "core", swap)
    gathered = [value.reshape((n_mp, n_root) + value.shape[1:]) for value in (mine, theirs)]
    (update,) = kernel_call(finish_kernel, "finish", [VMEM], [shape((half, 2 * B))])(parts)

    new_stats, new_roots = kernel_call(
        refresh_kernel,
        "refresh",
        [SMEM, SMEM] + [VMEM] * 7,
        [shape((quarter, B), F32)] * 2,
        [pltpu.VMEM((B, B), BF16), pltpu.VMEM((B, B), F32), pltpu.VMEM((B, B), BF16)],
        cost(2 * B ** 3 + 10 * quarter * B * B, 2 * B * B * 2),
    )(info, owner, *gathered, old_own, *olds)
    return update[None], new_stats[None, None], new_roots[None, None]


def solution(mesh):
    n_dp, n_mp, n_root = mesh.devices.shape
    fine = Mesh(
        mesh.devices.reshape(X, ZH, CORE, n_mp, n_root), ("x", "zh", "core", "mp", "root")
    )
    dp = ("x", "zh", "core")
    in_specs = (
        P(dp, "mp"),
        P(dp, "root"),
        P("mp", "root", dp, None),
        P("mp", "root", dp, None),
        P(dp, "mp", None),
        P(),
        P(),
    )
    out_specs = (P("mp", dp, "root"), P("root", dp, "mp", None), P("root", dp, "mp", None))
    return jax.shard_map(local, mesh=fine, in_specs=in_specs, out_specs=out_specs, check_vma=False)
```

```python
import functools

import jax
import jax.numpy as jnp
from jax import lax
from jax.experimental import pallas as pl
from jax.experimental.pallas import tpu as pltpu
from jax.sharding import Mesh, PartitionSpec as P

B = 512
DECAY = 0.6
KAPPA = 1.25 ** 4
X, ZH, CORE = 4, 4, 2
CHIPS = X * ZH
PART = B // X
ROWS = B // CHIPS
F32, BF16 = jnp.float32, jnp.bfloat16
VMEM = pl.BlockSpec(memory_space=pltpu.VMEM)
SMEM = pl.BlockSpec(memory_space=pltpu.SMEM)


def dot(left, right, left_dim=1, right_dim=0):
    dims = (((left_dim,), (right_dim,)), ((), ()))
    return lax.dot_general(left, right, dims, preferred_element_type=F32)


def params():
    return pltpu.CompilerParams(vmem_limit_bytes=32 * 1024 * 1024)


def cost(flops, nbytes):
    return pl.CostEstimate(flops=flops, bytes_accessed=nbytes, transcendentals=0)


def shape(dims, dtype=BF16):
    return jax.ShapeDtypeStruct(dims, dtype)


def other_kernel(index_ref, acts_ref, grads_ref, turned_ref, out_ref, own_ref, acts_buf, grads_buf, total, sems):
    other = index_ref[0]
    steps, piece = acts_buf.shape[:2]

    def half(which):
        return pl.ds(pl.multiple_of(which * B, B), B)

    copies = []
    for k in range(steps):
        rows = pl.ds(k * piece, piece)
        copies.append(
            (
                pltpu.make_async_copy(acts_ref.at[rows, :], acts_buf.at[k], sems.at[0, k]),
                pltpu.make_async_copy(
                    grads_ref.at[rows, half(other)], grads_buf.at[k], sems.at[1, k]
                ),
            )
        )
        for copy in copies[-1]:
            copy.start()
    last = pltpu.make_async_copy(grads_ref.at[:, half(1 - other)], own_ref, sems.at[2, 0])
    last.start()
    for k, (acts_copy, grads_copy) in enumerate(copies):
        acts_copy.wait()
        turned = acts_buf[k].T
        turned_ref[:, k * piece : (k + 1) * piece] = turned
        grads_copy.wait()
        part = dot(turned, grads_buf[k])
        if k == 0:
            total[...] = part
        elif k < steps - 1:
            total[...] += part
        else:
            out_ref[...] = (total[...] + part).astype(BF16)
    last.wait()


def other_half(acts, grads, index):
    tokens, steps = acts.shape[0], 2
    anywhere = pl.BlockSpec(memory_space=pl.ANY)
    buffer = pltpu.VMEM((steps, tokens // steps, B), BF16)
    return pl.pallas_call(
        other_kernel,
        in_specs=[SMEM, anywhere, anywhere],
        out_specs=[VMEM] * 3,
        out_shape=[shape((B, tokens)), shape((B, B)), shape((tokens, B))],
        scratch_shapes=[
            buffer,
            buffer,
            pltpu.VMEM((B, B), F32),
            pltpu.SemaphoreType.DMA((3, steps)),
        ],
        compiler_params=pltpu.CompilerParams(vmem_limit_bytes=51 * 1024 * 1024),
        cost_estimate=cost(2 * tokens * B * B, 6 * tokens * B),
        name="other_half",
    )(index.reshape(1), acts, grads)


def own_kernel(turned_ref, grads_ref, out_ref):
    out_ref[...] = dot(turned_ref[...], grads_ref[...])


def join_kernel(index_ref, own_ref, got_ref, mine_ref, theirs_ref, out_ref, right_ref):
    core = index_ref[0]
    rows = mine_ref.shape[1]
    total = (own_ref[...] + got_ref[...].astype(F32)).astype(BF16).T
    mine = pl.ds(pl.multiple_of(core * rows, rows), rows)
    theirs = pl.ds(pl.multiple_of((1 - core) * rows, rows), rows)
    right_ref[mine, :] = mine_ref[1]
    right_ref[theirs, :] = theirs_ref[1]
    mine = pl.ds(pl.multiple_of(PART + core * rows, rows), rows)
    theirs = pl.ds(pl.multiple_of(PART + (1 - core) * rows, rows), rows)
    for w in range(X):
        out_ref[w, :PART] = total[w * PART : (w + 1) * PART]
        out_ref[w, mine, :] = mine_ref[0]
        out_ref[w, theirs, :] = theirs_ref[0]


def shift(value, axis, step):
    size = lax.axis_size(axis)
    return lax.ppermute(value, axis, [(at, (at + step) % size) for at in range(size)])


def shifted(value, axis):
    return [shift(value, axis, step) for step in range(1, lax.axis_size(axis))]


def place(out_ref, parts, index):
    rows = parts[0].shape[0]
    for step, part in enumerate(parts):
        at = (index + len(parts) - step) % len(parts) * rows
        out_ref[pl.ds(pl.multiple_of(at, rows), rows), :] = part[...]


def sum_kernel(parts_ref, *refs):
    keep_ref, left_ref, pieces_ref = refs[-3:]
    total = parts_ref[0, :PART].astype(F32)
    for w in range(X):
        left_ref[w * ROWS : (w + 1) * ROWS] = parts_ref[w, PART:]
        if w:
            total = total + parts_ref[w, :PART].astype(F32)
    keep_ref[...] = total
    n_mp, n_root, cores, rows, lanes = pieces_ref.shape
    for c in range(cores):
        for r in range(n_root):
            at = (c * n_root + r) * rows
            for m in range(n_mp):
                piece = total[at : at + rows, m * lanes : (m + 1) * lanes]
                pieces_ref[m, r, c] = piece.astype(BF16)


def middle_kernel(keep_ref, sent_one, sent_two, got_one, got_two, *refs):
    out_ref, send_one, send_two = refs[-3:]
    half = PART // 2
    for part, (sent, got, ref) in enumerate(
        ((sent_one, got_one, send_one), (sent_two, got_two, send_two))
    ):
        at = slice(part * half, (part + 1) * half)
        total = keep_ref[at] + got[:half].astype(F32)
        out_ref[at] = total
        rows = sent.shape[0] - half
        ref[:half] = total.astype(BF16)
        ref[half : half + rows] = sent[half:]
        ref[half + rows :] = got[half:]


def choose_kernel(listed_ref, blocks_ref, keep_ref, right_ref, out_ref, send_one, send_two):
    for j in range(CHIPS):
        pair = listed_ref[j] // 2
        for c in range(CORE):
            out_ref[j * CORE + c] = blocks_ref[pair, c]
    half, rows = PART // 2, ROWS // 2
    for part, ref in enumerate((send_one, send_two)):
        ref[:half] = keep_ref[part * half : (part + 1) * half].astype(BF16)
        ref[half:] = right_ref[part * rows : (part + 1) * rows]


def spread_kernel(scale, info_ref, listed_ref, parts_ref, *refs):
    out_ref = refs[-1]
    holder = listed_ref[info_ref[1] * ZH + info_ref[2]] % 2
    for w in range(X):
        total = parts_ref[w * ZH * CORE + holder].astype(F32)
        for z in range(1, ZH):
            total = total + parts_ref[(w * ZH + z) * CORE + holder].astype(F32)
        tile = (total * scale).astype(BF16)
        for peer in range(out_ref.shape[0]):
            out_ref[peer, w] = tile


def update_kernel(scale, info_ref, keep_ref, sent_one, sent_two, got_one, got_two, *refs):
    left, out_ref, grad, right, total = refs
    zh = info_ref[2]
    half, rows = PART // 2, ROWS // 2
    near = zh + 1 - 2 * (zh % 2)
    far = ZH - 1 - zh
    across = far + 1 - 2 * (far % 2)
    for part, (sent, got, mates) in enumerate(
        (
            (sent_one, got_one, (zh, near, far, across)),
            (sent_two, got_two, (zh, far, near, across)),
        )
    ):
        at = slice(part * half, (part + 1) * half)
        grad[at] = ((keep_ref[at] + got[:half].astype(F32)) * scale).astype(BF16)
        for place_at, mate in enumerate(mates):
            source = (sent, got)[place_at // 2]
            start = half + place_at % 2 * rows
            to = pl.multiple_of(mate * ROWS + part * rows, rows)
            right[pl.ds(to, rows), :] = source[start : start + rows]
    product = dot(left[...], grad[...], 1, 1).astype(BF16)
    total[...] = dot(product, right[...])
    rows, lanes = out_ref.shape[2:]
    for peer in range(X * CORE):
        for lane in range(B // lanes):
            part = total[peer * rows : (peer + 1) * rows, lane * lanes : (lane + 1) * lanes]
            out_ref[peer, lane] = part.astype(BF16)


def finish_kernel(parts_ref, out_ref):
    lanes = parts_ref.shape[3]
    for c in range(CORE):
        for lane in range(B // lanes):
            total = parts_ref[c, lane].astype(F32)
            for w in range(1, X):
                total = total + parts_ref[w * CORE + c, lane].astype(F32)
            at = c * B + lane * lanes
            out_ref[:, at : at + lanes] = total.astype(BF16)


def refresh_kernel(info_ref, owner_ref, pieces_ref, own_ref, low_ref, one, two, three, stats_ref, roots_ref, block, product, old):
    core, x, zh, mp, root = (info_ref[at] for at in range(5))
    _, n_mp, n_root, _, rows, lanes = pieces_ref.shape
    quarter = own_ref.shape[0]
    for c in range(CORE):
        for r in range(n_root):
            for w in range(X):
                at = w * PART + (c * n_root + r) * rows
                for m in range(n_mp):
                    block[at : at + rows, m * lanes : (m + 1) * lanes] = pieces_ref[c, m, r, w]
    place(old, (low_ref, one, two, three), mp)

    @pl.when(core == 0)
    def _():
        value = block[...]
        product[...] = dot(value, value, 0, 0) * ((1.0 - DECAY) / B)

    @pl.when(core != 0)
    def _():
        value = block[...]
        product[...] = dot(value, value, 1, 1) * ((1.0 - DECAY) / B)

    mine = pl.ds(pl.multiple_of(mp * quarter, quarter), quarter)
    stats_rows = DECAY * own_ref[...] + product[mine, :]
    full = DECAY * old[...].astype(F32) + product[...]
    square = jnp.sum(full * full, axis=0, keepdims=True)
    factor = 2.5 / jnp.sqrt(jnp.sum(square, axis=1, keepdims=True))
    block[...] = (full * (factor * 0.2)).astype(BF16)
    e_rows = stats_rows * (factor * 0.2)
    y = e_rows
    for _ in range(5):
        y = y - dot(y.astype(BF16), block[...])
    line = lax.broadcasted_iota(jnp.int32, (quarter, B), 0) + mp * quarter
    unit = jnp.where(line == lax.broadcasted_iota(jnp.int32, (quarter, B), 1), 1.0, 0.0)
    roots_rows = (jnp.sqrt(jnp.sqrt(factor)) * 1.5625) * (unit - e_rows - KAPPA * y)
    owned = owner_ref[x * ZH + zh] == root
    stats_ref[...] = jnp.where(owned, stats_rows, 0.0)
    roots_ref[...] = jnp.where(owned, roots_rows, 0.0)


def kernel_call(kernel, name, in_specs, out_shape, scratch=(), work=None, awaited=0):
    return pl.pallas_call(
        kernel,
        in_specs=in_specs + [pl.BlockSpec(memory_space=pl.ANY)] * awaited,
        out_specs=[VMEM] * len(out_shape),
        out_shape=out_shape,
        scratch_shapes=list(scratch),
        compiler_params=params(),
        cost_estimate=work,
        name=name,
    )


def local(acts, grads_out, prec_left, prec_right, stats_old, listed, owner):
    x, zh, core = (lax.axis_index(name) for name in ("x", "zh", "core"))
    mp, root = lax.axis_index("mp"), lax.axis_index("root")
    n_mp, n_root = lax.axis_size("mp"), lax.axis_size("root")
    quarter = B // n_mp
    lanes, half = B // n_mp, ROWS // CORE
    tokens = acts.shape[0] * CHIPS * CORE
    swap = ((0, 1), (1, 0))
    info = jnp.stack([core, x, zh, mp, root])

    turned, send, grads_own = other_half(acts, grads_out, 1 - core)
    got = lax.ppermute(send, "core", swap)
    prec = jnp.stack([prec_left[0], prec_right[0]])
    mine = lax.dynamic_index_in_dim(prec, core, 1, keepdims=False)
    theirs = lax.ppermute(
        lax.dynamic_index_in_dim(prec, 1 - core, 1, keepdims=False), "core", swap
    )
    (own,) = kernel_call(
        own_kernel,
        "own_half",
        [VMEM, VMEM],
        [shape((B, B), F32)],
        work=cost(2 * acts.shape[0] * B * B, 4 * acts.shape[0] * B),
    )(turned, grads_own)
    total, right_rows = kernel_call(
        join_kernel,
        "join",
        [SMEM] + [VMEM] * 4,
        [shape((X, PART + ROWS, B)), shape((ROWS, B))],
    )(core.reshape(1), own, got, mine, theirs)
    total = lax.all_to_all(total, "x", 0, 0)
    old_own = stats_old[0]
    old_low = old_own.astype(BF16)
    olds = [old_low] + shifted(old_low, "mp")
    keep, left_part, pieces = kernel_call(
        sum_kernel,
        "sum_x",
        [VMEM],
        [shape((PART, B), F32), shape((PART, B)), shape((n_mp, n_root, CORE, half, lanes))],
        awaited=3,
    )(total, *olds[1:])

    pieces = pieces.reshape((n_mp * n_root,) + pieces.shape[2:])
    blocks = lax.all_to_all(pieces, ("mp", "root"), 0, 0)
    chosen, *sends = kernel_call(
        choose_kernel,
        "choose",
        [SMEM] + [VMEM] * 3,
        [shape((CHIPS * CORE, half, lanes))] + [shape((PART // 2 + half, B))] * 2,
    )(listed, blocks, keep, right_rows)
    parts = lax.all_to_all(chosen, ("x", "zh", "core"), 0, 0)
    near = [(z, z ^ 1) for z in range(ZH)]
    far = [(z, ZH - 1 - z) for z in range(ZH)]
    got = [lax.ppermute(sends[0], "zh", near), lax.ppermute(sends[1], "zh", far)]
    (spread,) = kernel_call(
        functools.partial(spread_kernel, tokens ** -0.5),
        "spread",
        [SMEM, SMEM, VMEM],
        [shape((CORE * n_mp * n_root, X, half, lanes))],
    )(info, listed, parts)
    gathered = lax.all_to_all(spread, ("core", "mp", "root"), 0, 0)
    gathered = gathered.reshape((CORE, n_mp, n_root) + gathered.shape[1:])

    keep, *sends = kernel_call(
        middle_kernel,
        "middle",
        [VMEM] * 5,
        [shape((PART, B), F32)] + [shape((PART // 2 + 2 * half, B))] * 2,
        awaited=1,
    )(keep, *sends, *got, spread)
    got = [lax.ppermute(sends[0], "zh", far), lax.ppermute(sends[1], "zh", near)]
    (send,) = kernel_call(
        functools.partial(update_kernel, tokens ** -0.5),
        "update",
        [SMEM] + [VMEM] * 6,
        [shape((X * CORE, B // lanes, half, lanes))],
        [pltpu.VMEM((PART, B), BF16)] * 2 + [pltpu.VMEM((PART, B), F32)],
        cost(2 * PART * B * (PART + B), 6 * PART * B),
    )(info, keep, *sends, *got, left_part)
    got = lax.all_to_all(send, ("x", "core"), 0, 0)
    (update,) = kernel_call(finish_kernel, "finish", [VMEM], [shape((half, 2 * B))])(got)

    new_stats, new_roots = kernel_call(
        refresh_kernel,
        "refresh",
        [SMEM, SMEM] + [VMEM] * 6,
        [shape((quarter, B), F32)] * 2,
        [pltpu.VMEM((B, B), BF16), pltpu.VMEM((B, B), F32), pltpu.VMEM((B, B), BF16)],
        cost(2 * B ** 3 + 10 * quarter * B * B, 2 * B * B * 2),
    )(info, owner, gathered, old_own, *olds)
    return update[None], new_stats[None, None], new_roots[None, None]


def solution(mesh):
    n_dp, n_mp, n_root = mesh.devices.shape
    fine = Mesh(
        mesh.devices.reshape(X, ZH, CORE, n_mp, n_root), ("x", "zh", "core", "mp", "root")
    )
    dp = ("x", "zh", "core")
    in_specs = (
        P(dp, "mp"),
        P(dp, "root"),
        P("mp", "root", dp, None),
        P("mp", "root", dp, None),
        P(dp, "mp", None),
        P(),
        P(),
    )
    out_specs = (P("mp", dp, "root"), P("root", dp, "mp", None), P("root", dp, "mp", None))
    return jax.shard_map(local, mesh=fine, in_specs=in_specs, out_specs=out_specs, check_vma=False)
```

```python
import functools

import jax
import jax.numpy as jnp
from jax import lax
from jax.experimental import pallas as pl
from jax.experimental.pallas import tpu as pltpu
from jax.sharding import Mesh, PartitionSpec as P

B = 512
DECAY = 0.6
KAPPA = 1.25 ** 4
X, ZH, CORE = 4, 4, 2
CHIPS = X * ZH
PART = B // X
ROWS = B // CHIPS
F32, BF16 = jnp.float32, jnp.bfloat16
VMEM = pl.BlockSpec(memory_space=pltpu.VMEM)
SMEM = pl.BlockSpec(memory_space=pltpu.SMEM)


def dot(left, right, left_dim=1, right_dim=0):
    dims = (((left_dim,), (right_dim,)), ((), ()))
    return lax.dot_general(left, right, dims, preferred_element_type=F32)


def params():
    return pltpu.CompilerParams(vmem_limit_bytes=32 * 1024 * 1024)


def cost(flops, nbytes):
    return pl.CostEstimate(flops=flops, bytes_accessed=nbytes, transcendentals=0)


def shape(dims, dtype=BF16):
    return jax.ShapeDtypeStruct(dims, dtype)


def other_kernel(index_ref, acts_ref, grads_ref, turned_ref, out_ref, own_ref, acts_buf, grads_buf, total, sems):
    other = index_ref[0]
    steps, piece = acts_buf.shape[:2]

    def half(which):
        return pl.ds(pl.multiple_of(which * B, B), B)

    copies = []
    for k in range(steps):
        rows = pl.ds(k * piece, piece)
        copies.append(
            (
                pltpu.make_async_copy(acts_ref.at[rows, :], acts_buf.at[k], sems.at[0, k]),
                pltpu.make_async_copy(
                    grads_ref.at[rows, half(other)], grads_buf.at[k], sems.at[1, k]
                ),
            )
        )
        for copy in copies[-1]:
            copy.start()
    last = pltpu.make_async_copy(grads_ref.at[:, half(1 - other)], own_ref, sems.at[2, 0])
    last.start()
    for k, (acts_copy, grads_copy) in enumerate(copies):
        acts_copy.wait()
        turned = acts_buf[k].T
        turned_ref[:, k * piece : (k + 1) * piece] = turned
        grads_copy.wait()
        part = dot(turned, grads_buf[k])
        if k == 0:
            total[...] = part
        elif k < steps - 1:
            total[...] += part
        else:
            out_ref[...] = (total[...] + part).astype(BF16)
    last.wait()


def other_half(acts, grads, index):
    tokens, steps = acts.shape[0], 2
    anywhere = pl.BlockSpec(memory_space=pl.ANY)
    buffer = pltpu.VMEM((steps, tokens // steps, B), BF16)
    return pl.pallas_call(
        other_kernel,
        in_specs=[SMEM, anywhere, anywhere],
        out_specs=[VMEM] * 3,
        out_shape=[shape((B, tokens)), shape((B, B)), shape((tokens, B))],
        scratch_shapes=[
            buffer,
            buffer,
            pltpu.VMEM((B, B), F32),
            pltpu.SemaphoreType.DMA((3, steps)),
        ],
        compiler_params=pltpu.CompilerParams(vmem_limit_bytes=51 * 1024 * 1024),
        cost_estimate=cost(2 * tokens * B * B, 6 * tokens * B),
        name="other_half",
    )(index.reshape(1), acts, grads)


def own_kernel(turned_ref, grads_ref, out_ref):
    out_ref[...] = dot(turned_ref[...], grads_ref[...])


def join_kernel(index_ref, own_ref, got_ref, mine_ref, theirs_ref, out_ref, right_ref):
    core = index_ref[0]
    rows = mine_ref.shape[1]
    total = (own_ref[...] + got_ref[...].astype(F32)).astype(BF16).T
    mine = pl.ds(pl.multiple_of(core * rows, rows), rows)
    theirs = pl.ds(pl.multiple_of((1 - core) * rows, rows), rows)
    right_ref[mine, :] = mine_ref[1]
    right_ref[theirs, :] = theirs_ref[1]
    mine = pl.ds(pl.multiple_of(PART + core * rows, rows), rows)
    theirs = pl.ds(pl.multiple_of(PART + (1 - core) * rows, rows), rows)
    for w in range(X):
        out_ref[w, :PART] = total[w * PART : (w + 1) * PART]
        out_ref[w, mine, :] = mine_ref[0]
        out_ref[w, theirs, :] = theirs_ref[0]


def shift(value, axis, step):
    size = lax.axis_size(axis)
    return lax.ppermute(value, axis, [(at, (at + step) % size) for at in range(size)])


def shifted(value, axis):
    return [shift(value, axis, step) for step in range(1, lax.axis_size(axis))]


def place(out_ref, parts, index):
    rows = parts[0].shape[0]
    for step, part in enumerate(parts):
        at = (index + len(parts) - step) % len(parts) * rows
        out_ref[pl.ds(pl.multiple_of(at, rows), rows), :] = part[...]


def sum_kernel(parts_ref, *refs):
    keep_ref, left_ref, pieces_ref = refs[-3:]
    total = parts_ref[0, :PART].astype(F32)
    for w in range(X):
        left_ref[w * ROWS : (w + 1) * ROWS] = parts_ref[w, PART:]
        if w:
            total = total + parts_ref[w, :PART].astype(F32)
    keep_ref[...] = total
    cores, n_mp, n_root, rows, lanes = pieces_ref.shape
    for c in range(cores):
        for r in range(n_root):
            at = (c * n_root + r) * rows
            for m in range(n_mp):
                piece = total[at : at + rows, m * lanes : (m + 1) * lanes]
                pieces_ref[c, m, r] = piece.astype(BF16)


def middle_kernel(keep_ref, sent_one, sent_two, got_one, got_two, *refs):
    out_ref, send_one, send_two = refs[-3:]
    half = PART // 2
    for part, (sent, got, ref) in enumerate(
        ((sent_one, got_one, send_one), (sent_two, got_two, send_two))
    ):
        at = slice(part * half, (part + 1) * half)
        total = keep_ref[at] + got[:half].astype(F32)
        out_ref[at] = total
        rows = sent.shape[0] - half
        ref[:half] = total.astype(BF16)
        ref[half : half + rows] = sent[half:]
        ref[half + rows :] = got[half:]


def choose_kernel(place_ref, blocks_ref, keep_ref, right_ref, *refs):
    out_ref, send_one, send_two = refs[-3:]
    for j in range(CHIPS):
        out_ref[j] = blocks_ref[place_ref[j]]
    half, rows = PART // 2, ROWS // 2
    for part, ref in enumerate((send_one, send_two)):
        ref[:half] = keep_ref[part * half : (part + 1) * half].astype(BF16)
        ref[half:] = right_ref[part * rows : (part + 1) * rows]


def spread_kernel(scale, parts_ref, out_ref):
    for w in range(X):
        total = parts_ref[w * ZH].astype(F32)
        for z in range(1, ZH):
            total = total + parts_ref[w * ZH + z].astype(F32)
        tile = (total * scale).astype(BF16)
        for peer in range(out_ref.shape[0]):
            out_ref[peer, w] = tile


def update_kernel(scale, info_ref, keep_ref, sent_one, sent_two, got_one, got_two, *refs):
    left, (out_ref, grad, right, total) = refs[0], refs[-4:]
    zh = info_ref[2]
    half, rows = PART // 2, ROWS // 2
    near = zh + 1 - 2 * (zh % 2)
    far = ZH - 1 - zh
    across = far + 1 - 2 * (far % 2)
    for part, (sent, got, mates) in enumerate(
        (
            (sent_one, got_one, (zh, near, far, across)),
            (sent_two, got_two, (zh, far, near, across)),
        )
    ):
        at = slice(part * half, (part + 1) * half)
        grad[at] = ((keep_ref[at] + got[:half].astype(F32)) * scale).astype(BF16)
        for place_at, mate in enumerate(mates):
            source = (sent, got)[place_at // 2]
            start = half + place_at % 2 * rows
            to = pl.multiple_of(mate * ROWS + part * rows, rows)
            right[pl.ds(to, rows), :] = source[start : start + rows]
    product = dot(left[...], grad[...], 1, 1).astype(BF16)
    total[...] = dot(product, right[...])
    rows, lanes = out_ref.shape[2:]
    for peer in range(X * CORE):
        for lane in range(B // lanes):
            part = total[peer * rows : (peer + 1) * rows, lane * lanes : (lane + 1) * lanes]
            out_ref[peer, lane] = part.astype(BF16)


def finish_kernel(parts_ref, out_ref):
    lanes = parts_ref.shape[3]
    for c in range(CORE):
        for lane in range(B // lanes):
            total = parts_ref[c, lane].astype(F32)
            for w in range(1, X):
                total = total + parts_ref[w * CORE + c, lane].astype(F32)
            at = c * B + lane * lanes
            out_ref[:, at : at + lanes] = total.astype(BF16)


def refresh_kernel(info_ref, owner_ref, pieces_ref, own_ref, low_ref, one, two, three, stats_ref, roots_ref, block, product, old):
    core, x, zh, mp, root = (info_ref[at] for at in range(5))
    _, n_mp, n_root, _, rows, lanes = pieces_ref.shape
    quarter = own_ref.shape[0]
    for c in range(CORE):
        for r in range(n_root):
            for w in range(X):
                at = w * PART + (c * n_root + r) * rows
                for m in range(n_mp):
                    block[at : at + rows, m * lanes : (m + 1) * lanes] = pieces_ref[c, m, r, w]
    place(old, (low_ref, one, two, three), mp)

    @pl.when(core == 0)
    def _():
        value = block[...]
        product[...] = dot(value, value, 0, 0) * ((1.0 - DECAY) / B)

    @pl.when(core != 0)
    def _():
        value = block[...]
        product[...] = dot(value, value, 1, 1) * ((1.0 - DECAY) / B)

    mine = pl.ds(pl.multiple_of(mp * quarter, quarter), quarter)
    stats_rows = DECAY * own_ref[...] + product[mine, :]
    full = DECAY * old[...].astype(F32) + product[...]
    square = jnp.sum(full * full, axis=0, keepdims=True)
    factor = 2.5 / jnp.sqrt(jnp.sum(square, axis=1, keepdims=True))
    block[...] = (full * (factor * 0.2)).astype(BF16)
    e_rows = stats_rows * (factor * 0.2)
    y = e_rows
    for _ in range(5):
        y = y - dot(y.astype(BF16), block[...])
    line = lax.broadcasted_iota(jnp.int32, (quarter, B), 0) + mp * quarter
    unit = jnp.where(line == lax.broadcasted_iota(jnp.int32, (quarter, B), 1), 1.0, 0.0)
    roots_rows = (jnp.sqrt(jnp.sqrt(factor)) * 1.5625) * (unit - e_rows - KAPPA * y)
    owned = owner_ref[x * ZH + zh] == root
    stats_ref[...] = jnp.where(owned, stats_rows, 0.0)
    roots_ref[...] = jnp.where(owned, roots_rows, 0.0)


def kernel_call(kernel, name, in_specs, out_shape, scratch=(), work=None, awaited=0):
    return pl.pallas_call(
        kernel,
        in_specs=in_specs + [pl.BlockSpec(memory_space=pl.ANY)] * awaited,
        out_specs=[VMEM] * len(out_shape),
        out_shape=out_shape,
        scratch_shapes=list(scratch),
        compiler_params=params(),
        cost_estimate=work,
        name=name,
    )


def local(acts, grads_out, prec_left, prec_right, stats_old, listed, owner):
    x, zh, core = (lax.axis_index(name) for name in ("x", "zh", "core"))
    mp, root = lax.axis_index("mp"), lax.axis_index("root")
    n_mp, n_root = lax.axis_size("mp"), lax.axis_size("root")
    quarter = B // n_mp
    lanes, half = B // n_mp, ROWS // CORE
    tokens = acts.shape[0] * CHIPS * CORE
    swap = ((0, 1), (1, 0))
    info = jnp.stack([core, x, zh, mp, root])

    turned, send, grads_own = other_half(acts, grads_out, 1 - core)
    got = lax.ppermute(send, "core", swap)
    prec = jnp.stack([prec_left[0], prec_right[0]])
    mine = lax.dynamic_index_in_dim(prec, core, 1, keepdims=False)
    theirs = lax.ppermute(
        lax.dynamic_index_in_dim(prec, 1 - core, 1, keepdims=False), "core", swap
    )
    (own,) = kernel_call(
        own_kernel,
        "own_half",
        [VMEM, VMEM],
        [shape((B, B), F32)],
        work=cost(2 * acts.shape[0] * B * B, 4 * acts.shape[0] * B),
    )(turned, grads_own)
    total, right_rows = kernel_call(
        join_kernel,
        "join",
        [SMEM] + [VMEM] * 4,
        [shape((X, PART + ROWS, B)), shape((ROWS, B))],
    )(core.reshape(1), own, got, mine, theirs)
    total = lax.all_to_all(total, "x", 0, 0)
    old_own = stats_old[0]
    old_low = old_own.astype(BF16)
    olds = [old_low] + shifted(old_low, "mp")
    keep, left_part, pieces = kernel_call(
        sum_kernel,
        "sum_x",
        [VMEM],
        [shape((PART, B), F32), shape((PART, B)), shape((CORE, n_mp, n_root, half, lanes))],
        awaited=2,
    )(total, *olds[1:3])

    pieces = pieces.reshape((-1,) + pieces.shape[3:])
    blocks = lax.all_to_all(pieces, ("core", "mp", "root"), 0, 0)
    at = (listed % 2) * (n_mp * n_root) + listed // 2
    chosen, *sends = kernel_call(
        choose_kernel,
        "choose",
        [SMEM] + [VMEM] * 3,
        [shape((CHIPS, half, lanes))] + [shape((PART // 2 + half, B))] * 2,
        awaited=1,
    )(at, blocks, keep, right_rows, olds[3])
    parts = lax.all_to_all(chosen, ("x", "zh"), 0, 0)
    near = [(z, z ^ 1) for z in range(ZH)]
    far = [(z, ZH - 1 - z) for z in range(ZH)]
    got = [lax.ppermute(sends[0], "zh", near), lax.ppermute(sends[1], "zh", far)]
    (spread,) = kernel_call(
        functools.partial(spread_kernel, tokens ** -0.5),
        "spread",
        [VMEM],
        [shape((CORE * n_mp * n_root, X, half, lanes))],
    )(parts)
    gathered = lax.all_to_all(spread, ("core", "mp", "root"), 0, 0)
    gathered = gathered.reshape((CORE, n_mp, n_root) + gathered.shape[1:])

    keep, *sends = kernel_call(
        middle_kernel,
        "middle",
        [VMEM] * 5,
        [shape((PART, B), F32)] + [shape((PART // 2 + 2 * half, B))] * 2,
        awaited=1,
    )(keep, *sends, *got, spread)
    got = [lax.ppermute(sends[0], "zh", far), lax.ppermute(sends[1], "zh", near)]
    (send,) = kernel_call(
        functools.partial(update_kernel, tokens ** -0.5),
        "update",
        [SMEM] + [VMEM] * 6,
        [shape((X * CORE, B // lanes, half, lanes))],
        [pltpu.VMEM((PART, B), BF16)] * 2 + [pltpu.VMEM((PART, B), F32)],
        cost(2 * PART * B * (PART + B), 6 * PART * B),
        awaited=1,
    )(info, keep, *sends, *got, left_part, gathered)
    got = lax.all_to_all(send, ("x", "core"), 0, 0)
    (update,) = kernel_call(finish_kernel, "finish", [VMEM], [shape((half, 2 * B))])(got)

    new_stats, new_roots = kernel_call(
        refresh_kernel,
        "refresh",
        [SMEM, SMEM] + [VMEM] * 6,
        [shape((quarter, B), F32)] * 2,
        [pltpu.VMEM((B, B), BF16), pltpu.VMEM((B, B), F32), pltpu.VMEM((B, B), BF16)],
        cost(2 * B ** 3 + 10 * quarter * B * B, 2 * B * B * 2),
    )(info, owner, gathered, old_own, *olds)
    return update[None], new_stats[None, None], new_roots[None, None]


def solution(mesh):
    n_dp, n_mp, n_root = mesh.devices.shape
    fine = Mesh(
        mesh.devices.reshape(X, ZH, CORE, n_mp, n_root), ("x", "zh", "core", "mp", "root")
    )
    dp = ("x", "zh", "core")
    in_specs = (
        P(dp, "mp"),
        P(dp, "root"),
        P("mp", "root", dp, None),
        P("mp", "root", dp, None),
        P(dp, "mp", None),
        P(),
        P(),
    )
    out_specs = (P("mp", dp, "root"), P("root", dp, "mp", None), P("root", dp, "mp", None))
    return jax.shard_map(local, mesh=fine, in_specs=in_specs, out_specs=out_specs, check_vma=False)
```

```python
import functools

import jax
import jax.numpy as jnp
from jax import lax
from jax.experimental import pallas as pl
from jax.experimental.pallas import tpu as pltpu
from jax.sharding import Mesh, PartitionSpec as P

B = 512
DECAY = 0.6
KAPPA = 1.25 ** 4
X, ZH, CORE = 4, 4, 2
CHIPS = X * ZH
PART = B // X
ROWS = B // CHIPS
F32, BF16 = jnp.float32, jnp.bfloat16
VMEM = pl.BlockSpec(memory_space=pltpu.VMEM)
SMEM = pl.BlockSpec(memory_space=pltpu.SMEM)


def dot(left, right, left_dim=1, right_dim=0):
    dims = (((left_dim,), (right_dim,)), ((), ()))
    return lax.dot_general(left, right, dims, preferred_element_type=F32)


def params():
    return pltpu.CompilerParams(vmem_limit_bytes=32 * 1024 * 1024)


def cost(flops, nbytes):
    return pl.CostEstimate(flops=flops, bytes_accessed=nbytes, transcendentals=0)


def shape(dims, dtype=BF16):
    return jax.ShapeDtypeStruct(dims, dtype)


def other_kernel(index_ref, acts_ref, grads_ref, turned_ref, out_ref, own_ref, acts_buf, grads_buf, total, sems):
    other = index_ref[0]
    steps, piece = acts_buf.shape[:2]

    def half(which):
        return pl.ds(pl.multiple_of(which * B, B), B)

    copies = []
    for k in range(steps):
        rows = pl.ds(k * piece, piece)
        copies.append(
            (
                pltpu.make_async_copy(acts_ref.at[rows, :], acts_buf.at[k], sems.at[0, k]),
                pltpu.make_async_copy(
                    grads_ref.at[rows, half(other)], grads_buf.at[k], sems.at[1, k]
                ),
            )
        )
        for copy in copies[-1]:
            copy.start()
    last = pltpu.make_async_copy(grads_ref.at[:, half(1 - other)], own_ref, sems.at[2, 0])
    last.start()
    for k, (acts_copy, grads_copy) in enumerate(copies):
        acts_copy.wait()
        turned = acts_buf[k].T
        turned_ref[:, k * piece : (k + 1) * piece] = turned
        grads_copy.wait()
        part = dot(turned, grads_buf[k])
        if k == 0:
            total[...] = part
        elif k < steps - 1:
            total[...] += part
        else:
            out_ref[...] = (total[...] + part).astype(BF16)
    last.wait()


def other_half(acts, grads, index):
    tokens, steps = acts.shape[0], 2
    anywhere = pl.BlockSpec(memory_space=pl.ANY)
    buffer = pltpu.VMEM((steps, tokens // steps, B), BF16)
    return pl.pallas_call(
        other_kernel,
        in_specs=[SMEM, anywhere, anywhere],
        out_specs=[VMEM] * 3,
        out_shape=[shape((B, tokens)), shape((B, B)), shape((tokens, B))],
        scratch_shapes=[
            buffer,
            buffer,
            pltpu.VMEM((B, B), F32),
            pltpu.SemaphoreType.DMA((3, steps)),
        ],
        compiler_params=pltpu.CompilerParams(vmem_limit_bytes=51 * 1024 * 1024),
        cost_estimate=cost(2 * tokens * B * B, 6 * tokens * B),
        name="other_half",
    )(index.reshape(1), acts, grads)


def own_kernel(turned_ref, grads_ref, out_ref):
    out_ref[...] = dot(turned_ref[...], grads_ref[...])


def join_kernel(index_ref, own_ref, got_ref, mine_ref, theirs_ref, out_ref, right_ref):
    core = index_ref[0]
    rows = mine_ref.shape[1]
    total = (own_ref[...] + got_ref[...].astype(F32)).astype(BF16).T
    mine = pl.ds(pl.multiple_of(core * rows, rows), rows)
    theirs = pl.ds(pl.multiple_of((1 - core) * rows, rows), rows)
    right_ref[mine, :] = mine_ref[1]
    right_ref[theirs, :] = theirs_ref[1]
    mine = pl.ds(pl.multiple_of(PART + core * rows, rows), rows)
    theirs = pl.ds(pl.multiple_of(PART + (1 - core) * rows, rows), rows)
    for w in range(X):
        out_ref[w, :PART] = total[w * PART : (w + 1) * PART]
        out_ref[w, mine, :] = mine_ref[0]
        out_ref[w, theirs, :] = theirs_ref[0]


def shift(value, axis, step):
    size = lax.axis_size(axis)
    return lax.ppermute(value, axis, [(at, (at + step) % size) for at in range(size)])


def shifted(value, axis):
    return [shift(value, axis, step) for step in range(1, lax.axis_size(axis))]


def place(out_ref, parts, index):
    rows = parts[0].shape[0]
    for step, part in enumerate(parts):
        at = (index + len(parts) - step) % len(parts) * rows
        out_ref[pl.ds(pl.multiple_of(at, rows), rows), :] = part[...]


def sum_kernel(parts_ref, right_ref, *refs):
    keep_ref, left_ref, send_ref = refs[-3:]
    total = parts_ref[0, :PART].astype(F32)
    for w in range(X):
        left_ref[w * ROWS : (w + 1) * ROWS] = parts_ref[w, PART:]
        if w:
            total = total + parts_ref[w, :PART].astype(F32)
    keep_ref[...] = total
    send_ref[:PART] = total.astype(BF16)
    send_ref[PART:] = right_ref[...]


def middle_kernel(keep_ref, right_ref, got_ref, out_ref, send_ref):
    total = keep_ref[...] + got_ref[:PART].astype(F32)
    out_ref[...] = total
    send_ref[:PART] = total.astype(BF16)
    send_ref[PART : PART + ROWS] = right_ref[...]
    send_ref[PART + ROWS :] = got_ref[PART:]


def pack_kernel(scale, info_ref, keep_ref, sent_ref, got_ref, grad_ref, pieces_ref, right_ref):
    core, zh = info_ref[0], info_ref[2]
    grad = ((keep_ref[...] + got_ref[:PART].astype(F32)) * scale).astype(BF16)
    grad_ref[...] = grad
    near = zh + 1 - 2 * (zh % 2)
    far = ZH - 1 - zh
    across = far + 1 - 2 * (far % 2)
    first = jnp.where(core == 0, near, far)
    second = jnp.where(core == 0, far, near)
    for place_at, mate in enumerate((zh, first, second, across)):
        source = (sent_ref, got_ref)[place_at // 2]
        start = PART + place_at % 2 * ROWS
        to = pl.multiple_of(mate * ROWS, ROWS)
        right_ref[pl.ds(to, ROWS), :] = source[start : start + ROWS]
    n_mp, n_root, cores, rows, lanes = pieces_ref.shape
    for c in range(cores):
        for r in range(n_root):
            at = (c * n_root + r) * rows
            for m in range(n_mp):
                pieces_ref[m, r, c] = grad[at : at + rows, m * lanes : (m + 1) * lanes]


def choose_kernel(info_ref, listed_ref, blocks_ref, total_ref, *refs):
    out_ref = refs[-1]
    rows, lanes = out_ref.shape[2:]
    for w in range(X):
        pair = listed_ref[w * ZH + info_ref[2]] // 2
        for c in range(CORE):
            out_ref[w * CORE + c, 0] = blocks_ref[pair, c]
            at = w * ROWS + c * rows
            for lane in range(B // lanes):
                part = total_ref[at : at + rows, lane * lanes : (lane + 1) * lanes]
                out_ref[w * CORE + c, 1 + lane] = part.astype(BF16)


def spread_kernel(info_ref, listed_ref, parts_ref, out_ref):
    holder = listed_ref[info_ref[1] * ZH + info_ref[2]] % 2
    for w in range(X):
        tile = parts_ref[w * CORE + holder, 0]
        for peer in range(out_ref.shape[0]):
            out_ref[peer, w] = tile


def finish_kernel(parts_ref, out_ref):
    lanes = parts_ref.shape[3]
    for c in range(CORE):
        for lane in range(B // lanes):
            total = parts_ref[c, 1 + lane].astype(F32)
            for w in range(1, X):
                total = total + parts_ref[w * CORE + c, 1 + lane].astype(F32)
            at = c * B + lane * lanes
            out_ref[:, at : at + lanes] = total.astype(BF16)


def update_kernel(left_ref, grad_ref, right_ref, out_ref):
    product = dot(left_ref[...], grad_ref[...], 1, 1).astype(BF16)
    out_ref[...] = dot(product, right_ref[...])


def refresh_kernel(info_ref, owner_ref, mine_ref, theirs_ref, own_ref, low_ref, one, two, three, stats_ref, roots_ref, block, product, old):
    core, x, zh, mp, root = (info_ref[at] for at in range(5))
    n_mp, n_root, _, rows, lanes = mine_ref.shape
    quarter = own_ref.shape[0]
    for ref, side in ((mine_ref, core), (theirs_ref, 1 - core)):
        for r in range(n_root):
            for w in range(X):
                at = pl.ds(pl.multiple_of(w * PART + (side * n_root + r) * rows, rows), rows)
                for m in range(n_mp):
                    block[at, m * lanes : (m + 1) * lanes] = ref[m, r, w]
    place(old, (low_ref, one, two, three), mp)

    @pl.when(core == 0)
    def _():
        value = block[...]
        product[...] = dot(value, value, 0, 0) * ((1.0 - DECAY) / B)

    @pl.when(core != 0)
    def _():
        value = block[...]
        product[...] = dot(value, value, 1, 1) * ((1.0 - DECAY) / B)

    mine = pl.ds(pl.multiple_of(mp * quarter, quarter), quarter)
    stats_rows = DECAY * own_ref[...] + product[mine, :]
    full = DECAY * old[...].astype(F32) + product[...]
    square = jnp.sum(full * full, axis=0, keepdims=True)
    factor = 2.5 / jnp.sqrt(jnp.sum(square, axis=1, keepdims=True))
    block[...] = (full * (factor * 0.2)).astype(BF16)
    e_rows = stats_rows * (factor * 0.2)
    y = e_rows
    for _ in range(5):
        y = y - dot(y.astype(BF16), block[...])
    line = lax.broadcasted_iota(jnp.int32, (quarter, B), 0) + mp * quarter
    unit = jnp.where(line == lax.broadcasted_iota(jnp.int32, (quarter, B), 1), 1.0, 0.0)
    roots_rows = (jnp.sqrt(jnp.sqrt(factor)) * 1.5625) * (unit - e_rows - KAPPA * y)
    owned = owner_ref[x * ZH + zh] == root
    stats_ref[...] = jnp.where(owned, stats_rows, 0.0)
    roots_ref[...] = jnp.where(owned, roots_rows, 0.0)


def kernel_call(kernel, name, in_specs, out_shape, scratch=(), work=None, awaited=0):
    return pl.pallas_call(
        kernel,
        in_specs=in_specs + [pl.BlockSpec(memory_space=pl.ANY)] * awaited,
        out_specs=[VMEM] * len(out_shape),
        out_shape=out_shape,
        scratch_shapes=list(scratch),
        compiler_params=params(),
        cost_estimate=work,
        name=name,
    )


def local(acts, grads_out, prec_left, prec_right, stats_old, listed, owner):
    x, zh, core = (lax.axis_index(name) for name in ("x", "zh", "core"))
    mp, root = lax.axis_index("mp"), lax.axis_index("root")
    n_mp, n_root = lax.axis_size("mp"), lax.axis_size("root")
    quarter = B // n_mp
    lanes, half = B // n_mp, ROWS // CORE
    tokens = acts.shape[0] * CHIPS * CORE
    swap = ((0, 1), (1, 0))
    info = jnp.stack([core, x, zh, mp, root])

    turned, send, grads_own = other_half(acts, grads_out, 1 - core)
    got = lax.ppermute(send, "core", swap)
    prec = jnp.stack([prec_left[0], prec_right[0]])
    mine = lax.dynamic_index_in_dim(prec, core, 1, keepdims=False)
    theirs = lax.ppermute(
        lax.dynamic_index_in_dim(prec, 1 - core, 1, keepdims=False), "core", swap
    )
    (own,) = kernel_call(
        own_kernel,
        "own_half",
        [VMEM, VMEM],
        [shape((B, B), F32)],
        work=cost(2 * acts.shape[0] * B * B, 4 * acts.shape[0] * B),
    )(turned, grads_own)
    total, right_rows = kernel_call(
        join_kernel,
        "join",
        [SMEM] + [VMEM] * 4,
        [shape((X, PART + ROWS, B)), shape((ROWS, B))],
    )(core.reshape(1), own, got, mine, theirs)
    total = lax.all_to_all(total, "x", 0, 0)
    old_own = stats_old[0]
    old_low = old_own.astype(BF16)
    olds = [old_low] + shifted(old_low, "mp")
    keep, left_part, send = kernel_call(
        sum_kernel,
        "sum_x",
        [VMEM, VMEM],
        [shape((PART, B), F32), shape((PART, B)), shape((PART + ROWS, B))],
        awaited=2,
    )(total, right_rows, *olds[1:3])

    near_far = [
        [
            (z * CORE + c, ((z ^ 1) if c == step else ZH - 1 - z) * CORE + c)
            for z in range(ZH)
            for c in range(CORE)
        ]
        for step in range(2)
    ]
    got = lax.ppermute(send, ("zh", "core"), near_far[0])
    keep, send = kernel_call(
        middle_kernel,
        "middle",
        [VMEM] * 3,
        [shape((PART, B), F32), shape((PART + 2 * ROWS, B))],
    )(keep, right_rows, got)
    got = lax.ppermute(send, ("zh", "core"), near_far[1])
    grad, pieces, right_part = kernel_call(
        functools.partial(pack_kernel, tokens ** -0.5),
        "pack",
        [SMEM] + [VMEM] * 3,
        [shape((PART, B)), shape((n_mp, n_root, CORE, half, lanes)), shape((PART, B))],
    )(info, keep, send, got)

    pieces = pieces.reshape((n_mp * n_root,) + pieces.shape[2:])
    blocks = lax.all_to_all(pieces, ("mp", "root"), 0, 0)

    (total,) = kernel_call(
        update_kernel,
        "update",
        [VMEM] * 3,
        [shape((PART, B), F32)],
        work=cost(2 * PART * B * (PART + B), 6 * PART * B),
    )(left_part, grad, right_part)

    (chosen,) = kernel_call(
        choose_kernel,
        "choose",
        [SMEM, SMEM, VMEM, VMEM],
        [shape((X * CORE, 1 + B // lanes, half, lanes))],
        awaited=1,
    )(info, listed, blocks, total, olds[3])
    parts = lax.all_to_all(chosen, ("x", "core"), 0, 0)
    (mine,) = kernel_call(
        spread_kernel, "spread", [SMEM, SMEM, VMEM], [shape((n_mp * n_root, X, half, lanes))]
    )(info, listed, parts)
    mine = lax.all_to_all(mine, ("mp", "root"), 0, 0)
    theirs = lax.ppermute(mine, "core", swap)
    gathered = [value.reshape((n_mp, n_root) + value.shape[1:]) for value in (mine, theirs)]
    (update,) = kernel_call(finish_kernel, "finish", [VMEM], [shape((half, 2 * B))])(parts)

    new_stats, new_roots = kernel_call(
        refresh_kernel,
        "refresh",
        [SMEM, SMEM] + [VMEM] * 7,
        [shape((quarter, B), F32)] * 2,
        [pltpu.VMEM((B, B), BF16), pltpu.VMEM((B, B), F32), pltpu.VMEM((B, B), BF16)],
        cost(2 * B ** 3 + 10 * quarter * B * B, 2 * B * B * 2),
    )(info, owner, *gathered, old_own, *olds)
    return update[None], new_stats[None, None], new_roots[None, None]


def solution(mesh):
    n_dp, n_mp, n_root = mesh.devices.shape
    fine = Mesh(
        mesh.devices.reshape(X, ZH, CORE, n_mp, n_root), ("x", "zh", "core", "mp", "root")
    )
    dp = ("x", "zh", "core")
    in_specs = (
        P(dp, "mp"),
        P(dp, "root"),
        P("mp", "root", dp, None),
        P("mp", "root", dp, None),
        P(dp, "mp", None),
        P(),
        P(),
    )
    out_specs = (P("mp", dp, "root"), P("root", dp, "mp", None), P("root", dp, "mp", None))
    return jax.shard_map(local, mesh=fine, in_specs=in_specs, out_specs=out_specs, check_vma=False)
```

```python
import functools

import jax
import jax.numpy as jnp
from jax import lax
from jax.experimental import pallas as pl
from jax.experimental.pallas import tpu as pltpu
from jax.sharding import Mesh, PartitionSpec as P

B = 512
DECAY = 0.6
KAPPA = 1.25 ** 4
X, ZH, CORE = 4, 4, 2
CHIPS = X * ZH
PART = B // X
ROWS = B // CHIPS
F32, BF16 = jnp.float32, jnp.bfloat16
VMEM = pl.BlockSpec(memory_space=pltpu.VMEM)
SMEM = pl.BlockSpec(memory_space=pltpu.SMEM)


def dot(left, right, left_dim=1, right_dim=0):
    dims = (((left_dim,), (right_dim,)), ((), ()))
    return lax.dot_general(left, right, dims, preferred_element_type=F32)


def params():
    return pltpu.CompilerParams(vmem_limit_bytes=32 * 1024 * 1024)


def cost(flops, nbytes):
    return pl.CostEstimate(flops=flops, bytes_accessed=nbytes, transcendentals=0)


def shape(dims, dtype=BF16):
    return jax.ShapeDtypeStruct(dims, dtype)


def other_kernel(index_ref, acts_ref, grads_ref, turned_ref, out_ref, own_ref, acts_buf, grads_buf, total, sems):
    other = index_ref[0]
    steps, piece = acts_buf.shape[:2]

    def half(which):
        return pl.ds(pl.multiple_of(which * B, B), B)

    copies = []
    for k in range(steps):
        rows = pl.ds(k * piece, piece)
        copies.append(
            (
                pltpu.make_async_copy(acts_ref.at[rows, :], acts_buf.at[k], sems.at[0, k]),
                pltpu.make_async_copy(
                    grads_ref.at[rows, half(other)], grads_buf.at[k], sems.at[1, k]
                ),
            )
        )
        for copy in copies[-1]:
            copy.start()
    last = pltpu.make_async_copy(grads_ref.at[:, half(1 - other)], own_ref, sems.at[2, 0])
    last.start()
    for k, (acts_copy, grads_copy) in enumerate(copies):
        acts_copy.wait()
        turned = acts_buf[k].T
        turned_ref[:, k * piece : (k + 1) * piece] = turned
        grads_copy.wait()
        part = dot(turned, grads_buf[k])
        if k == 0:
            total[...] = part
        elif k < steps - 1:
            total[...] += part
        else:
            out_ref[...] = (total[...] + part).astype(BF16)
    last.wait()


def other_half(acts, grads, index):
    tokens, steps = acts.shape[0], 2
    anywhere = pl.BlockSpec(memory_space=pl.ANY)
    buffer = pltpu.VMEM((steps, tokens // steps, B), BF16)
    return pl.pallas_call(
        other_kernel,
        in_specs=[SMEM, anywhere, anywhere],
        out_specs=[VMEM] * 3,
        out_shape=[shape((B, tokens)), shape((B, B)), shape((tokens, B))],
        scratch_shapes=[
            buffer,
            buffer,
            pltpu.VMEM((B, B), F32),
            pltpu.SemaphoreType.DMA((3, steps)),
        ],
        compiler_params=pltpu.CompilerParams(vmem_limit_bytes=51 * 1024 * 1024),
        cost_estimate=cost(2 * tokens * B * B, 6 * tokens * B),
        name="other_half",
    )(index.reshape(1), acts, grads)


def own_kernel(turned_ref, grads_ref, out_ref):
    out_ref[...] = dot(turned_ref[...], grads_ref[...])


def join_kernel(own_ref, got_ref, prec_ref, out_ref):
    total = (own_ref[...] + got_ref[...].astype(F32)).astype(BF16).T
    rows = prec_ref.shape[2]
    for w in range(X):
        out_ref[w, :PART] = total[w * PART : (w + 1) * PART]
        for c in range(CORE):
            out_ref[w, PART + c * rows : PART + (c + 1) * rows] = prec_ref[0, c]


def shift(value, axis, step):
    size = lax.axis_size(axis)
    return lax.ppermute(value, axis, [(at, (at + step) % size) for at in range(size)])


def shifted(value, axis):
    return [shift(value, axis, step) for step in range(1, lax.axis_size(axis))]


def place(out_ref, parts, index):
    rows = parts[0].shape[0]
    for step, part in enumerate(parts):
        at = (index + len(parts) - step) % len(parts) * rows
        out_ref[pl.ds(pl.multiple_of(at, rows), rows), :] = part[...]


def sum_kernel(info_ref, parts_ref, mine_ref, theirs_ref, old_ref, *refs):
    keep_ref, right_ref, left_ref, left_send, old_low, send_ref = refs
    core = info_ref[0]
    rows = mine_ref.shape[0]
    right_ref[pl.ds(pl.multiple_of(core * rows, rows), rows), :] = mine_ref[...]
    right_ref[pl.ds(pl.multiple_of((1 - core) * rows, rows), rows), :] = theirs_ref[...]
    total = parts_ref[0, :PART].astype(F32)
    for w in range(X):
        for ref, c in ((left_ref, core), (left_send, 1 - core)):
            at = pl.multiple_of(PART + c * rows, rows)
            ref[w * rows : (w + 1) * rows] = parts_ref[w, pl.ds(at, rows), :]
        if w:
            total = total + parts_ref[w, :PART].astype(F32)
    keep_ref[...] = total
    send_ref[:PART] = total.astype(BF16)
    send_ref[PART:] = right_ref[...]
    old_low[...] = old_ref[...].astype(BF16)


def middle_kernel(keep_ref, right_ref, got_ref, old_ref, *refs):
    out_ref, send_ref, old_low = refs[-3:]
    total = keep_ref[...] + got_ref[:PART].astype(F32)
    out_ref[...] = total
    send_ref[:PART] = total.astype(BF16)
    send_ref[PART : PART + ROWS] = right_ref[...]
    send_ref[PART + ROWS :] = got_ref[PART:]
    old_low[...] = old_ref[...].astype(BF16)


def pack_kernel(scale, info_ref, keep_ref, sent_ref, got_ref, *refs):
    grad_ref, pieces_ref, right_ref = refs[-3:]
    core, zh = info_ref[0], info_ref[2]
    grad = ((keep_ref[...] + got_ref[:PART].astype(F32)) * scale).astype(BF16)
    grad_ref[...] = grad
    near = zh + 1 - 2 * (zh % 2)
    far = ZH - 1 - zh
    across = far + 1 - 2 * (far % 2)
    first = jnp.where(core == 0, near, far)
    second = jnp.where(core == 0, far, near)
    for place_at, mate in enumerate((zh, first, second, across)):
        source = (sent_ref, got_ref)[place_at // 2]
        start = PART + place_at % 2 * ROWS
        to = pl.multiple_of(mate * ROWS, ROWS)
        right_ref[pl.ds(to, ROWS), :] = source[start : start + ROWS]
    n_mp, n_root, cores, rows, lanes = pieces_ref.shape
    for c in range(cores):
        for r in range(n_root):
            at = (c * n_root + r) * rows
            for m in range(n_mp):
                pieces_ref[m, r, c] = grad[at : at + rows, m * lanes : (m + 1) * lanes]


def choose_kernel(info_ref, listed_ref, blocks_ref, total_ref, *refs):
    out_ref = refs[-1]
    rows, lanes = out_ref.shape[2:]
    for w in range(X):
        pair = listed_ref[w * ZH + info_ref[2]] // 2
        for c in range(CORE):
            out_ref[w * CORE + c, 0] = blocks_ref[pair, c]
            at = w * ROWS + c * rows
            for lane in range(B // lanes):
                part = total_ref[at : at + rows, lane * lanes : (lane + 1) * lanes]
                out_ref[w * CORE + c, 1 + lane] = part.astype(BF16)


def spread_kernel(info_ref, listed_ref, parts_ref, out_ref):
    holder = listed_ref[info_ref[1] * ZH + info_ref[2]] % 2
    for w in range(X):
        tile = parts_ref[w * CORE + holder, 0]
        for peer in range(out_ref.shape[0]):
            out_ref[peer, w] = tile


def finish_kernel(parts_ref, out_ref):
    lanes = parts_ref.shape[3]
    for c in range(CORE):
        for lane in range(B // lanes):
            total = parts_ref[c, 1 + lane].astype(F32)
            for w in range(1, X):
                total = total + parts_ref[w * CORE + c, 1 + lane].astype(F32)
            at = c * B + lane * lanes
            out_ref[:, at : at + lanes] = total.astype(BF16)


def update_kernel(info_ref, mine_ref, theirs_ref, grad_ref, right_ref, out_ref, left):
    rows = ROWS // CORE
    for ref, c in ((mine_ref, info_ref[0]), (theirs_ref, 1 - info_ref[0])):
        for w in range(X):
            at = pl.multiple_of(w * ROWS + c * rows, rows)
            left[pl.ds(at, rows), :] = ref[w * rows : (w + 1) * rows]
    product = dot(left[...], grad_ref[...], 1, 1).astype(BF16)
    out_ref[...] = dot(product, right_ref[...])


def refresh_kernel(info_ref, owner_ref, mine_ref, theirs_ref, own_ref, low_ref, one, two, three, stats_ref, roots_ref, block, product, old):
    core, x, zh, mp, root = (info_ref[at] for at in range(5))
    n_mp, n_root, _, rows, lanes = mine_ref.shape
    quarter = own_ref.shape[0]
    for ref, side in ((mine_ref, core), (theirs_ref, 1 - core)):
        for r in range(n_root):
            for w in range(X):
                at = pl.ds(pl.multiple_of(w * PART + (side * n_root + r) * rows, rows), rows)
                for m in range(n_mp):
                    block[at, m * lanes : (m + 1) * lanes] = ref[m, r, w]
    place(old, (low_ref, one, two, three), mp)

    @pl.when(core == 0)
    def _():
        value = block[...]
        product[...] = dot(value, value, 0, 0) * ((1.0 - DECAY) / B)

    @pl.when(core != 0)
    def _():
        value = block[...]
        product[...] = dot(value, value, 1, 1) * ((1.0 - DECAY) / B)

    mine = pl.ds(pl.multiple_of(mp * quarter, quarter), quarter)
    stats_rows = DECAY * own_ref[...] + product[mine, :]
    full = DECAY * old[...].astype(F32) + product[...]
    square = jnp.sum(full * full, axis=0, keepdims=True)
    factor = 2.5 / jnp.sqrt(jnp.sum(square, axis=1, keepdims=True))
    block[...] = (full * (factor * 0.2)).astype(BF16)
    e_rows = stats_rows * (factor * 0.2)
    y = e_rows
    for _ in range(5):
        y = y - dot(y.astype(BF16), block[...])
    line = lax.broadcasted_iota(jnp.int32, (quarter, B), 0) + mp * quarter
    unit = jnp.where(line == lax.broadcasted_iota(jnp.int32, (quarter, B), 1), 1.0, 0.0)
    roots_rows = (jnp.sqrt(jnp.sqrt(factor)) * 1.5625) * (unit - e_rows - KAPPA * y)
    owned = owner_ref[x * ZH + zh] == root
    stats_ref[...] = jnp.where(owned, stats_rows, 0.0)
    roots_ref[...] = jnp.where(owned, roots_rows, 0.0)


def kernel_call(kernel, name, in_specs, out_shape, scratch=(), work=None, awaited=0):
    return pl.pallas_call(
        kernel,
        in_specs=in_specs + [pl.BlockSpec(memory_space=pl.ANY)] * awaited,
        out_specs=[VMEM] * len(out_shape),
        out_shape=out_shape,
        scratch_shapes=list(scratch),
        compiler_params=params(),
        cost_estimate=work,
        name=name,
    )


def local(acts, grads_out, prec_left, prec_right, stats_old, listed, owner):
    x, zh, core = (lax.axis_index(name) for name in ("x", "zh", "core"))
    mp, root = lax.axis_index("mp"), lax.axis_index("root")
    n_mp, n_root = lax.axis_size("mp"), lax.axis_size("root")
    quarter = B // n_mp
    lanes, half = B // n_mp, ROWS // CORE
    tokens = acts.shape[0] * CHIPS * CORE
    swap = ((0, 1), (1, 0))
    info = jnp.stack([core, x, zh, mp, root])

    turned, send, grads_own = other_half(acts, grads_out, 1 - core)
    got = lax.ppermute(send, "core", swap)
    (own,) = kernel_call(
        own_kernel,
        "own_half",
        [VMEM, VMEM],
        [shape((B, B), F32)],
        work=cost(2 * acts.shape[0] * B * B, 4 * acts.shape[0] * B),
    )(turned, grads_own)
    (total,) = kernel_call(
        join_kernel, "join", [VMEM] * 3, [shape((X, PART + ROWS, B))]
    )(own, got, prec_left)
    total = lax.all_to_all(total, "x", 0, 0)
    mine = lax.dynamic_index_in_dim(prec_right[0], core, 0, keepdims=False)
    theirs = lax.ppermute(
        lax.dynamic_index_in_dim(prec_right[0], 1 - core, 0, keepdims=False), "core", swap
    )
    old_own = stats_old[0]
    keep, right_rows, left_mine, left_send, old_low, send = kernel_call(
        sum_kernel,
        "sum_x",
        [SMEM] + [VMEM] * 4,
        [shape((PART, B), F32), shape((ROWS, B))]
        + [shape((PART // CORE, B))] * 2
        + [shape((quarter, B)), shape((PART + ROWS, B))],
    )(info, total, mine, theirs, old_own)

    near_far = [
        [
            (z * CORE + c, ((z ^ 1) if c == step else ZH - 1 - z) * CORE + c)
            for z in range(ZH)
            for c in range(CORE)
        ]
        for step in range(2)
    ]
    got = lax.ppermute(send, ("zh", "core"), near_far[0])
    left_theirs = lax.ppermute(left_send, "core", swap)
    olds = [old_low, shift(old_low, "mp", 1)]
    keep, send, old_later = kernel_call(
        middle_kernel,
        "middle",
        [VMEM] * 4,
        [shape((PART, B), F32), shape((PART + 2 * ROWS, B)), shape((quarter, B))],
        awaited=2,
    )(keep, right_rows, got, old_own, left_theirs, olds[1])
    got = lax.ppermute(send, ("zh", "core"), near_far[1])
    olds += [shift(old_later, "mp", step) for step in range(2, n_mp)]
    grad, pieces, right_part = kernel_call(
        functools.partial(pack_kernel, tokens ** -0.5),
        "pack",
        [SMEM] + [VMEM] * 3,
        [shape((PART, B)), shape((n_mp, n_root, CORE, half, lanes)), shape((PART, B))],
        awaited=2,
    )(info, keep, send, got, *olds[2:])

    pieces = pieces.reshape((n_mp * n_root,) + pieces.shape[2:])
    blocks = lax.all_to_all(pieces, ("mp", "root"), 0, 0)

    (total,) = kernel_call(
        update_kernel,
        "update",
        [SMEM] + [VMEM] * 4,
        [shape((PART, B), F32)],
        [pltpu.VMEM((PART, B), BF16)],
        cost(2 * PART * B * (PART + B), 6 * PART * B),
    )(info, left_mine, left_theirs, grad, right_part)

    (chosen,) = kernel_call(
        choose_kernel,
        "choose",
        [SMEM, SMEM, VMEM, VMEM],
        [shape((X * CORE, 1 + B // lanes, half, lanes))],
    )(info, listed, blocks, total)
    parts = lax.all_to_all(chosen, ("x", "core"), 0, 0)
    (mine,) = kernel_call(
        spread_kernel, "spread", [SMEM, SMEM, VMEM], [shape((n_mp * n_root, X, half, lanes))]
    )(info, listed, parts)
    mine = lax.all_to_all(mine, ("mp", "root"), 0, 0)
    theirs = lax.ppermute(mine, "core", swap)
    gathered = [value.reshape((n_mp, n_root) + value.shape[1:]) for value in (mine, theirs)]
    (update,) = kernel_call(finish_kernel, "finish", [VMEM], [shape((half, 2 * B))])(parts)

    new_stats, new_roots = kernel_call(
        refresh_kernel,
        "refresh",
        [SMEM, SMEM] + [VMEM] * 7,
        [shape((quarter, B), F32)] * 2,
        [pltpu.VMEM((B, B), BF16), pltpu.VMEM((B, B), F32), pltpu.VMEM((B, B), BF16)],
        cost(2 * B ** 3 + 10 * quarter * B * B, 2 * B * B * 2),
    )(info, owner, *gathered, old_own, *olds)
    return update[None], new_stats[None, None], new_roots[None, None]


def solution(mesh):
    n_dp, n_mp, n_root = mesh.devices.shape
    fine = Mesh(
        mesh.devices.reshape(X, ZH, CORE, n_mp, n_root), ("x", "zh", "core", "mp", "root")
    )
    dp = ("x", "zh", "core")
    in_specs = (
        P(dp, "mp"),
        P(dp, "root"),
        P("mp", "root", dp, None),
        P("mp", "root", dp, None),
        P(dp, "mp", None),
        P(),
        P(),
    )
    out_specs = (P("mp", dp, "root"), P("root", dp, "mp", None), P("root", dp, "mp", None))
    return jax.shard_map(local, mesh=fine, in_specs=in_specs, out_specs=out_specs, check_vma=False)
```

```python
import functools

import jax
import jax.numpy as jnp
from jax import lax
from jax.experimental import pallas as pl
from jax.experimental.pallas import tpu as pltpu
from jax.sharding import Mesh, PartitionSpec as P

B = 512
DECAY = 0.6
KAPPA = 1.25 ** 4
X, ZH, CORE = 4, 4, 2
CHIPS = X * ZH
PART = B // X
ROWS = B // CHIPS
F32, BF16 = jnp.float32, jnp.bfloat16
VMEM = pl.BlockSpec(memory_space=pltpu.VMEM)
SMEM = pl.BlockSpec(memory_space=pltpu.SMEM)


def dot(left, right, left_dim=1, right_dim=0):
    dims = (((left_dim,), (right_dim,)), ((), ()))
    return lax.dot_general(left, right, dims, preferred_element_type=F32)


def params():
    return pltpu.CompilerParams(vmem_limit_bytes=32 * 1024 * 1024)


def cost(flops, nbytes):
    return pl.CostEstimate(flops=flops, bytes_accessed=nbytes, transcendentals=0)


def shape(dims, dtype=BF16):
    return jax.ShapeDtypeStruct(dims, dtype)


def other_kernel(index_ref, acts_ref, grads_ref, turned_ref, out_ref, own_ref, acts_buf, grads_buf, total, sems):
    other = index_ref[0]
    steps, piece = acts_buf.shape[:2]

    def half(which):
        return pl.ds(pl.multiple_of(which * B, B), B)

    copies = []
    for k in range(steps):
        rows = pl.ds(k * piece, piece)
        copies.append(
            (
                pltpu.make_async_copy(acts_ref.at[rows, :], acts_buf.at[k], sems.at[0, k]),
                pltpu.make_async_copy(
                    grads_ref.at[rows, half(other)], grads_buf.at[k], sems.at[1, k]
                ),
            )
        )
        for copy in copies[-1]:
            copy.start()
    last = pltpu.make_async_copy(grads_ref.at[:, half(1 - other)], own_ref, sems.at[2, 0])
    last.start()
    for k, (acts_copy, grads_copy) in enumerate(copies):
        acts_copy.wait()
        turned = acts_buf[k].T
        turned_ref[:, k * piece : (k + 1) * piece] = turned
        grads_copy.wait()
        part = dot(turned, grads_buf[k])
        if k == 0:
            total[...] = part
        elif k < steps - 1:
            total[...] += part
        else:
            out_ref[...] = (total[...] + part).astype(BF16)
    last.wait()


def other_half(acts, grads, index):
    tokens, steps = acts.shape[0], 2
    anywhere = pl.BlockSpec(memory_space=pl.ANY)
    buffer = pltpu.VMEM((steps, tokens // steps, B), BF16)
    return pl.pallas_call(
        other_kernel,
        in_specs=[SMEM, anywhere, anywhere],
        out_specs=[VMEM] * 3,
        out_shape=[shape((B, tokens)), shape((B, B)), shape((tokens, B))],
        scratch_shapes=[
            buffer,
            buffer,
            pltpu.VMEM((B, B), F32),
            pltpu.SemaphoreType.DMA((3, steps)),
        ],
        compiler_params=pltpu.CompilerParams(vmem_limit_bytes=51 * 1024 * 1024),
        cost_estimate=cost(2 * tokens * B * B, 6 * tokens * B),
        name="other_half",
    )(index.reshape(1), acts, grads)


def own_kernel(turned_ref, grads_ref, out_ref):
    out_ref[...] = dot(turned_ref[...], grads_ref[...])


def join_kernel(own_ref, got_ref, prec_ref, right_ref, out_ref, right_out):
    total = (own_ref[...] + got_ref[...].astype(F32)).astype(BF16).T
    rows = prec_ref.shape[2]
    for w in range(X):
        out_ref[w, :PART] = total[w * PART : (w + 1) * PART]
        for c in range(CORE):
            out_ref[w, PART + c * rows : PART + (c + 1) * rows] = prec_ref[0, c]
    right_out[...] = right_ref[0]


def shift(value, axis, step):
    size = lax.axis_size(axis)
    return lax.ppermute(value, axis, [(at, (at + step) % size) for at in range(size)])


def shifted(value, axis):
    return [shift(value, axis, step) for step in range(1, lax.axis_size(axis))]


def place(out_ref, parts, index):
    rows = parts[0].shape[0]
    for step, part in enumerate(parts):
        at = (index + len(parts) - step) % len(parts) * rows
        out_ref[pl.ds(pl.multiple_of(at, rows), rows), :] = part[...]


def sum_kernel(info_ref, parts_ref, old_ref, *refs):
    keep_ref, left_ref, left_send, old_low, send_ref = refs[-5:]
    core = info_ref[0]
    rows = left_ref.shape[0] // X
    total = parts_ref[0, :PART].astype(F32)
    for w in range(X):
        for ref, c in ((left_ref, core), (left_send, 1 - core)):
            at = pl.multiple_of(PART + c * rows, rows)
            ref[w * rows : (w + 1) * rows] = parts_ref[w, pl.ds(at, rows), :]
        if w:
            total = total + parts_ref[w, :PART].astype(F32)
    keep_ref[...] = total
    send_ref[...] = total.astype(BF16)
    old_low[...] = old_ref[...].astype(BF16)


def halves_kernel(info_ref, own_ref, one, two, left_ref, keep_ref, send_ref):
    core, zh = info_ref[0], info_ref[2]
    rows = own_ref.shape[2]
    near = zh + 1 - 2 * (zh % 2)
    far = ZH - 1 - zh
    across = far + 1 - 2 * (far % 2)
    first = jnp.where(core == 0, near, far)
    second = jnp.where(core == 0, far, near)
    sources = (own_ref.at[0], one, two.at[0], two.at[1])
    send_ref[: ZH * rows] = left_ref[...]
    for mate, source in zip((zh, first, second, across), sources):
        keep_ref[pl.ds(pl.multiple_of(mate * rows, rows), rows), :] = source[core]
        at = pl.multiple_of((ZH + mate) * rows, rows)
        send_ref[pl.ds(at, rows), :] = source[1 - core]


def middle_kernel(keep_ref, got_ref, old_ref, *refs):
    out_ref, send_ref, old_low = refs[-3:]
    total = keep_ref[...] + got_ref[...].astype(F32)
    out_ref[...] = total
    send_ref[...] = total.astype(BF16)
    old_low[...] = old_ref[...].astype(BF16)


def pack_kernel(scale, keep_ref, got_ref, *refs):
    pieces_ref = refs[-1]
    grad = ((keep_ref[...] + got_ref[...].astype(F32)) * scale).astype(BF16)
    n_mp, n_root, cores, rows, lanes = pieces_ref.shape
    for c in range(cores):
        for r in range(n_root):
            at = (c * n_root + r) * rows
            for m in range(n_mp):
                pieces_ref[m, r, c] = grad[at : at + rows, m * lanes : (m + 1) * lanes]


def choose_kernel(info_ref, listed_ref, blocks_ref, total_ref, *refs):
    out_ref = refs[-1]
    rows, lanes = out_ref.shape[2:]
    for w in range(X):
        pair = listed_ref[w * ZH + info_ref[2]] // 2
        for c in range(CORE):
            out_ref[w * CORE + c, 0] = blocks_ref[pair, c]
            at = w * ROWS + c * rows
            for lane in range(B // lanes):
                part = total_ref[at : at + rows, lane * lanes : (lane + 1) * lanes]
                out_ref[w * CORE + c, 1 + lane] = part.astype(BF16)


def spread_kernel(info_ref, listed_ref, parts_ref, out_ref):
    holder = listed_ref[info_ref[1] * ZH + info_ref[2]] % 2
    for w in range(X):
        tile = parts_ref[w * CORE + holder, 0]
        for peer in range(out_ref.shape[0]):
            out_ref[peer, w] = tile


def finish_kernel(parts_ref, out_ref):
    lanes = parts_ref.shape[3]
    for c in range(CORE):
        for lane in range(B // lanes):
            total = parts_ref[c, 1 + lane].astype(F32)
            for w in range(1, X):
                total = total + parts_ref[w * CORE + c, 1 + lane].astype(F32)
            at = c * B + lane * lanes
            out_ref[:, at : at + lanes] = total.astype(BF16)


def update_kernel(scale, info_ref, keep_ref, got_ref, left_ref, right_ref, theirs_ref, out_ref, left, right):
    grad = ((keep_ref[...] + got_ref[...].astype(F32)) * scale).astype(BF16)
    core, rows, side = info_ref[0], ROWS // CORE, PART // CORE
    for ref, mine, start in ((left, left_ref, 0), (right, right_ref, side)):
        for w in range(PART // ROWS):
            at = pl.multiple_of(w * ROWS + core * rows, rows)
            ref[pl.ds(at, rows), :] = mine[w * rows : (w + 1) * rows]
            at = pl.multiple_of(w * ROWS + (1 - core) * rows, rows)
            ref[pl.ds(at, rows), :] = theirs_ref[start + w * rows : start + (w + 1) * rows]
    product = dot(left[...], grad, 1, 1).astype(BF16)
    out_ref[...] = dot(product, right[...])


def refresh_kernel(info_ref, owner_ref, mine_ref, theirs_ref, own_ref, low_ref, one, two, three, stats_ref, roots_ref, block, product, old):
    core, x, zh, mp, root = (info_ref[at] for at in range(5))
    n_mp, n_root, _, rows, lanes = mine_ref.shape
    quarter = own_ref.shape[0]
    for ref, side in ((mine_ref, core), (theirs_ref, 1 - core)):
        for r in range(n_root):
            for w in range(X):
                at = pl.ds(pl.multiple_of(w * PART + (side * n_root + r) * rows, rows), rows)
                for m in range(n_mp):
                    block[at, m * lanes : (m + 1) * lanes] = ref[m, r, w]
    place(old, (low_ref, one, two, three), mp)

    @pl.when(core == 0)
    def _():
        value = block[...]
        product[...] = dot(value, value, 0, 0) * ((1.0 - DECAY) / B)

    @pl.when(core != 0)
    def _():
        value = block[...]
        product[...] = dot(value, value, 1, 1) * ((1.0 - DECAY) / B)

    mine = pl.ds(pl.multiple_of(mp * quarter, quarter), quarter)
    stats_rows = DECAY * own_ref[...] + product[mine, :]
    full = DECAY * old[...].astype(F32) + product[...]
    square = jnp.sum(full * full, axis=0, keepdims=True)
    factor = 2.5 / jnp.sqrt(jnp.sum(square, axis=1, keepdims=True))
    block[...] = (full * (factor * 0.2)).astype(BF16)
    e_rows = stats_rows * (factor * 0.2)
    y = e_rows
    for _ in range(5):
        y = y - dot(y.astype(BF16), block[...])
    line = lax.broadcasted_iota(jnp.int32, (quarter, B), 0) + mp * quarter
    unit = jnp.where(line == lax.broadcasted_iota(jnp.int32, (quarter, B), 1), 1.0, 0.0)
    roots_rows = (jnp.sqrt(jnp.sqrt(factor)) * 1.5625) * (unit - e_rows - KAPPA * y)
    owned = owner_ref[x * ZH + zh] == root
    stats_ref[...] = jnp.where(owned, stats_rows, 0.0)
    roots_ref[...] = jnp.where(owned, roots_rows, 0.0)


def kernel_call(kernel, name, in_specs, out_shape, scratch=(), work=None, awaited=0):
    return pl.pallas_call(
        kernel,
        in_specs=in_specs + [pl.BlockSpec(memory_space=pl.ANY)] * awaited,
        out_specs=[VMEM] * len(out_shape),
        out_shape=out_shape,
        scratch_shapes=list(scratch),
        compiler_params=params(),
        cost_estimate=work,
        name=name,
    )


def local(acts, grads_out, prec_left, prec_right, stats_old, listed, owner):
    x, zh, core = (lax.axis_index(name) for name in ("x", "zh", "core"))
    mp, root = lax.axis_index("mp"), lax.axis_index("root")
    n_mp, n_root = lax.axis_size("mp"), lax.axis_size("root")
    quarter = B // n_mp
    lanes, half = B // n_mp, ROWS // CORE
    tokens = acts.shape[0] * CHIPS * CORE
    swap = ((0, 1), (1, 0))
    info = jnp.stack([core, x, zh, mp, root])

    turned, send, grads_own = other_half(acts, grads_out, 1 - core)
    got = lax.ppermute(send, "core", swap)
    (own,) = kernel_call(
        own_kernel,
        "own_half",
        [VMEM, VMEM],
        [shape((B, B), F32)],
        work=cost(2 * acts.shape[0] * B * B, 4 * acts.shape[0] * B),
    )(turned, grads_own)
    total, right_own = kernel_call(
        join_kernel,
        "join",
        [VMEM] * 4,
        [shape((X, PART + ROWS, B)), shape((CORE, half, B))],
    )(own, got, prec_left, prec_right)
    total = lax.all_to_all(total, "x", 0, 0)
    near_far = [
        [
            (z * CORE + c, ((z ^ 1) if c == step else ZH - 1 - z) * CORE + c)
            for z in range(ZH)
            for c in range(CORE)
        ]
        for step in range(2)
    ]
    right_one = lax.ppermute(right_own, ("zh", "core"), near_far[0])
    right_two = lax.ppermute(jnp.stack([right_own, right_one]), ("zh", "core"), near_far[1])
    old_own = stats_old[0]
    keep, left_mine, left_send, old_low, send = kernel_call(
        sum_kernel,
        "sum_x",
        [SMEM] + [VMEM] * 2,
        [shape((PART, B), F32)]
        + [shape((PART // CORE, B))] * 2
        + [shape((quarter, B)), shape((PART, B))],
        awaited=1,
    )(info, total, old_own, right_one)
    got = lax.ppermute(send, ("zh", "core"), near_far[0])
    right_mine, prec_send = kernel_call(
        halves_kernel,
        "halves",
        [SMEM] + [VMEM] * 4,
        [shape((PART // CORE, B)), shape((PART, B))],
    )(info, prec_right, right_one, right_two, left_send)
    theirs = lax.ppermute(prec_send, "core", swap)
    olds = [old_low, shift(old_low, "mp", 1)]
    keep, send, old_later = kernel_call(
        middle_kernel,
        "middle",
        [VMEM] * 3,
        [shape((PART, B), F32), shape((PART, B)), shape((quarter, B))],
        awaited=2,
    )(keep, got, old_own, theirs, olds[1])
    got = lax.ppermute(send, ("zh", "core"), near_far[1])
    olds += [shift(old_later, "mp", step) for step in range(2, n_mp)]
    (pieces,) = kernel_call(
        functools.partial(pack_kernel, tokens ** -0.5),
        "pack",
        [VMEM] * 2,
        [shape((n_mp, n_root, CORE, half, lanes))],
        awaited=1,
    )(keep, got, olds[2])

    pieces = pieces.reshape((n_mp * n_root,) + pieces.shape[2:])
    blocks = lax.all_to_all(pieces, ("mp", "root"), 0, 0)

    (total,) = kernel_call(
        functools.partial(update_kernel, tokens ** -0.5),
        "update",
        [SMEM] + [VMEM] * 5,
        [shape((PART, B), F32)],
        [pltpu.VMEM((PART, B), BF16)] * 2,
        cost(2 * PART * B * (PART + B), 6 * PART * B),
    )(info, keep, got, left_mine, right_mine, theirs)

    (chosen,) = kernel_call(
        choose_kernel,
        "choose",
        [SMEM, SMEM, VMEM, VMEM],
        [shape((X * CORE, 1 + B // lanes, half, lanes))],
        awaited=1,
    )(info, listed, blocks, total, olds[3])
    parts = lax.all_to_all(chosen, ("x", "core"), 0, 0)
    (mine,) = kernel_call(
        spread_kernel, "spread", [SMEM, SMEM, VMEM], [shape((n_mp * n_root, X, half, lanes))]
    )(info, listed, parts)
    mine = lax.all_to_all(mine, ("mp", "root"), 0, 0)
    theirs = lax.ppermute(mine, "core", swap)
    gathered = [value.reshape((n_mp, n_root) + value.shape[1:]) for value in (mine, theirs)]
    (update,) = kernel_call(finish_kernel, "finish", [VMEM], [shape((half, 2 * B))])(parts)

    new_stats, new_roots = kernel_call(
        refresh_kernel,
        "refresh",
        [SMEM, SMEM] + [VMEM] * 7,
        [shape((quarter, B), F32)] * 2,
        [pltpu.VMEM((B, B), BF16), pltpu.VMEM((B, B), F32), pltpu.VMEM((B, B), BF16)],
        cost(2 * B ** 3 + 10 * quarter * B * B, 2 * B * B * 2),
    )(info, owner, *gathered, old_own, *olds)
    return update[None], new_stats[None, None], new_roots[None, None]


def solution(mesh):
    n_dp, n_mp, n_root = mesh.devices.shape
    fine = Mesh(
        mesh.devices.reshape(X, ZH, CORE, n_mp, n_root), ("x", "zh", "core", "mp", "root")
    )
    dp = ("x", "zh", "core")
    in_specs = (
        P(dp, "mp"),
        P(dp, "root"),
        P("mp", "root", dp, None),
        P("mp", "root", dp, None),
        P(dp, "mp", None),
        P(),
        P(),
    )
    out_specs = (P("mp", dp, "root"), P("root", dp, "mp", None), P("root", dp, "mp", None))
    return jax.shard_map(local, mesh=fine, in_specs=in_specs, out_specs=out_specs, check_vma=False)
```

```python
import functools

import jax
import jax.numpy as jnp
from jax import lax
from jax.experimental import pallas as pl
from jax.experimental.pallas import tpu as pltpu
from jax.sharding import Mesh, PartitionSpec as P

B = 512
DECAY = 0.6
KAPPA = 1.25 ** 4
X, ZH, CORE = 4, 4, 2
CHIPS = X * ZH
PART = B // X
ROWS = B // CHIPS
F32, BF16 = jnp.float32, jnp.bfloat16
VMEM = pl.BlockSpec(memory_space=pltpu.VMEM)
SMEM = pl.BlockSpec(memory_space=pltpu.SMEM)


def dot(left, right, left_dim=1, right_dim=0):
    dims = (((left_dim,), (right_dim,)), ((), ()))
    return lax.dot_general(left, right, dims, preferred_element_type=F32)


def params():
    return pltpu.CompilerParams(vmem_limit_bytes=32 * 1024 * 1024)


def cost(flops, nbytes):
    return pl.CostEstimate(flops=flops, bytes_accessed=nbytes, transcendentals=0)


def shape(dims, dtype=BF16):
    return jax.ShapeDtypeStruct(dims, dtype)


def other_kernel(index_ref, acts_ref, grads_ref, turned_ref, out_ref, own_ref, acts_buf, grads_buf, total, sems):
    other = index_ref[0]
    steps, piece = acts_buf.shape[:2]

    def half(which):
        return pl.ds(pl.multiple_of(which * B, B), B)

    copies = []
    for k in range(steps):
        rows = pl.ds(k * piece, piece)
        copies.append(
            (
                pltpu.make_async_copy(acts_ref.at[rows, :], acts_buf.at[k], sems.at[0, k]),
                pltpu.make_async_copy(
                    grads_ref.at[rows, half(other)], grads_buf.at[k], sems.at[1, k]
                ),
            )
        )
        for copy in copies[-1]:
            copy.start()
    last = pltpu.make_async_copy(grads_ref.at[:, half(1 - other)], own_ref, sems.at[2, 0])
    last.start()
    for k, (acts_copy, grads_copy) in enumerate(copies):
        acts_copy.wait()
        turned = acts_buf[k].T
        turned_ref[:, k * piece : (k + 1) * piece] = turned
        grads_copy.wait()
        part = dot(turned, grads_buf[k])
        if k == 0:
            total[...] = part
        elif k < steps - 1:
            total[...] += part
        else:
            out_ref[...] = (total[...] + part).astype(BF16)
    last.wait()


def other_half(acts, grads, index):
    tokens, steps = acts.shape[0], 2
    anywhere = pl.BlockSpec(memory_space=pl.ANY)
    buffer = pltpu.VMEM((steps, tokens // steps, B), BF16)
    return pl.pallas_call(
        other_kernel,
        in_specs=[SMEM, anywhere, anywhere],
        out_specs=[VMEM] * 3,
        out_shape=[shape((B, tokens)), shape((B, B)), shape((tokens, B))],
        scratch_shapes=[
            buffer,
            buffer,
            pltpu.VMEM((B, B), F32),
            pltpu.SemaphoreType.DMA((3, steps)),
        ],
        compiler_params=pltpu.CompilerParams(vmem_limit_bytes=51 * 1024 * 1024),
        cost_estimate=cost(2 * tokens * B * B, 6 * tokens * B),
        name="other_half",
    )(index.reshape(1), acts, grads)


def own_kernel(turned_ref, grads_ref, out_ref):
    out_ref[...] = dot(turned_ref[...], grads_ref[...])


def join_kernel(own_ref, got_ref, prec_ref, out_ref):
    total = (own_ref[...] + got_ref[...].astype(F32)).astype(BF16).T
    rows = prec_ref.shape[2]
    for w in range(X):
        out_ref[w, :PART] = total[w * PART : (w + 1) * PART]
        for c in range(CORE):
            out_ref[w, PART + c * rows : PART + (c + 1) * rows] = prec_ref[0, c]


def shift(value, axis, step):
    size = lax.axis_size(axis)
    return lax.ppermute(value, axis, [(at, (at + step) % size) for at in range(size)])


def shifted(value, axis):
    return [shift(value, axis, step) for step in range(1, lax.axis_size(axis))]


def place(out_ref, parts, index):
    rows = parts[0].shape[0]
    for step, part in enumerate(parts):
        at = (index + len(parts) - step) % len(parts) * rows
        out_ref[pl.ds(pl.multiple_of(at, rows), rows), :] = part[...]


def sum_kernel(info_ref, parts_ref, mine_ref, theirs_ref, old_ref, *refs):
    keep_ref, right_ref, left_ref, left_send, old_low, send_ref = refs
    core = info_ref[0]
    rows = mine_ref.shape[0]
    right_ref[pl.ds(pl.multiple_of(core * rows, rows), rows), :] = mine_ref[...]
    right_ref[pl.ds(pl.multiple_of((1 - core) * rows, rows), rows), :] = theirs_ref[...]
    total = parts_ref[0, :PART].astype(F32)
    for w in range(X):
        for ref, c in ((left_ref, core), (left_send, 1 - core)):
            at = pl.multiple_of(PART + c * rows, rows)
            ref[w * rows : (w + 1) * rows] = parts_ref[w, pl.ds(at, rows), :]
        if w:
            total = total + parts_ref[w, :PART].astype(F32)
    keep_ref[...] = total
    send_ref[:PART] = total.astype(BF16)
    send_ref[PART:] = right_ref[...]
    old_low[...] = old_ref[...].astype(BF16)


def middle_kernel(keep_ref, right_ref, got_ref, old_ref, *refs):
    out_ref, send_ref, old_low = refs[-3:]
    total = keep_ref[...] + got_ref[:PART].astype(F32)
    out_ref[...] = total
    send_ref[:PART] = total.astype(BF16)
    send_ref[PART : PART + ROWS] = right_ref[...]
    send_ref[PART + ROWS :] = got_ref[PART:]
    old_low[...] = old_ref[...].astype(BF16)


def pack_kernel(scale, keep_ref, got_ref, pieces_ref):
    grad = ((keep_ref[...] + got_ref[:PART].astype(F32)) * scale).astype(BF16)
    n_mp, n_root, cores, rows, lanes = pieces_ref.shape
    for c in range(cores):
        for r in range(n_root):
            at = (c * n_root + r) * rows
            for m in range(n_mp):
                pieces_ref[m, r, c] = grad[at : at + rows, m * lanes : (m + 1) * lanes]


def choose_kernel(info_ref, listed_ref, blocks_ref, total_ref, *refs):
    out_ref = refs[-1]
    rows, lanes = out_ref.shape[2:]
    for w in range(X):
        pair = listed_ref[w * ZH + info_ref[2]] // 2
        for c in range(CORE):
            out_ref[w * CORE + c, 0] = blocks_ref[pair, c]
            at = w * ROWS + c * rows
            for lane in range(B // lanes):
                part = total_ref[at : at + rows, lane * lanes : (lane + 1) * lanes]
                out_ref[w * CORE + c, 1 + lane] = part.astype(BF16)


def spread_kernel(info_ref, listed_ref, parts_ref, *refs):
    out_ref = refs[-1]
    holder = listed_ref[info_ref[1] * ZH + info_ref[2]] % 2
    for w in range(X):
        tile = parts_ref[w * CORE + holder, 0]
        for peer in range(out_ref.shape[0]):
            out_ref[peer, w] = tile


def finish_kernel(parts_ref, out_ref):
    lanes = parts_ref.shape[3]
    for c in range(CORE):
        for lane in range(B // lanes):
            total = parts_ref[c, 1 + lane].astype(F32)
            for w in range(1, X):
                total = total + parts_ref[w * CORE + c, 1 + lane].astype(F32)
            at = c * B + lane * lanes
            out_ref[:, at : at + lanes] = total.astype(BF16)


def update_kernel(scale, info_ref, keep_ref, sent_ref, got_ref, mine_ref, theirs_ref, out_ref, left, right):
    core, zh = info_ref[0], info_ref[2]
    rows = ROWS // CORE
    for ref, c in ((mine_ref, core), (theirs_ref, 1 - core)):
        for w in range(X):
            at = pl.multiple_of(w * ROWS + c * rows, rows)
            left[pl.ds(at, rows), :] = ref[w * rows : (w + 1) * rows]
    near = zh + 1 - 2 * (zh % 2)
    far = ZH - 1 - zh
    across = far + 1 - 2 * (far % 2)
    first = jnp.where(core == 0, near, far)
    second = jnp.where(core == 0, far, near)
    for place_at, mate in enumerate((zh, first, second, across)):
        source = (sent_ref, got_ref)[place_at // 2]
        start = PART + place_at % 2 * ROWS
        to = pl.multiple_of(mate * ROWS, ROWS)
        right[pl.ds(to, ROWS), :] = source[start : start + ROWS]
    grad = ((keep_ref[...] + got_ref[:PART].astype(F32)) * scale).astype(BF16)
    product = dot(left[...], grad, 1, 1).astype(BF16)
    out_ref[...] = dot(product, right[...])


def refresh_kernel(info_ref, owner_ref, mine_ref, theirs_ref, own_ref, low_ref, one, two, three, stats_ref, roots_ref, block, product, old):
    core, x, zh, mp, root = (info_ref[at] for at in range(5))
    n_mp, n_root, _, rows, lanes = mine_ref.shape
    quarter = own_ref.shape[0]
    for ref, side in ((mine_ref, core), (theirs_ref, 1 - core)):
        for r in range(n_root):
            for w in range(X):
                at = pl.ds(pl.multiple_of(w * PART + (side * n_root + r) * rows, rows), rows)
                for m in range(n_mp):
                    block[at, m * lanes : (m + 1) * lanes] = ref[m, r, w]
    place(old, (low_ref, one, two, three), mp)

    @pl.when(core == 0)
    def _():
        value = block[...]
        product[...] = dot(value, value, 0, 0) * ((1.0 - DECAY) / B)

    @pl.when(core != 0)
    def _():
        value = block[...]
        product[...] = dot(value, value, 1, 1) * ((1.0 - DECAY) / B)

    mine = pl.ds(pl.multiple_of(mp * quarter, quarter), quarter)
    stats_rows = DECAY * own_ref[...] + product[mine, :]
    full = DECAY * old[...].astype(F32) + product[...]
    square = jnp.sum(full * full, axis=0, keepdims=True)
    factor = 2.5 / jnp.sqrt(jnp.sum(square, axis=1, keepdims=True))
    block[...] = (full * (factor * 0.2)).astype(BF16)
    e_rows = stats_rows * (factor * 0.2)
    y = e_rows
    for _ in range(5):
        y = y - dot(y.astype(BF16), block[...])
    line = lax.broadcasted_iota(jnp.int32, (quarter, B), 0) + mp * quarter
    unit = jnp.where(line == lax.broadcasted_iota(jnp.int32, (quarter, B), 1), 1.0, 0.0)
    roots_rows = (jnp.sqrt(jnp.sqrt(factor)) * 1.5625) * (unit - e_rows - KAPPA * y)
    owned = owner_ref[x * ZH + zh] == root
    stats_ref[...] = jnp.where(owned, stats_rows, 0.0)
    roots_ref[...] = jnp.where(owned, roots_rows, 0.0)


def kernel_call(kernel, name, in_specs, out_shape, scratch=(), work=None, awaited=0):
    return pl.pallas_call(
        kernel,
        in_specs=in_specs + [pl.BlockSpec(memory_space=pl.ANY)] * awaited,
        out_specs=[VMEM] * len(out_shape),
        out_shape=out_shape,
        scratch_shapes=list(scratch),
        compiler_params=params(),
        cost_estimate=work,
        name=name,
    )


def local(acts, grads_out, prec_left, prec_right, stats_old, listed, owner):
    x, zh, core = (lax.axis_index(name) for name in ("x", "zh", "core"))
    mp, root = lax.axis_index("mp"), lax.axis_index("root")
    n_mp, n_root = lax.axis_size("mp"), lax.axis_size("root")
    quarter = B // n_mp
    lanes, half = B // n_mp, ROWS // CORE
    tokens = acts.shape[0] * CHIPS * CORE
    swap = ((0, 1), (1, 0))
    info = jnp.stack([core, x, zh, mp, root])

    turned, send, grads_own = other_half(acts, grads_out, 1 - core)
    got = lax.ppermute(send, "core", swap)
    (own,) = kernel_call(
        own_kernel,
        "own_half",
        [VMEM, VMEM],
        [shape((B, B), F32)],
        work=cost(2 * acts.shape[0] * B * B, 4 * acts.shape[0] * B),
    )(turned, grads_own)
    (total,) = kernel_call(
        join_kernel, "join", [VMEM] * 3, [shape((X, PART + ROWS, B))]
    )(own, got, prec_left)
    total = lax.all_to_all(total, "x", 0, 0)
    mine = lax.dynamic_index_in_dim(prec_right[0], core, 0, keepdims=False)
    theirs = lax.ppermute(
        lax.dynamic_index_in_dim(prec_right[0], 1 - core, 0, keepdims=False), "core", swap
    )
    old_own = stats_old[0]
    keep, right_rows, left_mine, left_send, old_low, send = kernel_call(
        sum_kernel,
        "sum_x",
        [SMEM] + [VMEM] * 4,
        [shape((PART, B), F32), shape((ROWS, B))]
        + [shape((PART // CORE, B))] * 2
        + [shape((quarter, B)), shape((PART + ROWS, B))],
    )(info, total, mine, theirs, old_own)

    near_far = [
        [
            (z * CORE + c, ((z ^ 1) if c == step else ZH - 1 - z) * CORE + c)
            for z in range(ZH)
            for c in range(CORE)
        ]
        for step in range(2)
    ]
    got = lax.ppermute(send, ("zh", "core"), near_far[0])
    left_theirs = lax.ppermute(left_send, "core", swap)
    olds = [old_low, shift(old_low, "mp", 1)]
    keep, send, old_later = kernel_call(
        middle_kernel,
        "middle",
        [VMEM] * 4,
        [shape((PART, B), F32), shape((PART + 2 * ROWS, B)), shape((quarter, B))],
        awaited=2,
    )(keep, right_rows, got, old_own, left_theirs, olds[1])
    got = lax.ppermute(send, ("zh", "core"), near_far[1])
    olds += [shift(old_later, "mp", step) for step in range(2, n_mp)]
    (pieces,) = kernel_call(
        functools.partial(pack_kernel, tokens ** -0.5),
        "pack",
        [VMEM] * 2,
        [shape((n_mp, n_root, CORE, half, lanes))],
    )(keep, got)

    pieces = pieces.reshape((n_mp * n_root,) + pieces.shape[2:])
    blocks = lax.all_to_all(pieces, ("mp", "root"), 0, 0)

    (total,) = kernel_call(
        functools.partial(update_kernel, tokens ** -0.5),
        "update",
        [SMEM] + [VMEM] * 5,
        [shape((PART, B), F32)],
        [pltpu.VMEM((PART, B), BF16)] * 2,
        cost(2 * PART * B * (PART + B), 6 * PART * B),
    )(info, keep, send, got, left_mine, left_theirs)

    (chosen,) = kernel_call(
        choose_kernel,
        "choose",
        [SMEM, SMEM, VMEM, VMEM],
        [shape((X * CORE, 1 + B // lanes, half, lanes))],
        awaited=1,
    )(info, listed, blocks, total, olds[2])
    parts = lax.all_to_all(chosen, ("x", "core"), 0, 0)
    (mine,) = kernel_call(
        spread_kernel,
        "spread",
        [SMEM, SMEM, VMEM],
        [shape((n_mp * n_root, X, half, lanes))],
        awaited=1,
    )(info, listed, parts, olds[3])
    mine = lax.all_to_all(mine, ("mp", "root"), 0, 0)
    theirs = lax.ppermute(mine, "core", swap)
    gathered = [value.reshape((n_mp, n_root) + value.shape[1:]) for value in (mine, theirs)]
    (update,) = kernel_call(finish_kernel, "finish", [VMEM], [shape((half, 2 * B))])(parts)

    new_stats, new_roots = kernel_call(
        refresh_kernel,
        "refresh",
        [SMEM, SMEM] + [VMEM] * 7,
        [shape((quarter, B), F32)] * 2,
        [pltpu.VMEM((B, B), BF16), pltpu.VMEM((B, B), F32), pltpu.VMEM((B, B), BF16)],
        cost(2 * B ** 3 + 10 * quarter * B * B, 2 * B * B * 2),
    )(info, owner, *gathered, old_own, *olds)
    return update[None], new_stats[None, None], new_roots[None, None]


def solution(mesh):
    n_dp, n_mp, n_root = mesh.devices.shape
    fine = Mesh(
        mesh.devices.reshape(X, ZH, CORE, n_mp, n_root), ("x", "zh", "core", "mp", "root")
    )
    dp = ("x", "zh", "core")
    in_specs = (
        P(dp, "mp"),
        P(dp, "root"),
        P("mp", "root", dp, None),
        P("mp", "root", dp, None),
        P(dp, "mp", None),
        P(),
        P(),
    )
    out_specs = (P("mp", dp, "root"), P("root", dp, "mp", None), P("root", dp, "mp", None))
    return jax.shard_map(local, mesh=fine, in_specs=in_specs, out_specs=out_specs, check_vma=False)
```

```python
import functools

import jax
import jax.numpy as jnp
from jax import lax
from jax.experimental import pallas as pl
from jax.experimental.pallas import tpu as pltpu
from jax.sharding import Mesh, PartitionSpec as P

B = 512
DECAY = 0.6
KAPPA = 1.25 ** 4
X, ZH, CORE = 4, 4, 2
CHIPS = X * ZH
PART = B // X
ROWS = B // CHIPS
F32, BF16 = jnp.float32, jnp.bfloat16
VMEM = pl.BlockSpec(memory_space=pltpu.VMEM)
SMEM = pl.BlockSpec(memory_space=pltpu.SMEM)


def dot(left, right, left_dim=1, right_dim=0):
    dims = (((left_dim,), (right_dim,)), ((), ()))
    return lax.dot_general(left, right, dims, preferred_element_type=F32)


def params():
    return pltpu.CompilerParams(vmem_limit_bytes=32 * 1024 * 1024)


def cost(flops, nbytes):
    return pl.CostEstimate(flops=flops, bytes_accessed=nbytes, transcendentals=0)


def shape(dims, dtype=BF16):
    return jax.ShapeDtypeStruct(dims, dtype)


def other_kernel(index_ref, acts_ref, grads_ref, turned_ref, out_ref, own_ref, acts_buf, grads_buf, total, sems):
    other = index_ref[0]
    steps, piece = acts_buf.shape[:2]

    def half(which):
        return pl.ds(pl.multiple_of(which * B, B), B)

    copies = []
    for k in range(steps):
        rows = pl.ds(k * piece, piece)
        copies.append(
            (
                pltpu.make_async_copy(acts_ref.at[rows, :], acts_buf.at[k], sems.at[0, k]),
                pltpu.make_async_copy(
                    grads_ref.at[rows, half(other)], grads_buf.at[k], sems.at[1, k]
                ),
            )
        )
        for copy in copies[-1]:
            copy.start()
    last = pltpu.make_async_copy(grads_ref.at[:, half(1 - other)], own_ref, sems.at[2, 0])
    last.start()
    for k, (acts_copy, grads_copy) in enumerate(copies):
        acts_copy.wait()
        turned = acts_buf[k].T
        turned_ref[:, k * piece : (k + 1) * piece] = turned
        grads_copy.wait()
        part = dot(turned, grads_buf[k])
        if k == 0:
            total[...] = part
        elif k < steps - 1:
            total[...] += part
        else:
            out_ref[...] = (total[...] + part).astype(BF16)
    last.wait()


def other_half(acts, grads, index):
    tokens, steps = acts.shape[0], 2
    anywhere = pl.BlockSpec(memory_space=pl.ANY)
    buffer = pltpu.VMEM((steps, tokens // steps, B), BF16)
    return pl.pallas_call(
        other_kernel,
        in_specs=[SMEM, anywhere, anywhere],
        out_specs=[VMEM] * 3,
        out_shape=[shape((B, tokens)), shape((B, B)), shape((tokens, B))],
        scratch_shapes=[
            buffer,
            buffer,
            pltpu.VMEM((B, B), F32),
            pltpu.SemaphoreType.DMA((3, steps)),
        ],
        compiler_params=pltpu.CompilerParams(vmem_limit_bytes=51 * 1024 * 1024),
        cost_estimate=cost(2 * tokens * B * B, 6 * tokens * B),
        name="other_half",
    )(index.reshape(1), acts, grads)


def own_kernel(turned_ref, grads_ref, out_ref):
    out_ref[...] = dot(turned_ref[...], grads_ref[...])


def join_kernel(own_ref, got_ref, prec_ref, out_ref):
    total = (own_ref[...] + got_ref[...].astype(F32)).astype(BF16).T
    rows = prec_ref.shape[2]
    for w in range(X):
        out_ref[w, :PART] = total[w * PART : (w + 1) * PART]
        for c in range(CORE):
            out_ref[w, PART + c * rows : PART + (c + 1) * rows] = prec_ref[0, c]


def shift(value, axis, step):
    size = lax.axis_size(axis)
    return lax.ppermute(value, axis, [(at, (at + step) % size) for at in range(size)])


def shifted(value, axis):
    return [shift(value, axis, step) for step in range(1, lax.axis_size(axis))]


def place(out_ref, parts, index):
    rows = parts[0].shape[0]
    for step, part in enumerate(parts):
        at = (index + len(parts) - step) % len(parts) * rows
        out_ref[pl.ds(pl.multiple_of(at, rows), rows), :] = part[...]


def sum_kernel(info_ref, parts_ref, mine_ref, theirs_ref, old_ref, *refs):
    keep_ref, right_ref, left_ref, left_send, old_low, send_ref = refs
    core = info_ref[0]
    rows = mine_ref.shape[0]
    right_ref[pl.ds(pl.multiple_of(core * rows, rows), rows), :] = mine_ref[...]
    right_ref[pl.ds(pl.multiple_of((1 - core) * rows, rows), rows), :] = theirs_ref[...]
    total = parts_ref[0, :PART].astype(F32)
    for w in range(X):
        for ref, c in ((left_ref, core), (left_send, 1 - core)):
            at = pl.multiple_of(PART + c * rows, rows)
            ref[w * rows : (w + 1) * rows] = parts_ref[w, pl.ds(at, rows), :]
        if w:
            total = total + parts_ref[w, :PART].astype(F32)
    keep_ref[...] = total
    send_ref[:PART] = total.astype(BF16)
    send_ref[PART:] = right_ref[...]
    old_low[...] = old_ref[...].astype(BF16)


def middle_kernel(keep_ref, right_ref, got_ref, old_ref, *refs):
    out_ref, send_ref, old_low = refs[-3:]
    total = keep_ref[...] + got_ref[:PART].astype(F32)
    out_ref[...] = total
    send_ref[:PART] = total.astype(BF16)
    send_ref[PART : PART + ROWS] = right_ref[...]
    send_ref[PART + ROWS :] = got_ref[PART:]
    old_low[...] = old_ref[...].astype(BF16)


def pack_kernel(scale, keep_ref, got_ref, *refs):
    pieces_ref = refs[-1]
    grad = ((keep_ref[...] + got_ref[:PART].astype(F32)) * scale).astype(BF16)
    n_mp, n_root, cores, rows, lanes = pieces_ref.shape
    for c in range(cores):
        for r in range(n_root):
            at = (c * n_root + r) * rows
            for m in range(n_mp):
                pieces_ref[m, r, c] = grad[at : at + rows, m * lanes : (m + 1) * lanes]


def choose_kernel(info_ref, listed_ref, blocks_ref, total_ref, *refs):
    out_ref = refs[-1]
    rows, lanes = out_ref.shape[2:]
    for w in range(X):
        pair = listed_ref[w * ZH + info_ref[2]] // 2
        for c in range(CORE):
            out_ref[w * CORE + c, 0] = blocks_ref[pair, c]
            at = w * ROWS + c * rows
            for lane in range(B // lanes):
                part = total_ref[at : at + rows, lane * lanes : (lane + 1) * lanes]
                out_ref[w * CORE + c, 1 + lane] = part.astype(BF16)


def spread_kernel(info_ref, listed_ref, parts_ref, *refs):
    out_ref = refs[-1]
    holder = listed_ref[info_ref[1] * ZH + info_ref[2]] % 2
    for w in range(X):
        tile = parts_ref[w * CORE + holder, 0]
        for peer in range(out_ref.shape[0]):
            out_ref[peer, w] = tile


def finish_kernel(parts_ref, out_ref):
    lanes = parts_ref.shape[3]
    for c in range(CORE):
        for lane in range(B // lanes):
            total = parts_ref[c, 1 + lane].astype(F32)
            for w in range(1, X):
                total = total + parts_ref[w * CORE + c, 1 + lane].astype(F32)
            at = c * B + lane * lanes
            out_ref[:, at : at + lanes] = total.astype(BF16)


def update_kernel(scale, info_ref, keep_ref, sent_ref, got_ref, mine_ref, theirs_ref, out_ref, left, right):
    core, zh = info_ref[0], info_ref[2]
    rows = ROWS // CORE
    for ref, c in ((mine_ref, core), (theirs_ref, 1 - core)):
        for w in range(X):
            at = pl.multiple_of(w * ROWS + c * rows, rows)
            left[pl.ds(at, rows), :] = ref[w * rows : (w + 1) * rows]
    near = zh + 1 - 2 * (zh % 2)
    far = ZH - 1 - zh
    across = far + 1 - 2 * (far % 2)
    first = jnp.where(core == 0, near, far)
    second = jnp.where(core == 0, far, near)
    for place_at, mate in enumerate((zh, first, second, across)):
        source = (sent_ref, got_ref)[place_at // 2]
        start = PART + place_at % 2 * ROWS
        to = pl.multiple_of(mate * ROWS, ROWS)
        right[pl.ds(to, ROWS), :] = source[start : start + ROWS]
    grad = ((keep_ref[...] + got_ref[:PART].astype(F32)) * scale).astype(BF16)
    product = dot(left[...], grad, 1, 1).astype(BF16)
    out_ref[...] = dot(product, right[...])


def refresh_kernel(info_ref, owner_ref, mine_ref, theirs_ref, own_ref, low_ref, one, two, three, stats_ref, roots_ref, block, product, old):
    core, x, zh, mp, root = (info_ref[at] for at in range(5))
    n_mp, n_root, _, rows, lanes = mine_ref.shape
    quarter = own_ref.shape[0]
    for ref, side in ((mine_ref, core), (theirs_ref, 1 - core)):
        for r in range(n_root):
            for w in range(X):
                at = pl.ds(pl.multiple_of(w * PART + (side * n_root + r) * rows, rows), rows)
                for m in range(n_mp):
                    block[at, m * lanes : (m + 1) * lanes] = ref[m, r, w]
    place(old, (low_ref, one, two, three), mp)

    @pl.when(core == 0)
    def _():
        value = block[...]
        product[...] = dot(value, value, 0, 0) * ((1.0 - DECAY) / B)

    @pl.when(core != 0)
    def _():
        value = block[...]
        product[...] = dot(value, value, 1, 1) * ((1.0 - DECAY) / B)

    mine = pl.ds(pl.multiple_of(mp * quarter, quarter), quarter)
    stats_rows = DECAY * own_ref[...] + product[mine, :]
    full = DECAY * old[...].astype(F32) + product[...]
    square = jnp.sum(full * full, axis=0, keepdims=True)
    factor = 2.5 / jnp.sqrt(jnp.sum(square, axis=1, keepdims=True))
    block[...] = (full * (factor * 0.2)).astype(BF16)
    e_rows = stats_rows * (factor * 0.2)
    y = e_rows
    for _ in range(5):
        y = y - dot(y.astype(BF16), block[...])
    line = lax.broadcasted_iota(jnp.int32, (quarter, B), 0) + mp * quarter
    unit = jnp.where(line == lax.broadcasted_iota(jnp.int32, (quarter, B), 1), 1.0, 0.0)
    roots_rows = (jnp.sqrt(jnp.sqrt(factor)) * 1.5625) * (unit - e_rows - KAPPA * y)
    owned = owner_ref[x * ZH + zh] == root
    stats_ref[...] = jnp.where(owned, stats_rows, 0.0)
    roots_ref[...] = jnp.where(owned, roots_rows, 0.0)


def kernel_call(kernel, name, in_specs, out_shape, scratch=(), work=None, awaited=0):
    return pl.pallas_call(
        kernel,
        in_specs=in_specs + [pl.BlockSpec(memory_space=pl.ANY)] * awaited,
        out_specs=[VMEM] * len(out_shape),
        out_shape=out_shape,
        scratch_shapes=list(scratch),
        compiler_params=params(),
        cost_estimate=work,
        name=name,
    )


def local(acts, grads_out, prec_left, prec_right, stats_old, listed, owner):
    x, zh, core = (lax.axis_index(name) for name in ("x", "zh", "core"))
    mp, root = lax.axis_index("mp"), lax.axis_index("root")
    n_mp, n_root = lax.axis_size("mp"), lax.axis_size("root")
    quarter = B // n_mp
    lanes, half = B // n_mp, ROWS // CORE
    tokens = acts.shape[0] * CHIPS * CORE
    swap = ((0, 1), (1, 0))
    info = jnp.stack([core, x, zh, mp, root])

    turned, send, grads_own = other_half(acts, grads_out, 1 - core)
    got = lax.ppermute(send, "core", swap)
    (own,) = kernel_call(
        own_kernel,
        "own_half",
        [VMEM, VMEM],
        [shape((B, B), F32)],
        work=cost(2 * acts.shape[0] * B * B, 4 * acts.shape[0] * B),
    )(turned, grads_own)
    (total,) = kernel_call(
        join_kernel, "join", [VMEM] * 3, [shape((X, PART + ROWS, B))]
    )(own, got, prec_left)
    total = lax.all_to_all(total, "x", 0, 0)
    mine = lax.dynamic_index_in_dim(prec_right[0], core, 0, keepdims=False)
    theirs = lax.ppermute(
        lax.dynamic_index_in_dim(prec_right[0], 1 - core, 0, keepdims=False), "core", swap
    )
    old_own = stats_old[0]
    keep, right_rows, left_mine, left_send, old_low, send = kernel_call(
        sum_kernel,
        "sum_x",
        [SMEM] + [VMEM] * 4,
        [shape((PART, B), F32), shape((ROWS, B))]
        + [shape((PART // CORE, B))] * 2
        + [shape((quarter, B)), shape((PART + ROWS, B))],
    )(info, total, mine, theirs, old_own)

    near_far = [
        [
            (z * CORE + c, ((z ^ 1) if c == step else ZH - 1 - z) * CORE + c)
            for z in range(ZH)
            for c in range(CORE)
        ]
        for step in range(2)
    ]
    got = lax.ppermute(send, ("zh", "core"), near_far[0])
    left_theirs = lax.ppermute(left_send, "core", swap)
    olds = [old_low, shift(old_low, "mp", 1)]
    keep, send, old_later = kernel_call(
        middle_kernel,
        "middle",
        [VMEM] * 4,
        [shape((PART, B), F32), shape((PART + 2 * ROWS, B)), shape((quarter, B))],
        awaited=2,
    )(keep, right_rows, got, old_own, left_theirs, olds[1])
    got = lax.ppermute(send, ("zh", "core"), near_far[1])
    olds += [shift(old_later, "mp", step) for step in range(2, n_mp)]
    (pieces,) = kernel_call(
        functools.partial(pack_kernel, tokens ** -0.5),
        "pack",
        [VMEM] * 2,
        [shape((n_mp, n_root, CORE, half, lanes))],
        awaited=2,
    )(keep, got, *olds[2:])

    pieces = pieces.reshape((n_mp * n_root,) + pieces.shape[2:])
    blocks = lax.all_to_all(pieces, ("mp", "root"), 0, 0)

    (total,) = kernel_call(
        functools.partial(update_kernel, tokens ** -0.5),
        "update",
        [SMEM] + [VMEM] * 5,
        [shape((PART, B), F32)],
        [pltpu.VMEM((PART, B), BF16)] * 2,
        cost(2 * PART * B * (PART + B), 6 * PART * B),
    )(info, keep, send, got, left_mine, left_theirs)

    (chosen,) = kernel_call(
        choose_kernel,
        "choose",
        [SMEM, SMEM, VMEM, VMEM],
        [shape((X * CORE, 1 + B // lanes, half, lanes))],
    )(info, listed, blocks, total)
    parts = lax.all_to_all(chosen, ("x", "core"), 0, 0)
    (mine,) = kernel_call(
        spread_kernel,
        "spread",
        [SMEM, SMEM, VMEM],
        [shape((n_mp * n_root, X, half, lanes))],
    )(info, listed, parts)
    mine = lax.all_to_all(mine, ("mp", "root"), 0, 0)
    theirs = lax.ppermute(mine, "core", swap)
    gathered = [value.reshape((n_mp, n_root) + value.shape[1:]) for value in (mine, theirs)]
    (update,) = kernel_call(finish_kernel, "finish", [VMEM], [shape((half, 2 * B))])(parts)

    new_stats, new_roots = kernel_call(
        refresh_kernel,
        "refresh",
        [SMEM, SMEM] + [VMEM] * 7,
        [shape((quarter, B), F32)] * 2,
        [pltpu.VMEM((B, B), BF16), pltpu.VMEM((B, B), F32), pltpu.VMEM((B, B), BF16)],
        cost(2 * B ** 3 + 10 * quarter * B * B, 2 * B * B * 2),
    )(info, owner, *gathered, old_own, *olds)
    return update[None], new_stats[None, None], new_roots[None, None]


def solution(mesh):
    n_dp, n_mp, n_root = mesh.devices.shape
    fine = Mesh(
        mesh.devices.reshape(X, ZH, CORE, n_mp, n_root), ("x", "zh", "core", "mp", "root")
    )
    dp = ("x", "zh", "core")
    in_specs = (
        P(dp, "mp"),
        P(dp, "root"),
        P("mp", "root", dp, None),
        P("mp", "root", dp, None),
        P(dp, "mp", None),
        P(),
        P(),
    )
    out_specs = (P("mp", dp, "root"), P("root", dp, "mp", None), P("root", dp, "mp", None))
    return jax.shard_map(local, mesh=fine, in_specs=in_specs, out_specs=out_specs, check_vma=False)
```

```python
import functools

import jax
import jax.numpy as jnp
from jax import lax
from jax.experimental import pallas as pl
from jax.experimental.pallas import tpu as pltpu
from jax.sharding import Mesh, PartitionSpec as P

B = 512
DECAY = 0.6
KAPPA = 1.25 ** 4
X, ZH, CORE = 4, 4, 2
CHIPS = X * ZH
PART = B // X
ROWS = B // CHIPS
F32, BF16 = jnp.float32, jnp.bfloat16
VMEM = pl.BlockSpec(memory_space=pltpu.VMEM)
SMEM = pl.BlockSpec(memory_space=pltpu.SMEM)


def dot(left, right, left_dim=1, right_dim=0):
    dims = (((left_dim,), (right_dim,)), ((), ()))
    return lax.dot_general(left, right, dims, preferred_element_type=F32)


def params():
    return pltpu.CompilerParams(vmem_limit_bytes=32 * 1024 * 1024)


def cost(flops, nbytes):
    return pl.CostEstimate(flops=flops, bytes_accessed=nbytes, transcendentals=0)


def shape(dims, dtype=BF16):
    return jax.ShapeDtypeStruct(dims, dtype)


def other_kernel(index_ref, acts_ref, grads_ref, turned_ref, out_ref, own_ref, acts_buf, grads_buf, total, sems):
    other = index_ref[0]
    steps, piece = acts_buf.shape[:2]

    def half(which):
        return pl.ds(pl.multiple_of(which * B, B), B)

    copies = []
    for k in range(steps):
        rows = pl.ds(k * piece, piece)
        copies.append(
            (
                pltpu.make_async_copy(acts_ref.at[rows, :], acts_buf.at[k], sems.at[0, k]),
                pltpu.make_async_copy(
                    grads_ref.at[rows, half(other)], grads_buf.at[k], sems.at[1, k]
                ),
            )
        )
        for copy in copies[-1]:
            copy.start()
    last = pltpu.make_async_copy(grads_ref.at[:, half(1 - other)], own_ref, sems.at[2, 0])
    last.start()
    for k, (acts_copy, grads_copy) in enumerate(copies):
        acts_copy.wait()
        turned = acts_buf[k].T
        turned_ref[:, k * piece : (k + 1) * piece] = turned
        grads_copy.wait()
        part = dot(turned, grads_buf[k])
        if k == 0:
            total[...] = part
        elif k < steps - 1:
            total[...] += part
        else:
            out_ref[...] = (total[...] + part).astype(BF16)
    last.wait()


def other_half(acts, grads, index):
    tokens, steps = acts.shape[0], 2
    anywhere = pl.BlockSpec(memory_space=pl.ANY)
    buffer = pltpu.VMEM((steps, tokens // steps, B), BF16)
    return pl.pallas_call(
        other_kernel,
        in_specs=[SMEM, anywhere, anywhere],
        out_specs=[VMEM] * 3,
        out_shape=[shape((B, tokens)), shape((B, B)), shape((tokens, B))],
        scratch_shapes=[
            buffer,
            buffer,
            pltpu.VMEM((B, B), F32),
            pltpu.SemaphoreType.DMA((3, steps)),
        ],
        compiler_params=pltpu.CompilerParams(vmem_limit_bytes=51 * 1024 * 1024),
        cost_estimate=cost(2 * tokens * B * B, 6 * tokens * B),
        name="other_half",
    )(index.reshape(1), acts, grads)


def own_kernel(turned_ref, grads_ref, out_ref):
    out_ref[...] = dot(turned_ref[...], grads_ref[...])


def mates(core, at, size):
    near = at + 1 - 2 * (at % 2)
    far = size - 1 - at
    first = jnp.where(core == 0, near, far)
    second = jnp.where(core == 0, far, near)
    return first, second, far + 1 - 2 * (far % 2)


def join_kernel(info_ref, own_ref, got_ref, prec_ref, keep_ref, send_ref, total):
    x = info_ref[1]
    first, second, across = mates(info_ref[0], x, X)
    total[...] = (own_ref[...] + got_ref[...].astype(F32)).T
    for ref, pair in ((keep_ref, (x, second)), (send_ref, (first, across))):
        for part, mate in enumerate(pair):
            rows = total[pl.ds(pl.multiple_of(mate * PART, PART), PART), :]
            ref[part * PART : (part + 1) * PART] = rows.astype(ref.dtype)
    rows = prec_ref.shape[2]
    for c in range(CORE):
        send_ref[2 * PART + c * rows : 2 * PART + (c + 1) * rows] = prec_ref[0, c]


def half_kernel(keep_ref, sent_ref, got_ref, out_ref, send_ref):
    total = keep_ref[...] + got_ref[: 2 * PART].astype(F32)
    out_ref[...] = total[:PART]
    send_ref[:PART] = total[PART:].astype(BF16)
    send_ref[PART : PART + ROWS] = sent_ref[2 * PART :]
    send_ref[PART + ROWS :] = got_ref[2 * PART :]


def shift(value, axis, step):
    size = lax.axis_size(axis)
    return lax.ppermute(value, axis, [(at, (at + step) % size) for at in range(size)])


def shifted(value, axis):
    return [shift(value, axis, step) for step in range(1, lax.axis_size(axis))]


def place(out_ref, parts, index):
    rows = parts[0].shape[0]
    for step, part in enumerate(parts):
        at = (index + len(parts) - step) % len(parts) * rows
        out_ref[pl.ds(pl.multiple_of(at, rows), rows), :] = part[...]


def sum_kernel(info_ref, part_ref, sent_ref, got_ref, mine_ref, theirs_ref, old_ref, *refs):
    keep_ref, right_ref, left_ref, left_send, old_low, send_ref = refs
    core, x = info_ref[0], info_ref[1]
    rows = mine_ref.shape[0]
    right_ref[pl.ds(pl.multiple_of(core * rows, rows), rows), :] = mine_ref[...]
    right_ref[pl.ds(pl.multiple_of((1 - core) * rows, rows), rows), :] = theirs_ref[...]
    for place_at, mate in enumerate((x, *mates(core, x, X))):
        source = (sent_ref, got_ref)[place_at // 2]
        start = PART + place_at % 2 * ROWS
        to = pl.ds(pl.multiple_of(mate * rows, rows), rows)
        for ref, c in ((left_ref, core), (left_send, 1 - core)):
            ref[to, :] = source[pl.ds(pl.multiple_of(start + c * rows, rows), rows), :]
    total = part_ref[...] + got_ref[:PART].astype(F32)
    keep_ref[...] = total
    send_ref[:PART] = total.astype(BF16)
    send_ref[PART:] = right_ref[...]
    old_low[...] = old_ref[...].astype(BF16)


def middle_kernel(keep_ref, right_ref, got_ref, old_ref, *refs):
    out_ref, send_ref, old_low = refs[-3:]
    total = keep_ref[...] + got_ref[:PART].astype(F32)
    out_ref[...] = total
    send_ref[:PART] = total.astype(BF16)
    send_ref[PART : PART + ROWS] = right_ref[...]
    send_ref[PART + ROWS :] = got_ref[PART:]
    old_low[...] = old_ref[...].astype(BF16)


def pack_kernel(scale, keep_ref, got_ref, *refs):
    pieces_ref = refs[-1]
    grad = ((keep_ref[...] + got_ref[:PART].astype(F32)) * scale).astype(BF16)
    n_mp, n_root, cores, rows, lanes = pieces_ref.shape
    for c in range(cores):
        for r in range(n_root):
            at = (c * n_root + r) * rows
            for m in range(n_mp):
                pieces_ref[m, r, c] = grad[at : at + rows, m * lanes : (m + 1) * lanes]


def choose_kernel(info_ref, listed_ref, blocks_ref, total_ref, *refs):
    out_ref = refs[-1]
    rows, lanes = out_ref.shape[2:]
    for w in range(X):
        pair = listed_ref[w * ZH + info_ref[2]] // 2
        for c in range(CORE):
            out_ref[w * CORE + c, 0] = blocks_ref[pair, c]
            at = w * ROWS + c * rows
            for lane in range(B // lanes):
                part = total_ref[at : at + rows, lane * lanes : (lane + 1) * lanes]
                out_ref[w * CORE + c, 1 + lane] = part.astype(BF16)


def spread_kernel(info_ref, listed_ref, parts_ref, *refs):
    out_ref = refs[-1]
    holder = listed_ref[info_ref[1] * ZH + info_ref[2]] % 2
    for w in range(X):
        tile = parts_ref[w * CORE + holder, 0]
        for peer in range(out_ref.shape[0]):
            out_ref[peer, w] = tile


def finish_kernel(parts_ref, out_ref):
    lanes = parts_ref.shape[3]
    for c in range(CORE):
        for lane in range(B // lanes):
            total = parts_ref[c, 1 + lane].astype(F32)
            for w in range(1, X):
                total = total + parts_ref[w * CORE + c, 1 + lane].astype(F32)
            at = c * B + lane * lanes
            out_ref[:, at : at + lanes] = total.astype(BF16)


def update_kernel(scale, info_ref, keep_ref, sent_ref, got_ref, mine_ref, theirs_ref, out_ref, left, right):
    core, zh = info_ref[0], info_ref[2]
    rows = ROWS // CORE
    for ref, c in ((mine_ref, core), (theirs_ref, 1 - core)):
        for w in range(X):
            at = pl.multiple_of(w * ROWS + c * rows, rows)
            left[pl.ds(at, rows), :] = ref[w * rows : (w + 1) * rows]
    near = zh + 1 - 2 * (zh % 2)
    far = ZH - 1 - zh
    across = far + 1 - 2 * (far % 2)
    first = jnp.where(core == 0, near, far)
    second = jnp.where(core == 0, far, near)
    for place_at, mate in enumerate((zh, first, second, across)):
        source = (sent_ref, got_ref)[place_at // 2]
        start = PART + place_at % 2 * ROWS
        to = pl.multiple_of(mate * ROWS, ROWS)
        right[pl.ds(to, ROWS), :] = source[start : start + ROWS]
    grad = ((keep_ref[...] + got_ref[:PART].astype(F32)) * scale).astype(BF16)
    product = dot(left[...], grad, 1, 1).astype(BF16)
    out_ref[...] = dot(product, right[...])


def refresh_kernel(info_ref, owner_ref, mine_ref, theirs_ref, own_ref, low_ref, one, two, three, stats_ref, roots_ref, block, product, old):
    core, x, zh, mp, root = (info_ref[at] for at in range(5))
    n_mp, n_root, _, rows, lanes = mine_ref.shape
    quarter = own_ref.shape[0]
    for ref, side in ((mine_ref, core), (theirs_ref, 1 - core)):
        for r in range(n_root):
            for w in range(X):
                at = pl.ds(pl.multiple_of(w * PART + (side * n_root + r) * rows, rows), rows)
                for m in range(n_mp):
                    block[at, m * lanes : (m + 1) * lanes] = ref[m, r, w]
    place(old, (low_ref, one, two, three), mp)

    @pl.when(core == 0)
    def _():
        value = block[...]
        product[...] = dot(value, value, 0, 0) * ((1.0 - DECAY) / B)

    @pl.when(core != 0)
    def _():
        value = block[...]
        product[...] = dot(value, value, 1, 1) * ((1.0 - DECAY) / B)

    mine = pl.ds(pl.multiple_of(mp * quarter, quarter), quarter)
    stats_rows = DECAY * own_ref[...] + product[mine, :]
    full = DECAY * old[...].astype(F32) + product[...]
    square = jnp.sum(full * full, axis=0, keepdims=True)
    factor = 2.5 / jnp.sqrt(jnp.sum(square, axis=1, keepdims=True))
    block[...] = (full * (factor * 0.2)).astype(BF16)
    e_rows = stats_rows * (factor * 0.2)
    y = e_rows
    for _ in range(5):
        y = y - dot(y.astype(BF16), block[...])
    line = lax.broadcasted_iota(jnp.int32, (quarter, B), 0) + mp * quarter
    unit = jnp.where(line == lax.broadcasted_iota(jnp.int32, (quarter, B), 1), 1.0, 0.0)
    roots_rows = (jnp.sqrt(jnp.sqrt(factor)) * 1.5625) * (unit - e_rows - KAPPA * y)
    owned = owner_ref[x * ZH + zh] == root
    stats_ref[...] = jnp.where(owned, stats_rows, 0.0)
    roots_ref[...] = jnp.where(owned, roots_rows, 0.0)


def kernel_call(kernel, name, in_specs, out_shape, scratch=(), work=None, awaited=0):
    return pl.pallas_call(
        kernel,
        in_specs=in_specs + [pl.BlockSpec(memory_space=pl.ANY)] * awaited,
        out_specs=[VMEM] * len(out_shape),
        out_shape=out_shape,
        scratch_shapes=list(scratch),
        compiler_params=params(),
        cost_estimate=work,
        name=name,
    )


def local(acts, grads_out, prec_left, prec_right, stats_old, listed, owner):
    x, zh, core = (lax.axis_index(name) for name in ("x", "zh", "core"))
    mp, root = lax.axis_index("mp"), lax.axis_index("root")
    n_mp, n_root = lax.axis_size("mp"), lax.axis_size("root")
    quarter = B // n_mp
    lanes, half = B // n_mp, ROWS // CORE
    tokens = acts.shape[0] * CHIPS * CORE
    swap = ((0, 1), (1, 0))
    info = jnp.stack([core, x, zh, mp, root])

    turned, send, grads_own = other_half(acts, grads_out, 1 - core)
    got = lax.ppermute(send, "core", swap)
    (own,) = kernel_call(
        own_kernel,
        "own_half",
        [VMEM, VMEM],
        [shape((B, B), F32)],
        work=cost(2 * acts.shape[0] * B * B, 4 * acts.shape[0] * B),
    )(turned, grads_own)
    keep, send = kernel_call(
        join_kernel,
        "join",
        [SMEM] + [VMEM] * 3,
        [shape((2 * PART, B), F32), shape((2 * PART + ROWS, B))],
        [pltpu.VMEM((B, B), F32)],
    )(info, own, got, prec_left)
    near_far = [
        [
            (z * CORE + c, ((z ^ 1) if c == step else X - 1 - z) * CORE + c)
            for z in range(X)
            for c in range(CORE)
        ]
        for step in range(2)
    ]
    got = lax.ppermute(send, ("x", "core"), near_far[0])
    keep, send = kernel_call(
        half_kernel,
        "half_x",
        [VMEM] * 3,
        [shape((PART, B), F32), shape((PART + 2 * ROWS, B))],
    )(keep, send, got)
    got = lax.ppermute(send, ("x", "core"), near_far[1])
    mine = lax.dynamic_index_in_dim(prec_right[0], core, 0, keepdims=False)
    theirs = lax.ppermute(
        lax.dynamic_index_in_dim(prec_right[0], 1 - core, 0, keepdims=False), "core", swap
    )
    old_own = stats_old[0]
    keep, right_rows, left_mine, left_send, old_low, send = kernel_call(
        sum_kernel,
        "sum_x",
        [SMEM] + [VMEM] * 6,
        [shape((PART, B), F32), shape((ROWS, B))]
        + [shape((PART // CORE, B))] * 2
        + [shape((quarter, B)), shape((PART + ROWS, B))],
    )(info, keep, send, got, mine, theirs, old_own)

    near_far = [
        [
            (z * CORE + c, ((z ^ 1) if c == step else ZH - 1 - z) * CORE + c)
            for z in range(ZH)
            for c in range(CORE)
        ]
        for step in range(2)
    ]
    got = lax.ppermute(send, ("zh", "core"), near_far[0])
    left_theirs = lax.ppermute(left_send, "core", swap)
    olds = [old_low, shift(old_low, "mp", 1)]
    keep, send, old_later = kernel_call(
        middle_kernel,
        "middle",
        [VMEM] * 4,
        [shape((PART, B), F32), shape((PART + 2 * ROWS, B)), shape((quarter, B))],
        awaited=2,
    )(keep, right_rows, got, old_own, left_theirs, olds[1])
    got = lax.ppermute(send, ("zh", "core"), near_far[1])
    olds += [shift(old_later, "mp", step) for step in range(2, n_mp)]
    (pieces,) = kernel_call(
        functools.partial(pack_kernel, tokens ** -0.5),
        "pack",
        [VMEM] * 2,
        [shape((n_mp, n_root, CORE, half, lanes))],
        awaited=2,
    )(keep, got, *olds[2:])

    pieces = pieces.reshape((n_mp * n_root,) + pieces.shape[2:])
    blocks = lax.all_to_all(pieces, ("mp", "root"), 0, 0)

    (total,) = kernel_call(
        functools.partial(update_kernel, tokens ** -0.5),
        "update",
        [SMEM] + [VMEM] * 5,
        [shape((PART, B), F32)],
        [pltpu.VMEM((PART, B), BF16)] * 2,
        cost(2 * PART * B * (PART + B), 6 * PART * B),
    )(info, keep, send, got, left_mine, left_theirs)

    (chosen,) = kernel_call(
        choose_kernel,
        "choose",
        [SMEM, SMEM, VMEM, VMEM],
        [shape((X * CORE, 1 + B // lanes, half, lanes))],
    )(info, listed, blocks, total)
    parts = lax.all_to_all(chosen, ("x", "core"), 0, 0)
    (mine,) = kernel_call(
        spread_kernel,
        "spread",
        [SMEM, SMEM, VMEM],
        [shape((n_mp * n_root, X, half, lanes))],
    )(info, listed, parts)
    mine = lax.all_to_all(mine, ("mp", "root"), 0, 0)
    theirs = lax.ppermute(mine, "core", swap)
    gathered = [value.reshape((n_mp, n_root) + value.shape[1:]) for value in (mine, theirs)]
    (update,) = kernel_call(finish_kernel, "finish", [VMEM], [shape((half, 2 * B))])(parts)

    new_stats, new_roots = kernel_call(
        refresh_kernel,
        "refresh",
        [SMEM, SMEM] + [VMEM] * 7,
        [shape((quarter, B), F32)] * 2,
        [pltpu.VMEM((B, B), BF16), pltpu.VMEM((B, B), F32), pltpu.VMEM((B, B), BF16)],
        cost(2 * B ** 3 + 10 * quarter * B * B, 2 * B * B * 2),
    )(info, owner, *gathered, old_own, *olds)
    return update[None], new_stats[None, None], new_roots[None, None]


def solution(mesh):
    n_dp, n_mp, n_root = mesh.devices.shape
    fine = Mesh(
        mesh.devices.reshape(X, ZH, CORE, n_mp, n_root), ("x", "zh", "core", "mp", "root")
    )
    dp = ("x", "zh", "core")
    in_specs = (
        P(dp, "mp"),
        P(dp, "root"),
        P("mp", "root", dp, None),
        P("mp", "root", dp, None),
        P(dp, "mp", None),
        P(),
        P(),
    )
    out_specs = (P("mp", dp, "root"), P("root", dp, "mp", None), P("root", dp, "mp", None))
    return jax.shard_map(local, mesh=fine, in_specs=in_specs, out_specs=out_specs, check_vma=False)
```

```python
import functools

import jax
import jax.numpy as jnp
from jax import lax
from jax.experimental import pallas as pl
from jax.experimental.pallas import tpu as pltpu
from jax.sharding import Mesh, PartitionSpec as P

B = 512
DECAY = 0.6
KAPPA = 1.25 ** 4
X, ZH, CORE = 4, 4, 2
CHIPS = X * ZH
PART = B // X
ROWS = B // CHIPS
F32, BF16 = jnp.float32, jnp.bfloat16
VMEM = pl.BlockSpec(memory_space=pltpu.VMEM)
SMEM = pl.BlockSpec(memory_space=pltpu.SMEM)


def dot(left, right, left_dim=1, right_dim=0):
    dims = (((left_dim,), (right_dim,)), ((), ()))
    return lax.dot_general(left, right, dims, preferred_element_type=F32)


def params():
    return pltpu.CompilerParams(vmem_limit_bytes=32 * 1024 * 1024)


def cost(flops, nbytes):
    return pl.CostEstimate(flops=flops, bytes_accessed=nbytes, transcendentals=0)


def shape(dims, dtype=BF16):
    return jax.ShapeDtypeStruct(dims, dtype)


def other_kernel(index_ref, acts_ref, grads_ref, turned_ref, out_ref, own_ref, acts_buf, grads_buf, total, sems):
    other = index_ref[0]
    steps, piece = acts_buf.shape[:2]

    def half(which):
        return pl.ds(pl.multiple_of(which * B, B), B)

    copies = []
    for k in range(steps):
        rows = pl.ds(k * piece, piece)
        copies.append(
            (
                pltpu.make_async_copy(acts_ref.at[rows, :], acts_buf.at[k], sems.at[0, k]),
                pltpu.make_async_copy(
                    grads_ref.at[rows, half(other)], grads_buf.at[k], sems.at[1, k]
                ),
            )
        )
        for copy in copies[-1]:
            copy.start()
    last = pltpu.make_async_copy(grads_ref.at[:, half(1 - other)], own_ref, sems.at[2, 0])
    last.start()
    for k, (acts_copy, grads_copy) in enumerate(copies):
        acts_copy.wait()
        turned = acts_buf[k].T
        turned_ref[:, k * piece : (k + 1) * piece] = turned
        grads_copy.wait()
        part = dot(turned, grads_buf[k])
        if k == 0:
            total[...] = part
        elif k < steps - 1:
            total[...] += part
        else:
            out_ref[...] = (total[...] + part).astype(BF16)
    last.wait()


def other_half(acts, grads, index):
    tokens, steps = acts.shape[0], 2
    anywhere = pl.BlockSpec(memory_space=pl.ANY)
    buffer = pltpu.VMEM((steps, tokens // steps, B), BF16)
    return pl.pallas_call(
        other_kernel,
        in_specs=[SMEM, anywhere, anywhere],
        out_specs=[VMEM] * 3,
        out_shape=[shape((B, tokens)), shape((B, B)), shape((tokens, B))],
        scratch_shapes=[
            buffer,
            buffer,
            pltpu.VMEM((B, B), F32),
            pltpu.SemaphoreType.DMA((3, steps)),
        ],
        compiler_params=pltpu.CompilerParams(vmem_limit_bytes=51 * 1024 * 1024),
        cost_estimate=cost(2 * tokens * B * B, 6 * tokens * B),
        name="other_half",
    )(index.reshape(1), acts, grads)


def own_kernel(turned_ref, grads_ref, out_ref):
    out_ref[...] = dot(turned_ref[...], grads_ref[...])


def join_kernel(own_ref, got_ref, out_ref):
    out_ref[...] = (own_ref[...] + got_ref[...].astype(F32)).astype(BF16).T


def shift(value, axis, step):
    size = lax.axis_size(axis)
    return lax.ppermute(value, axis, [(at, (at + step) % size) for at in range(size)])


def shifted(value, axis):
    return [shift(value, axis, step) for step in range(1, lax.axis_size(axis))]


def place(out_ref, parts, index):
    rows = parts[0].shape[0]
    for step, part in enumerate(parts):
        at = (index + len(parts) - step) % len(parts) * rows
        out_ref[pl.ds(pl.multiple_of(at, rows), rows), :] = part[...]


def sum_kernel(info_ref, parts_ref, mine_ref, theirs_ref, prec_ref, *refs):
    keep_ref, right_ref, left_ref, send_ref = refs[-4:]
    core = info_ref[0]
    rows = mine_ref.shape[0]
    right_ref[pl.ds(pl.multiple_of(core * rows, rows), rows), :] = mine_ref[...]
    right_ref[pl.ds(pl.multiple_of((1 - core) * rows, rows), rows), :] = theirs_ref[...]
    for c in range(CORE):
        left_ref[c * rows : (c + 1) * rows] = prec_ref[0, c]
    total = parts_ref[0].astype(F32)
    for w in range(1, X):
        total = total + parts_ref[w].astype(F32)
    keep_ref[...] = total
    send_ref[:PART] = total.astype(BF16)
    send_ref[PART:] = right_ref[...]


def middle_kernel(info_ref, keep_ref, right_ref, got_ref, old_ref, own_ref, one, two, *refs):
    out_ref, send_ref, old_low, left_ref, left_send = refs
    total = keep_ref[...] + got_ref[:PART].astype(F32)
    out_ref[...] = total
    send_ref[:PART] = total.astype(BF16)
    send_ref[PART : PART + ROWS] = right_ref[...]
    send_ref[PART + ROWS :] = got_ref[PART:]
    old_low[...] = old_ref[...].astype(BF16)
    core, x = info_ref[0], info_ref[1]
    rows = ROWS // CORE
    near = x + 1 - 2 * (x % 2)
    far = X - 1 - x
    across = far + 1 - 2 * (far % 2)
    first = jnp.where(core == 0, near, far)
    second = jnp.where(core == 0, far, near)
    for mate, source, start in (
        (x, own_ref, 0),
        (first, one, 0),
        (second, two, 0),
        (across, two, ROWS),
    ):
        to = pl.ds(pl.multiple_of(mate * rows, rows), rows)
        for ref, c in ((left_ref, core), (left_send, 1 - core)):
            ref[to, :] = source[pl.ds(pl.multiple_of(start + c * rows, rows), rows), :]


def pack_kernel(scale, keep_ref, got_ref, *refs):
    pieces_ref = refs[-1]
    grad = ((keep_ref[...] + got_ref[:PART].astype(F32)) * scale).astype(BF16)
    n_mp, n_root, cores, rows, lanes = pieces_ref.shape
    for c in range(cores):
        for r in range(n_root):
            at = (c * n_root + r) * rows
            for m in range(n_mp):
                pieces_ref[m, r, c] = grad[at : at + rows, m * lanes : (m + 1) * lanes]


def choose_kernel(info_ref, listed_ref, blocks_ref, total_ref, *refs):
    out_ref = refs[-1]
    rows, lanes = out_ref.shape[2:]
    for w in range(X):
        pair = listed_ref[w * ZH + info_ref[2]] // 2
        for c in range(CORE):
            out_ref[w * CORE + c, 0] = blocks_ref[pair, c]
            at = w * ROWS + c * rows
            for lane in range(B // lanes):
                part = total_ref[at : at + rows, lane * lanes : (lane + 1) * lanes]
                out_ref[w * CORE + c, 1 + lane] = part.astype(BF16)


def spread_kernel(info_ref, listed_ref, parts_ref, *refs):
    out_ref = refs[-1]
    holder = listed_ref[info_ref[1] * ZH + info_ref[2]] % 2
    for w in range(X):
        tile = parts_ref[w * CORE + holder, 0]
        for peer in range(out_ref.shape[0]):
            out_ref[peer, w] = tile


def finish_kernel(parts_ref, out_ref):
    lanes = parts_ref.shape[3]
    for c in range(CORE):
        for lane in range(B // lanes):
            total = parts_ref[c, 1 + lane].astype(F32)
            for w in range(1, X):
                total = total + parts_ref[w * CORE + c, 1 + lane].astype(F32)
            at = c * B + lane * lanes
            out_ref[:, at : at + lanes] = total.astype(BF16)


def update_kernel(scale, info_ref, keep_ref, sent_ref, got_ref, mine_ref, theirs_ref, out_ref, left, right):
    core, zh = info_ref[0], info_ref[2]
    rows = ROWS // CORE
    for ref, c in ((mine_ref, core), (theirs_ref, 1 - core)):
        for w in range(X):
            at = pl.multiple_of(w * ROWS + c * rows, rows)
            left[pl.ds(at, rows), :] = ref[w * rows : (w + 1) * rows]
    near = zh + 1 - 2 * (zh % 2)
    far = ZH - 1 - zh
    across = far + 1 - 2 * (far % 2)
    first = jnp.where(core == 0, near, far)
    second = jnp.where(core == 0, far, near)
    for place_at, mate in enumerate((zh, first, second, across)):
        source = (sent_ref, got_ref)[place_at // 2]
        start = PART + place_at % 2 * ROWS
        to = pl.multiple_of(mate * ROWS, ROWS)
        right[pl.ds(to, ROWS), :] = source[start : start + ROWS]
    grad = ((keep_ref[...] + got_ref[:PART].astype(F32)) * scale).astype(BF16)
    product = dot(left[...], grad, 1, 1).astype(BF16)
    out_ref[...] = dot(product, right[...])


def refresh_kernel(info_ref, owner_ref, mine_ref, theirs_ref, own_ref, low_ref, one, two, three, stats_ref, roots_ref, block, product, old):
    core, x, zh, mp, root = (info_ref[at] for at in range(5))
    n_mp, n_root, _, rows, lanes = mine_ref.shape
    quarter = own_ref.shape[0]
    for ref, side in ((mine_ref, core), (theirs_ref, 1 - core)):
        for r in range(n_root):
            for w in range(X):
                at = pl.ds(pl.multiple_of(w * PART + (side * n_root + r) * rows, rows), rows)
                for m in range(n_mp):
                    block[at, m * lanes : (m + 1) * lanes] = ref[m, r, w]
    place(old, (low_ref, one, two, three), mp)

    @pl.when(core == 0)
    def _():
        value = block[...]
        product[...] = dot(value, value, 0, 0) * ((1.0 - DECAY) / B)

    @pl.when(core != 0)
    def _():
        value = block[...]
        product[...] = dot(value, value, 1, 1) * ((1.0 - DECAY) / B)

    mine = pl.ds(pl.multiple_of(mp * quarter, quarter), quarter)
    stats_rows = DECAY * own_ref[...] + product[mine, :]
    full = DECAY * old[...].astype(F32) + product[...]
    square = jnp.sum(full * full, axis=0, keepdims=True)
    factor = 2.5 / jnp.sqrt(jnp.sum(square, axis=1, keepdims=True))
    block[...] = (full * (factor * 0.2)).astype(BF16)
    e_rows = stats_rows * (factor * 0.2)
    y = e_rows
    for _ in range(5):
        y = y - dot(y.astype(BF16), block[...])
    line = lax.broadcasted_iota(jnp.int32, (quarter, B), 0) + mp * quarter
    unit = jnp.where(line == lax.broadcasted_iota(jnp.int32, (quarter, B), 1), 1.0, 0.0)
    roots_rows = (jnp.sqrt(jnp.sqrt(factor)) * 1.5625) * (unit - e_rows - KAPPA * y)
    owned = owner_ref[x * ZH + zh] == root
    stats_ref[...] = jnp.where(owned, stats_rows, 0.0)
    roots_ref[...] = jnp.where(owned, roots_rows, 0.0)


def kernel_call(kernel, name, in_specs, out_shape, scratch=(), work=None, awaited=0):
    return pl.pallas_call(
        kernel,
        in_specs=in_specs + [pl.BlockSpec(memory_space=pl.ANY)] * awaited,
        out_specs=[VMEM] * len(out_shape),
        out_shape=out_shape,
        scratch_shapes=list(scratch),
        compiler_params=params(),
        cost_estimate=work,
        name=name,
    )


def local(acts, grads_out, prec_left, prec_right, stats_old, listed, owner):
    x, zh, core = (lax.axis_index(name) for name in ("x", "zh", "core"))
    mp, root = lax.axis_index("mp"), lax.axis_index("root")
    n_mp, n_root = lax.axis_size("mp"), lax.axis_size("root")
    quarter = B // n_mp
    lanes, half = B // n_mp, ROWS // CORE
    tokens = acts.shape[0] * CHIPS * CORE
    swap = ((0, 1), (1, 0))
    info = jnp.stack([core, x, zh, mp, root])

    turned, send, grads_own = other_half(acts, grads_out, 1 - core)
    got = lax.ppermute(send, "core", swap)
    (own,) = kernel_call(
        own_kernel,
        "own_half",
        [VMEM, VMEM],
        [shape((B, B), F32)],
        work=cost(2 * acts.shape[0] * B * B, 4 * acts.shape[0] * B),
    )(turned, grads_own)
    (total,) = kernel_call(join_kernel, "join", [VMEM] * 2, [shape((B, B))])(own, got)
    total = total.reshape(X, PART, B)
    total = lax.all_to_all(total, "x", 0, 0)
    mine = lax.dynamic_index_in_dim(prec_right[0], core, 0, keepdims=False)
    theirs = lax.ppermute(
        lax.dynamic_index_in_dim(prec_right[0], 1 - core, 0, keepdims=False), "core", swap
    )
    old_own = stats_old[0]
    old_low = old_own.astype(BF16)
    olds = [old_low, shift(old_low, "mp", 1)]
    keep, right_rows, left_rows, send = kernel_call(
        sum_kernel,
        "sum_x",
        [SMEM] + [VMEM] * 4,
        [shape((PART, B), F32)] + [shape((ROWS, B))] * 2 + [shape((PART + ROWS, B))],
        awaited=1,
    )(info, total, mine, theirs, prec_left, olds[1])

    near_far = [
        [
            (z * CORE + c, ((z ^ 1) if c == step else ZH - 1 - z) * CORE + c)
            for z in range(ZH)
            for c in range(CORE)
        ]
        for step in range(2)
    ]
    got = lax.ppermute(send, ("zh", "core"), near_far[0])
    left_one = lax.ppermute(left_rows, ("x", "core"), near_far[0])
    left_two = lax.ppermute(
        jnp.concatenate([left_rows, left_one]), ("x", "core"), near_far[1]
    )
    keep, send, old_later, left_mine, left_send = kernel_call(
        middle_kernel,
        "middle",
        [SMEM] + [VMEM] * 7,
        [shape((PART, B), F32), shape((PART + 2 * ROWS, B)), shape((quarter, B))]
        + [shape((PART // CORE, B))] * 2,
    )(info, keep, right_rows, got, old_own, left_rows, left_one, left_two)
    left_theirs = lax.ppermute(left_send, "core", swap)
    got = lax.ppermute(send, ("zh", "core"), near_far[1])
    olds += [shift(old_later, "mp", step) for step in range(2, n_mp)]
    (pieces,) = kernel_call(
        functools.partial(pack_kernel, tokens ** -0.5),
        "pack",
        [VMEM] * 2,
        [shape((n_mp, n_root, CORE, half, lanes))],
        awaited=2,
    )(keep, got, *olds[2:])

    pieces = pieces.reshape((n_mp * n_root,) + pieces.shape[2:])
    blocks = lax.all_to_all(pieces, ("mp", "root"), 0, 0)

    (total,) = kernel_call(
        functools.partial(update_kernel, tokens ** -0.5),
        "update",
        [SMEM] + [VMEM] * 5,
        [shape((PART, B), F32)],
        [pltpu.VMEM((PART, B), BF16)] * 2,
        cost(2 * PART * B * (PART + B), 6 * PART * B),
    )(info, keep, send, got, left_mine, left_theirs)

    (chosen,) = kernel_call(
        choose_kernel,
        "choose",
        [SMEM, SMEM, VMEM, VMEM],
        [shape((X * CORE, 1 + B // lanes, half, lanes))],
    )(info, listed, blocks, total)
    parts = lax.all_to_all(chosen, ("x", "core"), 0, 0)
    (mine,) = kernel_call(
        spread_kernel,
        "spread",
        [SMEM, SMEM, VMEM],
        [shape((n_mp * n_root, X, half, lanes))],
    )(info, listed, parts)
    mine = lax.all_to_all(mine, ("mp", "root"), 0, 0)
    theirs = lax.ppermute(mine, "core", swap)
    gathered = [value.reshape((n_mp, n_root) + value.shape[1:]) for value in (mine, theirs)]
    (update,) = kernel_call(finish_kernel, "finish", [VMEM], [shape((half, 2 * B))])(parts)

    new_stats, new_roots = kernel_call(
        refresh_kernel,
        "refresh",
        [SMEM, SMEM] + [VMEM] * 7,
        [shape((quarter, B), F32)] * 2,
        [pltpu.VMEM((B, B), BF16), pltpu.VMEM((B, B), F32), pltpu.VMEM((B, B), BF16)],
        cost(2 * B ** 3 + 10 * quarter * B * B, 2 * B * B * 2),
    )(info, owner, *gathered, old_own, *olds)
    return update[None], new_stats[None, None], new_roots[None, None]


def solution(mesh):
    n_dp, n_mp, n_root = mesh.devices.shape
    fine = Mesh(
        mesh.devices.reshape(X, ZH, CORE, n_mp, n_root), ("x", "zh", "core", "mp", "root")
    )
    dp = ("x", "zh", "core")
    in_specs = (
        P(dp, "mp"),
        P(dp, "root"),
        P("mp", "root", dp, None),
        P("mp", "root", dp, None),
        P(dp, "mp", None),
        P(),
        P(),
    )
    out_specs = (P("mp", dp, "root"), P("root", dp, "mp", None), P("root", dp, "mp", None))
    return jax.shard_map(local, mesh=fine, in_specs=in_specs, out_specs=out_specs, check_vma=False)
```
